32 devices in a mesh: fsdp: 2 (over x), ctx: 8 (over z, y), tp: 2 (over core).
Axes of the slice: x: 2, y: 2, z: 4, core: 2. Of those that a mesh axis runs over, the one named last changes fastest.
Arguments:
- tokens: bfloat16 [8192, 768], P(('fsdp', 'ctx'), 'tp'), may hold values from -6 to 6
- cotangent: bfloat16 [8192, 768], P(('fsdp', 'ctx'), 'tp'), may hold values from -6 to 6
- w_qkv: float32 [768, 3, 768], P('fsdp', None, 'tp'), may hold values from -0.21875 to 0.21875
- w_attn: float32 [768, 768], P('tp', 'fsdp'), may hold values from -1.75 to 1.75
- w_up: float32 [768, 3072], P('fsdp', 'tp'), may hold values from -0.21875 to 0.21875
- w_down: float32 [3072, 768], P('tp', 'fsdp'), may hold values from -0.109375 to 0.109375
- norm_vectors: float32 [4, 768], replicated, may hold values from -0.8 to 1.5, as said below
- qkv_bias: float32 [3, 768], P(None, 'tp'), may hold values from -1 to 1
- up_bias: float32 [3072], P('tp'), may hold values from -1 to 1
- qkv_moment: float32 [768, 3, 768], P('fsdp', None, 'tp'), may hold values from -112 to 112
- attn_moment: float32 [768, 768], P('tp', 'fsdp'), may hold values from -80 to 80
- up_moment: float32 [768, 3072], P('fsdp', 'tp'), may hold values from -128 to 128
- down_moment: float32 [3072, 768], P('tp', 'fsdp'), may hold values from -256 to 256
- norm_moment: float32 [4, 768], replicated, may hold values from -256 to 256
- qbias_moment: float32 [3, 768], P(None, 'tp'), may hold values from -192 to 192
- ubias_moment: float32 [3072], P('tp'), may hold values from -128 to 128
- seq_lengths: int32 [2, 3], P('fsdp'), may hold values from 1024 to 2048, as said below
- block_source: int32 [2, 32], P('fsdp'), may hold values from 0 to 31, each once within a row
Outputs:
- mixed: bfloat16 [8192, 768], P(('fsdp', 'ctx'), 'tp')
- grad_tokens: float32 [8192, 768], P(('fsdp', 'ctx'), 'tp')
- mom_qkv: float32 [768, 3, 768], P('fsdp', None, 'tp')
- new_qkv: float32 [768, 3, 768], P(('fsdp', 'ctx'), None, 'tp')
- mom_attn: float32 [768, 768], P('tp', 'fsdp')
- new_attn: float32 [768, 768], P('tp', ('fsdp', 'ctx'))
- mom_up: float32 [768, 3072], P('fsdp', 'tp')
- new_up: float32 [768, 3072], P(('fsdp', 'ctx'), 'tp')
- mom_down: float32 [3072, 768], P('tp', 'fsdp')
- new_down: float32 [3072, 768], P('tp', ('fsdp', 'ctx'))
- mom_norm: float32 [4, 768], replicated
- new_norm: float32 [4, 768], replicated
- mom_qbias: float32 [3, 768], P(None, 'tp')
- new_qbias: float32 [3, 768], P(None, 'tp')
- mom_ubias: float32 [3072], P('tp')
- new_ubias: float32 [3072], P('tp')
The draws below stay inside these ranges and needn't reach their ends.
Inputs may be any that keep to these rules, and one draw needn't show every extreme that they name: `seq_lengths`: each row holds the 3 lengths of one group's sequences in packed order; each row sums to 4096 and holds one length of exactly 2048. `block_source`: each row is a permutation of the 32 blocks of one group. `norm_vectors`: row 0 holds gains, rows 1 to 3 shifts and biases.
All inputs are finite; a program needn't handle non-finite values.
Results may differ from the reference program's by a relative error of at most 0.02.
Values may be sent and summed in bfloat16 or wider, within the bound.
No kernel may reach another device: no remote copies, remote signals or barrier semaphores. Data moves between devices by JAX's collectives and lax.ppermute only.
A program may use at most 320 MiB of HBM per device.

```python
import math
import jax
import jax.numpy as jnp
from jax import lax

D = 768
FF = 3072
HD = 64
ROT = 16
BLK = 128
MIN_LEN = 1024
NS_STEPS = 5
HEADS = 12
PACK = 4096
TOKENS = 8192
NBLK = 32
SEQS = 3
N_FSDP = 2


def draw_norm_vectors(key, part):
    key = jax.random.fold_in(key, 11)
    gain_key, shift_key = jax.random.split(key)
    gains = jax.random.uniform(gain_key, (1, D), jnp.float32, 0.5, 1.5)
    shifts = 0.2 * jnp.clip(jax.random.normal(shift_key, (3, D), jnp.float32), -4.0, 4.0)
    return jnp.concatenate([gains, shifts], axis=0)


def draw_seq_lengths(key, part):
    key = jax.random.fold_in(key, 23)
    spare = PACK - SEQS * MIN_LEN - MIN_LEN

    def one_row(row_key):
        weight_key, order_key = jax.random.split(row_key)
        shares = jax.random.randint(weight_key, (SEQS - 1,), 1, 100)
        extra = jnp.minimum(MIN_LEN, spare * shares // jnp.sum(shares))
        remain = spare - jnp.sum(extra)
        pieces = []
        for position in range(SEQS - 1):
            added = jnp.minimum(MIN_LEN - extra[position], remain)
            remain = remain - added
            pieces.append(extra[position] + added)
        extras = jnp.concatenate([jnp.full((1,), MIN_LEN, jnp.int32), jnp.stack(pieces).astype(jnp.int32)])
        return (MIN_LEN + jax.random.permutation(order_key, extras)).astype(jnp.int32)
    return jax.vmap(one_row)(jax.random.split(key, N_FSDP))


def block_scale(key, dims, shards, smallest, top_value):
    level = 1.0
    for dim, blocks in shards:
        steps = jax.random.uniform(jax.random.fold_in(jax.random.fold_in(key, 6), dim), (blocks,), jnp.float32, smallest / len(shards), top_value / len(shards))
        level = level * jnp.repeat(jnp.exp(steps), dims[dim] // blocks).reshape((-1,) + (1,) * (len(dims) - 1 - dim))
    return level


def gaussian(own_key, extent, width, bound, cuts=(), kind=jnp.bfloat16):
    array = width * jax.random.normal(own_key, extent, jnp.float32)
    if cuts:
        array = array * block_scale(own_key, extent, cuts, -0.22, 0.18)
    return jnp.clip(array, -bound, bound).astype(kind)


def setup_inputs(seed: int = 0) -> dict:
    key_list = jax.random.split(jax.random.key(seed), 19)
    return {
        "tokens": gaussian(key_list[0], (TOKENS, D), 1.0, 6.0, ((0, 16), (1, 2))),
        "cotangent": gaussian(key_list[1], (TOKENS, D), 1.0, 6.0, ((0, 16), (1, 2))),
        "w_qkv": gaussian(key_list[2], (D, 3, D), D ** -0.5, 0.21875, ((0, 2), (2, 2)), jnp.float32),
        "w_attn": gaussian(key_list[3], (D, D), (D // 64) ** -0.5, 1.75, ((0, 2), (1, 2)), jnp.float32),
        "w_up": gaussian(key_list[4], (D, FF), D ** -0.5, 0.21875, ((0, 2), (1, 2)), jnp.float32),
        "w_down": gaussian(key_list[5], (FF, D), FF ** -0.5, 0.109375, ((0, 2), (1, 2)), jnp.float32),
        "norm_vectors": draw_norm_vectors(jax.random.fold_in(key_list[18], 71), 0),
        "qkv_bias": gaussian(key_list[7], (3, D), 0.2, 1.0, ((1, 2),), jnp.float32),
        "up_bias": gaussian(key_list[8], (FF,), 0.2, 1.0, ((0, 2),), jnp.float32),
        "qkv_moment": gaussian(key_list[9], (D, 3, D), (0.2 * TOKENS ** 0.5), 112.0, ((0, 2), (2, 2)), jnp.float32),
        "attn_moment": gaussian(key_list[10], (D, D), (0.15 * TOKENS ** 0.5), 80.0, ((0, 2), (1, 2)), jnp.float32),
        "up_moment": gaussian(key_list[11], (D, FF), (0.25 * TOKENS ** 0.5), 128.0, ((0, 2), (1, 2)), jnp.float32),
        "down_moment": gaussian(key_list[12], (FF, D), (0.5 * TOKENS ** 0.5), 256.0, ((0, 2), (1, 2)), jnp.float32),
        "norm_moment": gaussian(key_list[13], (4, D), (0.5 * TOKENS ** 0.5), 256.0, (), jnp.float32),
        "qbias_moment": gaussian(key_list[14], (3, D), (0.35 * TOKENS ** 0.5), 192.0, ((1, 2),), jnp.float32),
        "ubias_moment": gaussian(key_list[15], (FF,), (0.25 * TOKENS ** 0.5), 128.0, ((0, 2),), jnp.float32),
        "seq_lengths": draw_seq_lengths(jax.random.fold_in(key_list[18], 71), 0),
        "block_source": jax.vmap(lambda own: jax.random.permutation(own, NBLK))(jax.random.split(key_list[17], N_FSDP)).reshape((N_FSDP, NBLK)).astype(jnp.int32),
    }


HIGHEST = lax.Precision.HIGHEST
NS_COEF = (3.4445, -4.775, 2.0315)

@jax.custom_vjp
def low(v):
    return lax.optimization_barrier(v.astype(jnp.bfloat16)).astype(jnp.float32)

@jax.custom_vjp
def low_back(v):
    return v

def low_keep(v):
    return (low(v), None)

def low_pass(kept, grad):
    return (grad,)

def back_keep(v):
    return (v, None)

def back_low(kept, grad):
    return (low(grad),)
low.defvjp(low_keep, low_pass)
low_back.defvjp(back_keep, back_low)

def rotary_tables(places):
    exponent = jnp.arange(0, ROT, 2, dtype=jnp.float32) / ROT
    frequency = 1.0 / 10000.0 ** exponent
    angles = places.astype(jnp.float32)[:, None] * frequency[None, :]
    return (jnp.cos(angles)[:, None, :], jnp.sin(angles)[:, None, :])

def rotate(matrix, cosine, sine_tab):
    half_rot = ROT // 2
    first_half = matrix[..., :half_rot]
    second_half = matrix[..., half_rot:ROT]
    return jnp.concatenate([first_half * cosine - second_half * sine_tab, second_half * cosine + first_half * sine_tab, matrix[..., ROT:]], axis=-1)

def pack_layout(block_row, length_row):
    packed = jnp.arange(PACK, dtype=jnp.int32)
    placed = (block_row[packed // BLK] * BLK + packed % BLK).astype(jnp.int32)
    seq_ends = jnp.cumsum(length_row).astype(jnp.int32)
    starts = seq_ends - length_row
    sequence = lax.optimization_barrier(jnp.sum((packed[:, None] >= seq_ends[None, :]).astype(jnp.int32), axis=1))
    chosen = sequence[:, None] == jnp.arange(SEQS, dtype=jnp.int32)[None, :]
    offset = lax.optimization_barrier(jnp.sum(jnp.where(chosen, starts[None, :], 0), axis=1))
    return (placed, sequence, packed - offset)

def attention(query_all, key_all, value_all, sequence):
    block_rows = math.gcd(512, PACK)
    window = min(PACK, block_rows + 2 * MIN_LEN)

    def one_block(first_row):
        key_first = jnp.maximum(first_row + block_rows - window, 0).astype(jnp.int32)
        queries = lax.dynamic_slice_in_dim(query_all, first_row, block_rows, 0)
        key_rows = lax.dynamic_slice_in_dim(key_all, key_first, window, 0)
        value_rows = lax.dynamic_slice_in_dim(value_all, key_first, window, 0)
        query_seq = lax.dynamic_slice_in_dim(sequence, first_row, block_rows, 0)
        key_seq = lax.dynamic_slice_in_dim(sequence, key_first, window, 0)
        query_pos = first_row + jnp.arange(block_rows, dtype=jnp.int32)
        key_pos = key_first + jnp.arange(window, dtype=jnp.int32)
        allowed = ((query_seq[:, None] == key_seq[None, :]) & (key_pos[None, :] <= query_pos[:, None]))[None]
        scores = low_back(jnp.einsum('qhd,khd->hqk', queries, key_rows, precision=HIGHEST) * HD ** (-0.5))
        scores = jnp.where(allowed, scores, -1e+30)
        row_max = lax.optimization_barrier(jnp.max(scores, axis=2, keepdims=True))
        weights = jnp.where(allowed, jnp.exp(scores - row_max), 0.0)
        soft_probs = low(weights / lax.optimization_barrier(jnp.sum(weights, axis=2, keepdims=True)))
        return jnp.einsum('hqk,khd->qhd', soft_probs, value_rows, precision=HIGHEST)
    firsts = jnp.arange(0, PACK, block_rows, dtype=jnp.int32)
    blocks = lax.map(jax.checkpoint(one_block), firsts)
    return blocks.reshape(PACK, D)

def group_forward(x_rows, weight_qkv, weight_attn, weight_up, weight_down, vectors, bias_qkv, bias_up, layout):
    placed, sequence, places = layout
    inputs = jnp.zeros_like(x_rows).at[placed].set(x_rows)
    row_mean = lax.optimization_barrier(jnp.mean(inputs, axis=1, keepdims=True))
    centered = inputs - row_mean
    inv_std = lax.rsqrt(lax.optimization_barrier(jnp.mean(centered * centered, axis=1, keepdims=True)) + 1e-05)
    normed = centered * inv_std
    norm_out = low(normed * vectors[0] + vectors[1])
    projected = jnp.dot(norm_out, weight_qkv.reshape(D, 3 * D), precision=HIGHEST).reshape(PACK, 3, D) + bias_qkv[None]
    cosine, sine_tab = rotary_tables(places)
    queries = low(rotate(low_back(projected[:, 0]).reshape(PACK, HEADS, HD), cosine, sine_tab))
    key_rows = low(rotate(low_back(projected[:, 1]).reshape(PACK, HEADS, HD), cosine, sine_tab))
    value_rows = low(low_back(projected[:, 2])).reshape(PACK, HEADS, HD)
    attended = low(low_back(attention(queries, key_rows, value_rows, sequence)))
    hidden = low_back(jnp.dot(norm_out, weight_up, precision=HIGHEST) + bias_up)
    activated = low(jax.nn.gelu(hidden, approximate=False))
    output = inputs + jnp.dot(attended, weight_attn, precision=HIGHEST) + jnp.dot(activated, weight_down, precision=HIGHEST) + vectors[2] + vectors[3]
    return output[placed]

def orthogonalize(matrix):
    is_tall = matrix.shape[0] > matrix.shape[1]
    current = matrix.T if is_tall else matrix
    current = current / (jnp.sqrt(jnp.sum(current * current)) + 1e-07)
    for repeat in range(NS_STEPS):
        gram_mat = jnp.dot(current, current.T, precision=HIGHEST)
        poly_mat = NS_COEF[1] * gram_mat + NS_COEF[2] * jnp.dot(gram_mat, gram_mat, precision=HIGHEST)
        current = NS_COEF[0] * current + jnp.dot(poly_mat, current, precision=HIGHEST)
    return current.T if is_tall else current

def muon_step(weight, moment, gradient, fan_in):
    fresh = 0.95 * moment + gradient
    matrix = fresh.reshape(weight.shape[0], -1)
    orthogonal = orthogonalize(matrix)
    rate = 0.5 * math.sqrt(max(matrix.shape) / fan_in)
    return (fresh, weight - rate * orthogonal.reshape(weight.shape))

def reference(tokens, cotangent, w_qkv, w_attn, w_up, w_down, norm_vectors, qkv_bias, up_bias, qkv_moment, attn_moment, up_moment, down_moment, norm_moment, qbias_moment, ubias_moment, seq_lengths, block_source):
    layouts = [pack_layout(block_source[group], seq_lengths[group]) for group in range(N_FSDP)]

    def forward(inputs, weight_qkv, weight_attn, weight_up, weight_down, vectors, bias_qkv, bias_up):
        low_qkv = low(weight_qkv)
        low_attn = low(weight_attn)
        low_up = low(weight_up)
        low_down = low(weight_down)
        outputs = []
        for group in range(N_FSDP):
            rows_in = inputs[group * PACK:(group + 1) * PACK]
            outputs.append(group_forward(rows_in, low_qkv, low_attn, low_up, low_down, vectors, bias_qkv, bias_up, layouts[group]))
        return jnp.concatenate(outputs, axis=0)
    mixed, pullback = jax.vjp(forward, tokens.astype(jnp.float32), w_qkv, w_attn, w_up, w_down, norm_vectors, qkv_bias, up_bias)
    grads = pullback(cotangent.astype(jnp.float32))
    mom_qkv, new_qkv = muon_step(w_qkv, qkv_moment, grads[1], D)
    mom_attn, new_attn = muon_step(w_attn, attn_moment, grads[2], D // 64)
    mom_up, new_up = muon_step(w_up, up_moment, grads[3], D)
    mom_down, new_down = muon_step(w_down, down_moment, grads[4], FF)
    vector_rate = 0.3 / math.sqrt(TOKENS)
    mom_norm = 0.9 * norm_moment + grads[5]
    mom_qbias = 0.9 * qbias_moment + grads[6]
    mom_ubias = 0.9 * ubias_moment + grads[7]
    return (mixed.astype(jnp.bfloat16), grads[0], mom_qkv, new_qkv, mom_attn, new_attn, mom_up, new_up, mom_down, new_down, mom_norm, norm_vectors - vector_rate * mom_norm, mom_qbias, qkv_bias - vector_rate * mom_qbias, mom_ubias, up_bias - vector_rate * mom_ubias)
```

```python
from functools import partial
import math

import jax
import jax.numpy as jnp
from jax import lax
from jax.experimental import pallas as pl
from jax.experimental.pallas import tpu as pltpu
from jax.sharding import PartitionSpec as P

HD = 64
ROT = 16
BLK = 128
NS_STEPS = 5
CHUNK = 512
MAX_LEN = 2048
SPAN = (MAX_LEN + BLK) // CHUNK + 2
OWNERS = 4
NS_COEF = (3.4445, -4.775, 2.0315)
NEG_BIG = -1e30
SCALE = HD**-0.5
LOW = jnp.bfloat16
WIDE = jnp.float32
NT = (((1,), (1,)), ((), ()))
VMEM_ASK = 56 * 1024 * 1024


def dot_nn(left, right):
    return jnp.dot(left, right, preferred_element_type=WIDE)


def dot_nt(left, right):
    return lax.dot_general(left, right, NT, preferred_element_type=WIDE)


def partner(value, axis, step):
    size = lax.axis_size(axis)
    return lax.ppermute(value, axis, [(i, i ^ step) for i in range(size)])


def sum_scatter(pieces, axis, stride, index):
    count = pieces.shape[0]
    total = lax.dynamic_index_in_dim(pieces, index, 0, keepdims=False)
    for step in range(1, count):
        piece = lax.dynamic_index_in_dim(pieces, index ^ step, 0, keepdims=False)
        total = total + partner(piece.astype(LOW), axis, step * stride).astype(WIDE)
    return total


def gather_axis(shard, axis, dim):
    if lax.axis_size(axis) != 2:
        return lax.all_gather(shard, axis, axis=dim, tiled=True)
    other = partner(shard, axis, 1)
    first = lax.axis_index(axis) == 0
    return jnp.concatenate(
        [jnp.where(first, shard, other), jnp.where(first, other, shard)], axis=dim
    )


def sum_everywhere(value, axes):
    for axis in axes:
        step = 1
        while step < lax.axis_size(axis):
            value = value + partner(value, axis, step)
            step *= 2
    return value


def turned(block, cosine, sine, lane):
    half = ROT // 2
    swapped = jnp.where(
        lane % HD < half, pltpu.roll(block, BLK - half, 1), pltpu.roll(block, half, 1)
    )
    return block * cosine + swapped * sine


def two_heads(block, lane):
    zero = jnp.zeros_like(block)
    return jnp.concatenate(
        [jnp.where(lane < HD, block, zero), jnp.where(lane < HD, zero, block)], axis=0
    )


def one_of_two(stacked, lane):
    return jnp.where(lane < HD, stacked[:BLK], stacked[BLK:])


def project_kernel(count, inv_ref, *refs):
    x_own, x_far = refs[:count], refs[count : 2 * count]
    g_own, g_far = refs[2 * count : 3 * count], refs[3 * count : 4 * count]
    (
        w_own,
        w_far,
        bias,
        vec_own,
        vec_far,
        a_own,
        a_far,
        cos_ref,
        sin_ref,
        q_out,
        k_out,
        v_out,
        d_out,
    ) = refs[4 * count :]

    def whole(parts):
        return jnp.concatenate([part[...] for part in parts], axis=0)

    own, far = whole(x_own).astype(WIDE), whole(x_far).astype(WIDE)
    half = own.shape[1]
    width = 2 * half
    mean = (
        jnp.sum(own, axis=1, keepdims=True) + jnp.sum(far, axis=1, keepdims=True)
    ) / width
    own, far = own - mean, far - mean
    var = (
        jnp.sum(own * own, axis=1, keepdims=True) + jnp.sum(far * far, axis=1, keepdims=True)
    ) / width
    inv_std = lax.rsqrt(var + 1e-5)
    own = (own * inv_std * vec_own[0:1] + vec_own[1:2]).astype(LOW)
    far = (far * inv_std * vec_far[0:1] + vec_far[1:2]).astype(LOW)
    rows = own.shape[0]
    lane = lax.broadcasted_iota(jnp.int32, (rows, BLK), 1)
    cosine, sine = cos_ref[...], sin_ref[...]
    for part, out in enumerate((q_out, k_out, v_out)):
        cut = slice(part * half, (part + 1) * half)
        made = dot_nn(own, w_own[:, cut]) + dot_nn(far, w_far[:, cut]) + bias[:, cut]
        for pair in range(half // BLK):
            lanes = slice(pair * BLK, (pair + 1) * BLK)
            block = made[:, lanes]
            if part < 2:
                block = turned(block, cosine, sine, lane)
            out[:, lanes] = block.astype(LOW)
    d_out[...] = (dot_nt(whole(g_own), a_own[...]) + dot_nt(whole(g_far), a_far[...])).astype(LOW)


def project_all(inverse, x_own, x_far, g_own, g_far, weights, cosine, sine):
    rows, half = x_own.shape
    count = CHUNK // BLK

    def picked(place):
        return pl.BlockSpec((BLK, half), lambda i, inv: (inv[i * count + place], 0))

    def fixed(array):
        return pl.BlockSpec(array.shape, lambda i, inv: (0,) * array.ndim)

    def chunk(width):
        return pl.BlockSpec((CHUNK, width), lambda i, inv: (i, 0))

    return pl.pallas_call(
        partial(project_kernel, count),
        grid_spec=pltpu.PrefetchScalarGridSpec(
            num_scalar_prefetch=1,
            grid=(rows // CHUNK,),
            in_specs=[picked(i) for i in range(count)] * 4
            + [fixed(w) for w in weights]
            + [chunk(BLK)] * 2,
            out_specs=[chunk(half)] * 4,
        ),
        out_shape=[jax.ShapeDtypeStruct((rows, half), LOW)] * 4,
        compiler_params=pltpu.CompilerParams(vmem_limit_bytes=VMEM_ASK),
        cost_estimate=pl.CostEstimate(
            flops=16 * rows * half * half, bytes_accessed=20 * rows * half, transcendentals=0
        ),
        name="project_all",
    )(
        inverse,
        *([x_own] * count),
        *([x_far] * count),
        *([g_own] * count),
        *([g_far] * count),
        *weights,
        cosine,
        sine,
    )


def lane_tiles(array, combine):
    total = array[:, :BLK]
    for i in range(1, array.shape[1] // BLK):
        total = combine(total, array[:, i * BLK : (i + 1) * BLK])
    return total


def query_kernel(
    blocks,
    first,
    last,
    q_ref,
    k_ref,
    v_ref,
    d_ref,
    cos_ref,
    sin_ref,
    start_ref,
    att_out,
    dq_out,
    stat_out,
    s_scr,
    p_scr,
    q_scr,
    d_scr,
    m_scr,
    l_scr,
    e_scr,
    o_scr,
):
    pairs = q_ref.shape[1] // BLK
    own = att_out.shape[0] // BLK
    lane = lax.broadcasted_iota(jnp.int32, (BLK, BLK), 1)

    def lanes(pair):
        return slice(pair * BLK, (pair + 1) * BLK)

    @pl.loop(0, own)
    def _(j):
        row0 = pl.multiple_of(blocks[j] * BLK, BLK)
        out0 = pl.multiple_of(j * BLK, BLK)
        lo = first[j]
        hi = last[j]
        for g in range(pairs):
            q_scr[g] = two_heads(q_ref[pl.ds(row0, BLK), lanes(g)].astype(WIDE), lane).astype(
                LOW
            ) * LOW(SCALE)
            d_scr[g] = two_heads(d_ref[pl.ds(row0, BLK), lanes(g)].astype(WIDE), lane).astype(LOW)
        m_scr[...] = jnp.full(m_scr.shape, NEG_BIG, WIDE)
        l_scr[...] = jnp.zeros(l_scr.shape, WIDE)
        e_scr[...] = jnp.zeros(e_scr.shape, WIDE)
        o_scr[...] = jnp.zeros(o_scr.shape, WIDE)
        starts = start_ref[pl.ds(out0, BLK), :]
        places = row0 + lax.broadcasted_iota(jnp.int32, (BLK, 1), 0)
        starts = jnp.concatenate([starts, starts], axis=0)
        places = jnp.concatenate([places, places], axis=0)

        @pl.loop(lo, hi)
        def _(c):
            key0 = pl.multiple_of(c * CHUNK, CHUNK)
            key_place = key0 + lax.broadcasted_iota(jnp.int32, (2 * BLK, CHUNK), 1)
            allowed = (key_place >= starts) & (key_place <= places)
            for g in range(pairs):
                scores = dot_nt(q_scr[g], k_ref[pl.ds(key0, CHUNK), lanes(g)])
                scores = jnp.where(allowed, scores, NEG_BIG)
                s_scr[g, c - lo] = scores
                m_scr[g] = jnp.maximum(m_scr[g], lane_tiles(scores, jnp.maximum))

        for g in range(pairs):
            m_scr[g] = jnp.broadcast_to(
                jnp.max(m_scr[g], axis=1, keepdims=True), (2 * BLK, BLK)
            )

        @pl.loop(lo, hi)
        def _(c):
            key0 = pl.multiple_of(c * CHUNK, CHUNK)
            for g in range(pairs):
                values = v_ref[pl.ds(key0, CHUNK), lanes(g)]
                top = m_scr[g]
                weights = jnp.exp(s_scr[g, c - lo] - jnp.concatenate([top] * (CHUNK // BLK), 1))
                l_scr[g] += lane_tiles(weights, jnp.add)
                o_scr[g] += dot_nn(weights.astype(LOW), values)
                grad_prob = dot_nt(d_scr[g], values)
                e_scr[g] += lane_tiles(weights * grad_prob, jnp.add)
                s_scr[g, c - lo] = weights
                p_scr[g, c - lo] = grad_prob

        for g in range(pairs):
            total = jnp.sum(l_scr[g], axis=1, keepdims=True)
            inverse = 1.0 / total
            delta = jnp.sum(e_scr[g], axis=1, keepdims=True) * inverse
            att_out[pl.ds(out0, BLK), lanes(g)] = one_of_two(o_scr[g] * inverse, lane).astype(LOW)
            log_sum = m_scr[g] + jnp.log(total)
            stat_out[j, 2 * g : 2 * g + 1, :] = log_sum[:BLK].T[0:1]
            stat_out[j, 2 * g + 1 : 2 * g + 2, :] = log_sum[BLK:].T[0:1]
            wide = jnp.broadcast_to(delta, (2 * BLK, BLK))
            base = stat_out.shape[1] // 2 + 2 * g
            stat_out[j, base : base + 1, :] = wide[:BLK].T[0:1]
            stat_out[j, base + 1 : base + 2, :] = wide[BLK:].T[0:1]
            l_scr[g] = jnp.broadcast_to(inverse, (2 * BLK, BLK))
            e_scr[g] = wide
        o_scr[...] = jnp.zeros(o_scr.shape, WIDE)

        @pl.loop(lo, hi)
        def _(c):
            key0 = pl.multiple_of(c * CHUNK, CHUNK)
            for g in range(pairs):
                wide = jnp.concatenate([e_scr[g]] * (CHUNK // BLK), 1)
                grad_score = s_scr[g, c - lo] * (p_scr[g, c - lo] - wide)
                o_scr[g] += dot_nn(grad_score.astype(LOW), k_ref[pl.ds(key0, CHUNK), lanes(g)])

        cosine = cos_ref[pl.ds(row0, BLK), :]
        sine = sin_ref[pl.ds(row0, BLK), :]
        for g in range(pairs):
            grad = one_of_two(o_scr[g] * l_scr[g], lane) * SCALE
            dq_out[pl.ds(out0, BLK), lanes(g)] = turned(grad, cosine, -sine, lane).astype(LOW)


def smem():
    return pl.BlockSpec(memory_space=pltpu.SMEM)


def vmem():
    return pl.BlockSpec(memory_space=pltpu.VMEM)


def query_side(blocks, first, last, queries, keys, values, grads, cosine, sine, starts):
    own = blocks.shape[0]
    width = queries.shape[1]
    pairs = width // BLK
    stat_rows = 16 * ((2 * pairs + 7) // 8)
    work = 2 * BLK * CHUNK
    return pl.pallas_call(
        query_kernel,
        in_specs=[smem()] * 3 + [vmem()] * 7,
        out_specs=[vmem()] * 3,
        out_shape=[
            jax.ShapeDtypeStruct((own * BLK, width), LOW),
            jax.ShapeDtypeStruct((own * BLK, width), LOW),
            jax.ShapeDtypeStruct((own, stat_rows, BLK), WIDE),
        ],
        scratch_shapes=[
            pltpu.VMEM((pairs, SPAN, 2 * BLK, CHUNK), WIDE),
            pltpu.VMEM((pairs, SPAN, 2 * BLK, CHUNK), WIDE),
            pltpu.VMEM((pairs, 2 * BLK, BLK), LOW),
            pltpu.VMEM((pairs, 2 * BLK, BLK), LOW),
            pltpu.VMEM((pairs, 2 * BLK, BLK), WIDE),
            pltpu.VMEM((pairs, 2 * BLK, BLK), WIDE),
            pltpu.VMEM((pairs, 2 * BLK, BLK), WIDE),
            pltpu.VMEM((pairs, 2 * BLK, BLK), WIDE),
        ],
        compiler_params=pltpu.CompilerParams(vmem_limit_bytes=VMEM_ASK),
        cost_estimate=pl.CostEstimate(
            flops=own * pairs * 4 * 4 * 2 * work * BLK,
            bytes_accessed=4 * keys.shape[0] * width * 2,
            transcendentals=own * pairs * 4 * work,
        ),
        name="query_side",
    )(blocks, first, last, queries, keys, values, grads, cosine, sine, starts)


def key_kernel(
    blocks,
    first,
    last,
    inverse,
    q_ref,
    k_ref,
    v_ref,
    d_ref,
    cos_ref,
    sin_ref,
    end_ref,
    stat_ref,
    dk_out,
    dv_out,
    k_scr,
    v_scr,
    dk_scr,
    dv_scr,
):
    pairs = q_ref.shape[1] // BLK
    own = dk_out.shape[0] // BLK
    half_stat = stat_ref.shape[1] // 2
    lane = lax.broadcasted_iota(jnp.int32, (BLK, BLK), 1)

    def lanes(pair):
        return slice(pair * BLK, (pair + 1) * BLK)

    @pl.loop(0, own)
    def _(j):
        row0 = pl.multiple_of(blocks[j] * BLK, BLK)
        out0 = pl.multiple_of(j * BLK, BLK)
        for g in range(pairs):
            k_scr[g] = two_heads(k_ref[pl.ds(row0, BLK), lanes(g)].astype(WIDE), lane).astype(
                LOW
            ) * LOW(SCALE)
            v_scr[g] = two_heads(v_ref[pl.ds(row0, BLK), lanes(g)].astype(WIDE), lane).astype(LOW)
        dk_scr[...] = jnp.zeros(dk_scr.shape, WIDE)
        dv_scr[...] = jnp.zeros(dv_scr.shape, WIDE)
        ends = end_ref[pl.ds(out0, BLK), :]
        places = row0 + lax.broadcasted_iota(jnp.int32, (BLK, 1), 0)

        @pl.loop(first[j], last[j])
        def _(c):
            query0 = pl.multiple_of(c * CHUNK, CHUNK)
            query_place = query0 + lax.broadcasted_iota(jnp.int32, (BLK, CHUNK), 1)
            allowed = (query_place >= places) & (query_place < ends)
            count = CHUNK // BLK
            slots = [inverse[c * count + i] for i in range(count)]

            def stat(row):
                return jnp.concatenate([stat_ref[slot, row : row + 1, :] for slot in slots], 1)

            for g in range(pairs):
                queries = q_ref[pl.ds(query0, CHUNK), lanes(g)]
                grads = d_ref[pl.ds(query0, CHUNK), lanes(g)]
                scores = dot_nt(k_scr[g], queries)
                grad_prob = dot_nt(v_scr[g], grads)
                probs, grad_scores = [], []
                for h in range(2):
                    rows = slice(h * BLK, (h + 1) * BLK)
                    shifted = jnp.where(allowed, scores[rows] - stat(2 * g + h), NEG_BIG)
                    prob = jnp.exp(shifted)
                    probs.append(prob.astype(LOW))
                    grad_scores.append(
                        (prob * (grad_prob[rows] - stat(half_stat + 2 * g + h))).astype(LOW)
                    )
                dv_scr[g] += dot_nn(jnp.concatenate(probs, 0), grads)
                dk_scr[g] += dot_nn(jnp.concatenate(grad_scores, 0), queries)

        cosine = cos_ref[pl.ds(row0, BLK), :]
        sine = sin_ref[pl.ds(row0, BLK), :]
        for g in range(pairs):
            grad = one_of_two(dk_scr[g], lane) * SCALE
            dk_out[pl.ds(out0, BLK), lanes(g)] = turned(grad, cosine, -sine, lane).astype(LOW)
            dv_out[pl.ds(out0, BLK), lanes(g)] = one_of_two(dv_scr[g], lane).astype(LOW)


def key_side(
    blocks, first, last, inverse, queries, keys, values, grads, cosine, sine, ends, stats
):
    own = blocks.shape[0]
    width = queries.shape[1]
    pairs = width // BLK
    work = 2 * BLK * CHUNK
    return pl.pallas_call(
        key_kernel,
        in_specs=[smem()] * 4 + [vmem()] * 8,
        out_specs=[vmem()] * 2,
        out_shape=[jax.ShapeDtypeStruct((own * BLK, width), LOW)] * 2,
        scratch_shapes=[
            pltpu.VMEM((pairs, 2 * BLK, BLK), LOW),
            pltpu.VMEM((pairs, 2 * BLK, BLK), LOW),
            pltpu.VMEM((pairs, 2 * BLK, BLK), WIDE),
            pltpu.VMEM((pairs, 2 * BLK, BLK), WIDE),
        ],
        compiler_params=pltpu.CompilerParams(vmem_limit_bytes=VMEM_ASK),
        cost_estimate=pl.CostEstimate(
            flops=own * pairs * 4 * 4 * 2 * work * BLK,
            bytes_accessed=4 * keys.shape[0] * width * 2,
            transcendentals=own * pairs * 4 * work,
        ),
        name="key_side",
    )(blocks, first, last, inverse, queries, keys, values, grads, cosine, sine, ends, stats)


TILE = 256


def symmetric_product(out_ref, left, right):
    size = out_ref.shape[0]
    for i in range(0, size, TILE):
        out_ref[i : i + TILE, i:] = dot_nt(left[i : i + TILE, :], right[i:, :])
    for i in range(0, size, TILE):
        for j in range(i + TILE, size, TILE):
            out_ref[j : j + TILE, i : i + TILE] = out_ref[i : i + TILE, j : j + TILE].T


def ns_kernel(near_ref, far_ref, out_ref, wide_scr, low_scr, gram_scr, poly_scr):
    size, half = near_ref.shape
    span = 2 * half
    step = 768
    cuts = [slice(i, i + step) for i in range(0, span, step)]
    total = jnp.zeros((1, 1), WIDE)
    for source, base in ((near_ref, 0), (far_ref, half)):
        for i in range(0, half, step):
            part = source[:, i : i + step].astype(WIDE)
            wide_scr[:, base + i : base + i + step] = part
            total = total + jnp.sum(part * part)
    factor = 1.0 / (jnp.sqrt(total) + 1e-7)
    for cut in cuts:
        part = wide_scr[:, cut] * factor
        wide_scr[:, cut] = part
        low_scr[:, cut] = part.astype(LOW)

    def polynomial():
        symmetric_product(gram_scr, low_scr, low_scr)
        poly_scr[...] = gram_scr[...].astype(LOW)
        first = gram_scr[...] * NS_COEF[1]
        symmetric_product(gram_scr, poly_scr, poly_scr)
        poly_scr[...] = (first + NS_COEF[2] * gram_scr[...]).astype(LOW)

    @pl.loop(0, NS_STEPS - 1)
    def _(_):
        polynomial()
        for cut in cuts:
            part = NS_COEF[0] * wide_scr[:, cut] + dot_nn(poly_scr[...], low_scr[:, cut])
            wide_scr[:, cut] = part
            low_scr[:, cut] = part.astype(LOW)

    polynomial()
    rows = out_ref.shape[0]
    for i in range(0, half, step):
        cut = slice(i, i + step)
        out_ref[:, cut] = (
            NS_COEF[0] * wide_scr[:rows, cut] + dot_nn(poly_scr[:rows, :], low_scr[:, cut])
        ).astype(LOW)


def orthogonal_rows(near, far, rows):
    size, half = near.shape
    kept = rows if rows % 16 == 0 else size
    out = pl.pallas_call(
        ns_kernel,
        in_specs=[vmem()] * 2,
        out_specs=vmem(),
        out_shape=jax.ShapeDtypeStruct((kept, half), LOW),
        scratch_shapes=[
            pltpu.VMEM((size, 2 * half), WIDE),
            pltpu.VMEM((size, 2 * half), LOW),
            pltpu.VMEM((size, size), WIDE),
            pltpu.VMEM((size, size), LOW),
        ],
        compiler_params=pltpu.CompilerParams(vmem_limit_bytes=VMEM_ASK),
        cost_estimate=pl.CostEstimate(
            flops=NS_STEPS * 7 * size * size * half, bytes_accessed=4 * size * half, transcendentals=0
        ),
        name="orthogonal_rows",
    )(near, far)
    return out[:rows]


def rotary_tables(places):
    half = ROT // 2
    exponent = jnp.arange(0, ROT, 2, dtype=WIDE) / ROT
    frequency = 1.0 / 10000.0**exponent
    angles = frequency[:, None] * places.astype(WIDE)[None, :]
    lane = jnp.arange(BLK) % HD
    picked = ((lane % half)[None, :] == jnp.arange(half)[:, None]) & (lane < ROT)[None, :]
    sign = jnp.where(lane < half, -1.0, 1.0)[None, :]
    spread = partial(
        jnp.einsum, "fn,fl->nl", precision=lax.Precision.HIGHEST, preferred_element_type=WIDE
    )
    cosine = spread(jnp.cos(angles), picked.astype(WIDE)) + (lane >= ROT)[None, :].astype(WIDE)
    return cosine, spread(jnp.sin(angles), picked * sign)


def body(
    tokens,
    cotangent,
    w_qkv,
    w_attn,
    w_up,
    w_down,
    norm_vectors,
    qkv_bias,
    up_bias,
    qkv_moment,
    attn_moment,
    up_moment,
    down_moment,
    norm_moment,
    qbias_moment,
    ubias_moment,
    seq_lengths,
    block_source,
):
    row_count, half = tokens.shape
    fsdp_count = lax.axis_size("fsdp")
    ctx_count = lax.axis_size("ctx")
    tp_index = lax.axis_index("tp")
    fsdp_index = lax.axis_index("fsdp")
    ctx_index = lax.axis_index("ctx")
    low_count = ctx_count // OWNERS
    ctx_low = ctx_index % low_count
    ctx_high = ctx_index // low_count
    width = 2 * half
    own_blocks = row_count // BLK
    pack = ctx_count * row_count
    first_tp = tp_index == 0
    block_row = block_source[0]
    length_row = seq_lengths[0]

    def both_halves(mine, other, dim):
        return jnp.concatenate(
            [jnp.where(first_tp, mine, other), jnp.where(first_tp, other, mine)], axis=dim
        )

    tokens_far = partner(tokens, "tp", 1)
    cotangent_far = partner(cotangent, "tp", 1)
    full_cotangent = both_halves(cotangent, cotangent_far, 1)

    up_full = gather_axis(w_up.astype(LOW), "fsdp", 0)
    down_full = gather_axis(w_down.astype(LOW), "fsdp", 1)
    qkv_full = gather_axis(w_qkv.astype(LOW).reshape(w_qkv.shape[0], 3 * half), "fsdp", 0)
    attn_full = gather_axis(w_attn.astype(LOW), "fsdp", 1)

    def group_rows(own, own_far):
        near = [own] + [partner(own, "ctx", s * low_count) for s in range(1, OWNERS)]
        shards = [jnp.concatenate(near, axis=0)]
        for s in range(1, low_count):
            shards.append(jnp.concatenate([partner(part, "ctx", s) for part in near], axis=0))
        near_rest = jnp.concatenate(near[1:], axis=0)
        far = [own_far, partner(near_rest, "tp", 1)]
        far += [partner(shard, "tp", 1) for shard in shards[1:]]
        return jnp.concatenate(shards, axis=0), jnp.concatenate(far, axis=0)

    x_near, x_far = group_rows(tokens, tokens_far)
    g_near, g_far = group_rows(cotangent, cotangent_far)

    def group_place(ctx):
        differs = ctx ^ ctx_index
        return (differs % low_count) * OWNERS + differs // low_count

    slot_blocks = jnp.arange(block_row.shape[0], dtype=jnp.int32)
    slot_places = group_place(slot_blocks // own_blocks) * own_blocks + slot_blocks % own_blocks
    inverse = jnp.sum(
        jnp.where(block_row[None, :] == slot_blocks[:, None], slot_places[None, :], 0), axis=1
    ).astype(jnp.int32)
    my_blocks = lax.dynamic_slice_in_dim(block_row, ctx_index * own_blocks, own_blocks)

    seq_ends = jnp.cumsum(length_row).astype(jnp.int32)
    seq_starts = seq_ends - length_row

    def bounds(packed):
        inside = (packed[:, None] >= seq_starts[None, :]) & (packed[:, None] < seq_ends[None, :])
        return (
            jnp.sum(jnp.where(inside, seq_starts[None, :], 0), axis=1).astype(jnp.int32),
            jnp.sum(jnp.where(inside, seq_ends[None, :], 0), axis=1).astype(jnp.int32),
        )

    packed = jnp.arange(pack, dtype=jnp.int32)
    cosine, sine = rotary_tables(packed - bounds(packed)[0])
    my_packed = (
        my_blocks[:, None] * BLK + jnp.arange(BLK, dtype=jnp.int32)[None, :]
    ).reshape(-1)
    my_starts, my_ends = bounds(my_packed)
    key_first = bounds(my_blocks * BLK)[0] // CHUNK
    key_last = (my_blocks * BLK + BLK - 1) // CHUNK + 1
    query_first = my_blocks * BLK // CHUNK
    query_last = (bounds(my_blocks * BLK + BLK - 1)[1] + CHUNK - 1) // CHUNK

    def own_first(array, dim):
        left, right = jnp.split(array, 2, axis=dim)
        return jnp.where(first_tp, left, right), jnp.where(first_tp, right, left)

    queries, keys, values, d_attended = project_all(
        inverse,
        x_near,
        x_far,
        g_near,
        g_far,
        (
            *own_first(qkv_full, 0),
            qkv_bias.reshape(1, 3 * half),
            *own_first(norm_vectors, 1),
            *own_first(attn_full, 1),
        ),
        cosine,
        sine,
    )

    inputs = both_halves(tokens, tokens_far, 1).astype(WIDE)
    centered = inputs - jnp.mean(inputs, axis=1, keepdims=True)
    inv_std = lax.rsqrt(jnp.mean(centered * centered, axis=1, keepdims=True) + 1e-05)
    normed = centered * inv_std
    norm_out = (normed * norm_vectors[0] + norm_vectors[1]).astype(LOW)
    hidden = dot_nn(norm_out, up_full) + up_bias
    activated, gelu_pull = jax.vjp(partial(jax.nn.gelu, approximate=False), hidden)
    activated_low = activated.astype(LOW)
    d_hidden = gelu_pull(dot_nt(full_cotangent, down_full))[0].astype(LOW)

    def outer(left, right):
        return jnp.einsum("na,nb->ab", left, right, preferred_element_type=WIDE)

    def reduced(gradient):
        rows = gradient.shape[0] // fsdp_count
        part = sum_scatter(
            gradient.reshape(fsdp_count, rows, gradient.shape[1]), "fsdp", 1, fsdp_index
        )
        piece = rows // ctx_count
        part = part.reshape(OWNERS, low_count, piece, gradient.shape[1])
        part = sum_scatter(jnp.swapaxes(part, 0, 1), "ctx", 1, ctx_low)
        return sum_scatter(part, "ctx", low_count, ctx_high)

    sum_up = reduced(outer(norm_out, d_hidden))
    sum_down = reduced(outer(full_cotangent, activated_low))
    grad_ubias = jnp.sum(d_hidden.astype(WIDE), axis=0)
    grad_outbias = jnp.sum(cotangent.astype(WIDE), axis=0)

    attended, grad_q, stats = query_side(
        my_blocks,
        key_first,
        key_last,
        queries,
        keys,
        values,
        d_attended,
        cosine,
        sine,
        my_starts[:, None],
    )
    near = [stats] + [partner(stats, "ctx", s * low_count) for s in range(1, OWNERS)]
    all_stats = list(near)
    for s in range(1, low_count):
        all_stats += [partner(part, "ctx", s) for part in near]
    grad_k, grad_v = key_side(
        my_blocks,
        query_first,
        query_last,
        inverse,
        queries,
        keys,
        values,
        d_attended,
        cosine,
        sine,
        my_ends[:, None],
        jnp.concatenate(all_stats, axis=0),
    )
    grad_proj = jnp.concatenate([grad_q, grad_k, grad_v], axis=1)
    sum_joint = reduced(
        jnp.concatenate(
            [outer(norm_out, grad_proj), outer(full_cotangent, attended)], axis=1
        )
    )
    grad_qbias = jnp.sum(grad_proj.astype(WIDE), axis=0)

    partial_out = dot_nn(attended, attn_full) + dot_nn(activated_low, down_full)

    def own_half(array):
        return jnp.where(first_tp, array[:, :half], array[:, half:])

    def far_half(array):
        return jnp.where(first_tp, array[:, half:], array[:, :half])

    def sum_halves(array):
        return own_half(array) + partner(far_half(array).astype(LOW), "tp", 1).astype(WIDE)

    out_bias = own_half((norm_vectors[2] + norm_vectors[3])[None, :])
    mixed = (tokens.astype(WIDE) + sum_halves(partial_out) + out_bias).astype(LOW)

    grad_norm = sum_halves(dot_nt(grad_proj, qkv_full) + dot_nt(d_hidden, up_full))
    my_normed = own_half(normed)
    scaled = grad_norm * own_half(norm_vectors[0:1])
    row_sums = jnp.stack([jnp.sum(scaled, axis=1), jnp.sum(scaled * my_normed, axis=1)])
    row_means = (row_sums + partner(row_sums, "tp", 1)) / width
    grad_tokens = cotangent.astype(WIDE) + inv_std * (
        scaled - row_means[0][:, None] - my_normed * row_means[1][:, None]
    )

    vector_parts = jnp.stack(
        [jnp.sum(grad_norm * my_normed, axis=0), jnp.sum(grad_norm, axis=0), grad_outbias]
    )
    small = jnp.concatenate([vector_parts.reshape(-1), grad_qbias, grad_ubias])
    small = sum_everywhere(small, ("ctx", "fsdp"))
    mine = small[: 3 * half].reshape(3, half)
    vectors = both_halves(mine, partner(mine, "tp", 1), 1)
    sum_vectors = jnp.concatenate([vectors, vectors[2:3]], axis=0)
    sum_qbias = small[3 * half : 6 * half].reshape(3, half)
    sum_ubias = small[6 * half :]

    joint = jnp.concatenate([sum_up, sum_down, sum_joint], axis=1)
    hidden_here = up_bias.shape[0]
    gathered = lax.all_gather(joint.astype(LOW), "ctx", axis=0, tiled=True).astype(WIDE)
    cut_down, cut_qkv, cut_attn = hidden_here, 2 * hidden_here, 2 * hidden_here + 3 * half
    fresh_up = 0.95 * up_moment + gathered[:, :cut_down]
    fresh_down = 0.95 * down_moment + gathered[:, cut_down:cut_qkv].T
    fresh_qkv = 0.95 * qkv_moment + gathered[:, cut_qkv:cut_attn].reshape(qkv_moment.shape)
    fresh_attn = 0.95 * attn_moment + gathered[:, cut_attn:].T

    piece = joint.shape[0]

    def my_rows(array, dim):
        return lax.dynamic_slice_in_dim(array, ctx_index * piece, piece, dim)

    def as_rows(up, down, qkv, attn):
        return (
            my_rows(up, 0),
            my_rows(down, 1).T,
            my_rows(qkv, 0).reshape(piece, 3 * half),
            my_rows(attn, 1).T,
        )

    moments = as_rows(up_moment, down_moment, qkv_moment, attn_moment)
    sums = (sum_up, sum_down, sum_joint[:, : 3 * half], sum_joint[:, 3 * half :])
    pieces = jnp.stack(
        [
            jnp.pad(
                (0.95 * moment + total).astype(LOW), ((0, 0), (0, hidden_here - total.shape[1]))
            )
            for moment, total in zip(moments, sums)
        ]
    )

    def to_owner(array, step):
        if step == 0:
            return lax.dynamic_index_in_dim(array, ctx_high, 0, keepdims=False)
        picked = lax.dynamic_index_in_dim(array, ctx_high ^ step, 0, keepdims=False)
        return partner(picked, "ctx", step * low_count)

    matrix = jnp.concatenate([to_owner(pieces, s) for s in range(OWNERS)], axis=0)
    parts = [matrix] + [partner(matrix, "ctx", s) for s in range(1, low_count)]
    for s in range(1, fsdp_count):
        parts += [partner(part, "fsdp", s) for part in parts[:low_count]]
    near_cols = jnp.concatenate(parts, axis=0)
    far_cols = jnp.concatenate([partner(part, "tp", 1) for part in parts], axis=0)
    rows_out = orthogonal_rows(near_cols, far_cols, OWNERS * piece).reshape(
        OWNERS, piece, hidden_here
    )
    returned = jnp.stack(
        [rows_out[0]]
        + [partner(rows_out[s], "ctx", s * low_count) for s in range(1, OWNERS)]
    )
    orthogonal = [
        lax.dynamic_index_in_dim(returned, ctx_high ^ m, 0, keepdims=False).astype(WIDE)
        for m in range(OWNERS)
    ]
    full_hidden = hidden_here * 2
    olds = as_rows(w_up, w_down, w_qkv, w_attn)
    rates = (
        0.5 * math.sqrt(full_hidden / width),
        0.5 * math.sqrt(full_hidden / full_hidden),
        0.5 * math.sqrt(3 * width / width),
        0.5 * math.sqrt(width / (width // HD)),
    )
    new_up, new_down, new_qkv, new_attn = (
        old - rate * made[:, : old.shape[1]] for old, rate, made in zip(olds, rates, orthogonal)
    )

    vector_rate = 0.3 / math.sqrt(row_count * fsdp_count * ctx_count)
    mom_norm = 0.9 * norm_moment + sum_vectors
    mom_qbias = 0.9 * qbias_moment + sum_qbias
    mom_ubias = 0.9 * ubias_moment + sum_ubias
    return (
        mixed,
        grad_tokens,
        fresh_qkv,
        new_qkv.reshape(piece, 3, half),
        fresh_attn,
        new_attn.T,
        fresh_up,
        new_up,
        fresh_down,
        new_down.T,
        mom_norm,
        norm_vectors - vector_rate * mom_norm,
        mom_qbias,
        qkv_bias - vector_rate * mom_qbias,
        mom_ubias,
        up_bias - vector_rate * mom_ubias,
    )


def solution(mesh):
    return jax.shard_map(
        body,
        mesh=mesh,
        in_specs=(
            P(("fsdp", "ctx"), "tp"),
            P(("fsdp", "ctx"), "tp"),
            P("fsdp", None, "tp"),
            P("tp", "fsdp"),
            P("fsdp", "tp"),
            P("tp", "fsdp"),
            P(),
            P(None, "tp"),
            P("tp"),
            P("fsdp", None, "tp"),
            P("tp", "fsdp"),
            P("fsdp", "tp"),
            P("tp", "fsdp"),
            P(),
            P(None, "tp"),
            P("tp"),
            P("fsdp", None),
            P("fsdp", None),
        ),
        out_specs=(
            P(("fsdp", "ctx"), "tp"),
            P(("fsdp", "ctx"), "tp"),
            P("fsdp", None, "tp"),
            P(("fsdp", "ctx"), None, "tp"),
            P("tp", "fsdp"),
            P("tp", ("fsdp", "ctx")),
            P("fsdp", "tp"),
            P(("fsdp", "ctx"), "tp"),
            P("tp", "fsdp"),
            P("tp", ("fsdp", "ctx")),
            P(),
            P(),
            P(None, "tp"),
            P(None, "tp"),
            P("tp"),
            P("tp"),
        ),
        check_vma=False,
    )
```

```python
from functools import partial
import math

import jax
import jax.numpy as jnp
from jax import lax
from jax.experimental import pallas as pl
from jax.experimental.pallas import tpu as pltpu
from jax.sharding import PartitionSpec as P

HD = 64
ROT = 16
BLK = 128
NS_STEPS = 5
CHUNK = 512
MAX_LEN = 2048
SPAN = (MAX_LEN + BLK) // CHUNK + 2
OWNERS = 4
NS_COEF = (3.4445, -4.775, 2.0315)
NEG_BIG = -1e30
SCALE = HD**-0.5
LOW = jnp.bfloat16
WIDE = jnp.float32
NT = (((1,), (1,)), ((), ()))
VMEM_ASK = 56 * 1024 * 1024


def dot_nn(left, right):
    return jnp.dot(left, right, preferred_element_type=WIDE)


def dot_nt(left, right):
    return lax.dot_general(left, right, NT, preferred_element_type=WIDE)


def partner(value, axis, step):
    size = lax.axis_size(axis)
    return lax.ppermute(value, axis, [(i, i ^ step) for i in range(size)])


def partner_among(value, axes, strides, wanted):
    sizes = [lax.axis_size(axis) for axis in axes]
    pairs = []
    for flat in range(math.prod(sizes)):
        index, rest = [], flat
        for size in reversed(sizes):
            index.insert(0, rest % size)
            rest //= size
        if wanted(index):
            source = 0
            for size, i, stride in zip(sizes, index, strides):
                source = source * size + (i ^ stride)
            pairs.append((source, flat))
    return lax.ppermute(value, tuple(axes), pairs)


def sum_scatter(pieces, axis, stride, index):
    count = pieces.shape[0]
    total = lax.dynamic_index_in_dim(pieces, index, 0, keepdims=False).astype(WIDE)
    for step in range(1, count):
        piece = lax.dynamic_index_in_dim(pieces, index ^ step, 0, keepdims=False)
        total = total + partner(piece.astype(LOW), axis, step * stride).astype(WIDE)
    return total


def gather_axis(shard, axis, dim):
    if lax.axis_size(axis) != 2:
        return lax.all_gather(shard, axis, axis=dim, tiled=True)
    other = partner(shard, axis, 1)
    first = lax.axis_index(axis) == 0
    return jnp.concatenate(
        [jnp.where(first, shard, other), jnp.where(first, other, shard)], axis=dim
    )


def sum_everywhere(value, axes):
    for axis in axes:
        step = 1
        while step < lax.axis_size(axis):
            value = value + partner(value, axis, step)
            step *= 2
    return value


def turned(block, cosine, sine, lane):
    half = ROT // 2
    swapped = jnp.where(
        lane % HD < half, pltpu.roll(block, BLK - half, 1), pltpu.roll(block, half, 1)
    )
    return block * cosine + swapped * sine


def two_heads(block, lane):
    zero = jnp.zeros_like(block)
    return jnp.concatenate(
        [jnp.where(lane < HD, block, zero), jnp.where(lane < HD, zero, block)], axis=0
    )


def one_of_two(stacked, lane):
    return jnp.where(lane < HD, stacked[:BLK], stacked[BLK:])


def project_kernel(
    near, far, w_near, w_far, bias, vec_near, vec_far, cos_ref, sin_ref, *outs
):
    outs = outs[-4:]
    half = outs[0].shape[1]
    width = 2 * half
    own, other = near[:, :half].astype(WIDE), far[:, :half].astype(WIDE)
    mean = (
        jnp.sum(own, axis=1, keepdims=True) + jnp.sum(other, axis=1, keepdims=True)
    ) / width
    own, other = own - mean, other - mean
    var = (
        jnp.sum(own * own, axis=1, keepdims=True) + jnp.sum(other * other, axis=1, keepdims=True)
    ) / width
    inv_std = lax.rsqrt(var + 1e-5)
    own = (own * inv_std * vec_near[0:1] + vec_near[1:2]).astype(LOW)
    other = (other * inv_std * vec_far[0:1] + vec_far[1:2]).astype(LOW)
    lane = lax.broadcasted_iota(jnp.int32, (own.shape[0], BLK), 1)
    cosine, sine = cos_ref[...], sin_ref[...]
    for part, out in enumerate(outs[:3]):
        span = slice(part * half, (part + 1) * half)
        made = dot_nn(own, w_near[:, span]) + dot_nn(other, w_far[:, span]) + bias[:, span]
        for pair in range(half // BLK):
            lanes = slice(pair * BLK, (pair + 1) * BLK)
            block = made[:, lanes]
            if part < 2:
                block = turned(block, cosine, sine, lane)
            out[:, lanes] = block.astype(LOW)
    span = slice(3 * half, 4 * half)
    outs[3][...] = (
        dot_nn(near[:, half:], w_near[:, span]) + dot_nn(far[:, half:], w_far[:, span])
    ).astype(LOW)


def project_rows(part, pack, near, far, weights, cosine, sine, made):
    rows = near.shape[0]
    half = near.shape[1] // 2
    base = part * (rows // CHUNK)

    def fixed(array):
        return pl.BlockSpec(array.shape, lambda i: (0,) * array.ndim)

    def placed(width):
        return pl.BlockSpec((CHUNK, width), lambda i: (i + base, 0))

    here = pl.BlockSpec((CHUNK, 2 * half), lambda i: (i, 0))
    before = 4 + len(weights)
    return pl.pallas_call(
        project_kernel,
        grid=(rows // CHUNK,),
        in_specs=[here] * 2
        + [fixed(w) for w in weights]
        + [placed(BLK)] * 2
        + [pl.BlockSpec(memory_space=pl.ANY)] * len(made),
        out_specs=[placed(half)] * 4,
        out_shape=[jax.ShapeDtypeStruct((pack, half), LOW)] * 4,
        input_output_aliases={before + i: i for i in range(len(made))},
        compiler_params=pltpu.CompilerParams(vmem_limit_bytes=VMEM_ASK),
        cost_estimate=pl.CostEstimate(
            flops=48 * rows * half * half, bytes_accessed=20 * rows * half, transcendentals=0
        ),
        name="project_rows",
    )(near, far, *weights, cosine, sine, *made)


def feed_kernel(
    x_ref,
    xt_ref,
    g_ref,
    gt_ref,
    up_ref,
    down_ref,
    bias_ref,
    out_ref,
    dx_ref,
    dup_ref,
    ddown_ref,
    dbias_ref,
):
    hidden = dot_nn(x_ref[...], up_ref[...]) + bias_ref[...]
    grad = dot_nn(g_ref[...], down_ref[...])
    below = 0.5 + 0.5 * lax.erf(hidden * math.sqrt(0.5))
    density = jnp.exp(-0.5 * hidden * hidden) * (1.0 / math.sqrt(2.0 * math.pi))
    active = (hidden * below).astype(LOW)
    grad = (grad * (below + hidden * density)).astype(LOW)
    dbias_ref[...] = jnp.sum(grad.astype(WIDE), axis=0, keepdims=True)
    out = dot_nt(active, down_ref[...])
    dx = dot_nt(grad, up_ref[...])

    @pl.when(pl.program_id(0) == 0)
    def _():
        out_ref[...] = out
        dx_ref[...] = dx

    @pl.when(pl.program_id(0) != 0)
    def _():
        out_ref[...] += out
        dx_ref[...] += dx

    dup_ref[...] = dot_nn(xt_ref[...], grad).astype(LOW)
    ddown_ref[...] = dot_nn(gt_ref[...], active).astype(LOW)


def feed_forward(x, g, up_down, bias):
    rows, width = x.shape
    hidden = bias.shape[1]
    step = 512
    steps = hidden // step

    def whole(shape):
        return pl.BlockSpec(shape, lambda i: (0, 0))

    column = pl.BlockSpec((width, step), lambda i: (0, i))
    return pl.pallas_call(
        feed_kernel,
        grid=(steps,),
        in_specs=[
            whole((rows, width)),
            whole((width, rows)),
            whole((rows, width)),
            whole((width, rows)),
            column,
            pl.BlockSpec((width, step), lambda i: (0, i + steps)),
            pl.BlockSpec((1, step), lambda i: (0, i)),
        ],
        out_specs=[
            whole((rows, width)),
            whole((rows, width)),
            column,
            column,
            pl.BlockSpec((1, step), lambda i: (0, i)),
        ],
        out_shape=[
            jax.ShapeDtypeStruct((rows, width), WIDE),
            jax.ShapeDtypeStruct((rows, width), WIDE),
            jax.ShapeDtypeStruct((width, hidden), LOW),
            jax.ShapeDtypeStruct((width, hidden), LOW),
            jax.ShapeDtypeStruct((1, hidden), WIDE),
        ],
        compiler_params=pltpu.CompilerParams(vmem_limit_bytes=VMEM_ASK),
        cost_estimate=pl.CostEstimate(
            flops=20 * rows * width * hidden, bytes_accessed=12 * width * hidden, transcendentals=0
        ),
        name="feed_forward",
    )(x, x.T, g, g.T, up_down, up_down, bias)


def lane_tiles(array, combine):
    total = array[:, :BLK]
    for i in range(1, array.shape[1] // BLK):
        total = combine(total, array[:, i * BLK : (i + 1) * BLK])
    return total


def gathered_blocks(ref, inverse, chunk, lanes):
    count = CHUNK // BLK
    return jnp.concatenate(
        [
            ref[pl.ds(pl.multiple_of(inverse[chunk * count + i] * BLK, BLK), BLK), lanes]
            for i in range(count)
        ],
        axis=0,
    )


def query_kernel(
    blocks,
    first,
    last,
    inverse,
    q_ref,
    k_ref,
    v_ref,
    d_ref,
    cos_ref,
    sin_ref,
    start_ref,
    att_out,
    dq_out,
    stat_out,
    s_scr,
    p_scr,
    q_scr,
    d_scr,
    m_scr,
    l_scr,
    e_scr,
    o_scr,
):
    pairs = q_ref.shape[1] // BLK
    own = att_out.shape[0] // BLK
    lane = lax.broadcasted_iota(jnp.int32, (BLK, BLK), 1)

    def lanes(pair):
        return slice(pair * BLK, (pair + 1) * BLK)

    @pl.loop(0, own)
    def _(j):
        row0 = pl.multiple_of(blocks[j] * BLK, BLK)
        out0 = pl.multiple_of(j * BLK, BLK)
        lo = first[j]
        hi = last[j]
        for g in range(pairs):
            q_scr[g] = two_heads(q_ref[pl.ds(out0, BLK), lanes(g)].astype(WIDE), lane).astype(
                LOW
            ) * LOW(SCALE)
            d_scr[g] = two_heads(d_ref[pl.ds(out0, BLK), lanes(g)].astype(WIDE), lane).astype(LOW)
        m_scr[...] = jnp.full(m_scr.shape, NEG_BIG, WIDE)
        l_scr[...] = jnp.zeros(l_scr.shape, WIDE)
        e_scr[...] = jnp.zeros(e_scr.shape, WIDE)
        o_scr[...] = jnp.zeros(o_scr.shape, WIDE)
        starts = start_ref[pl.ds(out0, BLK), :]
        places = row0 + lax.broadcasted_iota(jnp.int32, (BLK, 1), 0)
        starts = jnp.concatenate([starts, starts], axis=0)
        places = jnp.concatenate([places, places], axis=0)

        @pl.loop(lo, hi)
        def _(c):
            key0 = pl.multiple_of(c * CHUNK, CHUNK)
            key_place = key0 + lax.broadcasted_iota(jnp.int32, (2 * BLK, CHUNK), 1)
            allowed = (key_place >= starts) & (key_place <= places)
            for g in range(pairs):
                scores = dot_nt(q_scr[g], gathered_blocks(k_ref, inverse, c, lanes(g)))
                scores = jnp.where(allowed, scores, NEG_BIG)
                s_scr[g, c - lo] = scores
                m_scr[g] = jnp.maximum(m_scr[g], lane_tiles(scores, jnp.maximum))

        for g in range(pairs):
            m_scr[g] = jnp.broadcast_to(
                jnp.max(m_scr[g], axis=1, keepdims=True), (2 * BLK, BLK)
            )

        @pl.loop(lo, hi)
        def _(c):
            for g in range(pairs):
                values = gathered_blocks(v_ref, inverse, c, lanes(g))
                top = m_scr[g]
                weights = jnp.exp(s_scr[g, c - lo] - jnp.concatenate([top] * (CHUNK // BLK), 1))
                l_scr[g] += lane_tiles(weights, jnp.add)
                o_scr[g] += dot_nn(weights.astype(LOW), values)
                grad_prob = dot_nt(d_scr[g], values)
                e_scr[g] += lane_tiles(weights * grad_prob, jnp.add)
                s_scr[g, c - lo] = weights
                p_scr[g, c - lo] = grad_prob

        for g in range(pairs):
            total = jnp.sum(l_scr[g], axis=1, keepdims=True)
            share = 1.0 / total
            delta = jnp.sum(e_scr[g], axis=1, keepdims=True) * share
            att_out[pl.ds(out0, BLK), lanes(g)] = one_of_two(o_scr[g] * share, lane).astype(LOW)
            log_sum = m_scr[g] + jnp.log(total)
            stat_out[j, 2 * g : 2 * g + 1, :] = log_sum[:BLK].T[0:1]
            stat_out[j, 2 * g + 1 : 2 * g + 2, :] = log_sum[BLK:].T[0:1]
            wide = jnp.broadcast_to(delta, (2 * BLK, BLK))
            base = stat_out.shape[1] // 2 + 2 * g
            stat_out[j, base : base + 1, :] = wide[:BLK].T[0:1]
            stat_out[j, base + 1 : base + 2, :] = wide[BLK:].T[0:1]
            l_scr[g] = jnp.broadcast_to(share, (2 * BLK, BLK))
            e_scr[g] = wide
        o_scr[...] = jnp.zeros(o_scr.shape, WIDE)

        @pl.loop(lo, hi)
        def _(c):
            for g in range(pairs):
                wide = jnp.concatenate([e_scr[g]] * (CHUNK // BLK), 1)
                grad_score = s_scr[g, c - lo] * (p_scr[g, c - lo] - wide)
                o_scr[g] += dot_nn(
                    grad_score.astype(LOW), gathered_blocks(k_ref, inverse, c, lanes(g))
                )

        cosine = cos_ref[pl.ds(out0, BLK), :]
        sine = sin_ref[pl.ds(out0, BLK), :]
        for g in range(pairs):
            grad = one_of_two(o_scr[g] * l_scr[g], lane) * SCALE
            dq_out[pl.ds(out0, BLK), lanes(g)] = turned(grad, cosine, -sine, lane).astype(LOW)


def smem():
    return pl.BlockSpec(memory_space=pltpu.SMEM)


def vmem():
    return pl.BlockSpec(memory_space=pltpu.VMEM)


def query_side(blocks, first, last, inverse, queries, keys, values, grads, cosine, sine, starts):
    own = blocks.shape[0]
    width = queries.shape[1]
    pairs = width // BLK
    stat_rows = 16 * ((2 * pairs + 7) // 8)
    work = 2 * BLK * CHUNK
    return pl.pallas_call(
        query_kernel,
        in_specs=[smem()] * 4 + [vmem()] * 7,
        out_specs=[vmem()] * 3,
        out_shape=[
            jax.ShapeDtypeStruct((own * BLK, width), LOW),
            jax.ShapeDtypeStruct((own * BLK, width), LOW),
            jax.ShapeDtypeStruct((own, stat_rows, BLK), WIDE),
        ],
        scratch_shapes=[
            pltpu.VMEM((pairs, SPAN, 2 * BLK, CHUNK), WIDE),
            pltpu.VMEM((pairs, SPAN, 2 * BLK, CHUNK), WIDE),
            pltpu.VMEM((pairs, 2 * BLK, BLK), LOW),
            pltpu.VMEM((pairs, 2 * BLK, BLK), LOW),
            pltpu.VMEM((pairs, 2 * BLK, BLK), WIDE),
            pltpu.VMEM((pairs, 2 * BLK, BLK), WIDE),
            pltpu.VMEM((pairs, 2 * BLK, BLK), WIDE),
            pltpu.VMEM((pairs, 2 * BLK, BLK), WIDE),
        ],
        compiler_params=pltpu.CompilerParams(vmem_limit_bytes=VMEM_ASK),
        cost_estimate=pl.CostEstimate(
            flops=own * pairs * 12 * 4 * 2 * work * BLK,
            bytes_accessed=4 * keys.shape[0] * width * 2,
            transcendentals=own * pairs * 4 * work,
        ),
        name="query_side",
    )(blocks, first, last, inverse, queries, keys, values, grads, cosine, sine, starts)


def key_kernel(
    blocks,
    first,
    last,
    inverse,
    q_ref,
    k_ref,
    v_ref,
    d_ref,
    cos_ref,
    sin_ref,
    end_ref,
    stat_ref,
    dk_out,
    dv_out,
    k_scr,
    v_scr,
    dk_scr,
    dv_scr,
):
    pairs = q_ref.shape[1] // BLK
    own = dk_out.shape[0] // BLK
    half_stat = stat_ref.shape[1] // 2
    lane = lax.broadcasted_iota(jnp.int32, (BLK, BLK), 1)

    def lanes(pair):
        return slice(pair * BLK, (pair + 1) * BLK)

    @pl.loop(0, own)
    def _(j):
        row0 = pl.multiple_of(blocks[j] * BLK, BLK)
        out0 = pl.multiple_of(j * BLK, BLK)
        for g in range(pairs):
            k_scr[g] = two_heads(k_ref[pl.ds(out0, BLK), lanes(g)].astype(WIDE), lane).astype(
                LOW
            ) * LOW(SCALE)
            v_scr[g] = two_heads(v_ref[pl.ds(out0, BLK), lanes(g)].astype(WIDE), lane).astype(LOW)
        dk_scr[...] = jnp.zeros(dk_scr.shape, WIDE)
        dv_scr[...] = jnp.zeros(dv_scr.shape, WIDE)
        ends = end_ref[pl.ds(out0, BLK), :]
        places = row0 + lax.broadcasted_iota(jnp.int32, (BLK, 1), 0)

        @pl.loop(first[j], last[j])
        def _(c):
            query0 = pl.multiple_of(c * CHUNK, CHUNK)
            query_place = query0 + lax.broadcasted_iota(jnp.int32, (BLK, CHUNK), 1)
            allowed = (query_place >= places) & (query_place < ends)
            count = CHUNK // BLK
            slots = [inverse[c * count + i] for i in range(count)]

            def stat(row):
                return jnp.concatenate([stat_ref[slot, row : row + 1, :] for slot in slots], 1)

            for g in range(pairs):
                queries = gathered_blocks(q_ref, inverse, c, lanes(g))
                grads = gathered_blocks(d_ref, inverse, c, lanes(g))
                scores = dot_nt(k_scr[g], queries)
                grad_prob = dot_nt(v_scr[g], grads)
                probs, grad_scores = [], []
                for h in range(2):
                    rows = slice(h * BLK, (h + 1) * BLK)
                    shifted = jnp.where(allowed, scores[rows] - stat(2 * g + h), NEG_BIG)
                    prob = jnp.exp(shifted)
                    probs.append(prob.astype(LOW))
                    grad_scores.append(
                        (prob * (grad_prob[rows] - stat(half_stat + 2 * g + h))).astype(LOW)
                    )
                dv_scr[g] += dot_nn(jnp.concatenate(probs, 0), grads)
                dk_scr[g] += dot_nn(jnp.concatenate(grad_scores, 0), queries)

        cosine = cos_ref[pl.ds(out0, BLK), :]
        sine = sin_ref[pl.ds(out0, BLK), :]
        for g in range(pairs):
            grad = one_of_two(dk_scr[g], lane) * SCALE
            dk_out[pl.ds(out0, BLK), lanes(g)] = turned(grad, cosine, -sine, lane).astype(LOW)
            dv_out[pl.ds(out0, BLK), lanes(g)] = one_of_two(dv_scr[g], lane).astype(LOW)


def key_side(
    blocks, first, last, inverse, queries, keys, values, grads, cosine, sine, ends, stats
):
    own = blocks.shape[0]
    width = queries.shape[1]
    pairs = width // BLK
    work = 2 * BLK * CHUNK
    return pl.pallas_call(
        key_kernel,
        in_specs=[smem()] * 4 + [vmem()] * 8,
        out_specs=[vmem()] * 2,
        out_shape=[jax.ShapeDtypeStruct((own * BLK, width), LOW)] * 2,
        scratch_shapes=[
            pltpu.VMEM((pairs, 2 * BLK, BLK), LOW),
            pltpu.VMEM((pairs, 2 * BLK, BLK), LOW),
            pltpu.VMEM((pairs, 2 * BLK, BLK), WIDE),
            pltpu.VMEM((pairs, 2 * BLK, BLK), WIDE),
        ],
        compiler_params=pltpu.CompilerParams(vmem_limit_bytes=VMEM_ASK),
        cost_estimate=pl.CostEstimate(
            flops=own * pairs * 12 * 4 * 2 * work * BLK,
            bytes_accessed=4 * keys.shape[0] * width * 2,
            transcendentals=own * pairs * 4 * work,
        ),
        name="key_side",
    )(blocks, first, last, inverse, queries, keys, values, grads, cosine, sine, ends, stats)


TILE = 256


def symmetric_product(out_ref, left, right, depth):
    size = out_ref.shape[0]
    for i in range(0, size, TILE):
        out_ref[i : i + TILE, i:] = dot_nt(left[i : i + TILE, :depth], right[i:, :depth])
    for i in range(0, size, TILE):
        for j in range(i + TILE, size, TILE):
            out_ref[j : j + TILE, i : i + TILE] = out_ref[i : i + TILE, j : j + TILE].T


def ns_matrix(span, near, far, out_ref, wide_scr, low_scr, gram_scr, poly_scr):
    half = span // 2
    step = 768
    cuts = [slice(i, i + step) for i in range(0, span, step)]
    total = jnp.zeros((1, 1), WIDE)
    for source, base in ((near, 0), (far, half)):
        for i in range(0, half, 384):
            part = source[:, i : i + 384].astype(WIDE)
            wide_scr[:, base + i : base + i + 384] = part
            total = total + jnp.sum(part * part)
    factor = 1.0 / (jnp.sqrt(total) + 1e-7)
    for cut in cuts:
        part = wide_scr[:, cut] * factor
        wide_scr[:, cut] = part
        low_scr[:, cut] = part.astype(LOW)

    def polynomial():
        symmetric_product(gram_scr, low_scr, low_scr, span)
        poly_scr[...] = gram_scr[...].astype(LOW)
        first = gram_scr[...] * NS_COEF[1]
        symmetric_product(gram_scr, poly_scr, poly_scr, poly_scr.shape[1])
        poly_scr[...] = (first + NS_COEF[2] * gram_scr[...]).astype(LOW)

    @pl.loop(0, NS_STEPS - 1)
    def _(_):
        polynomial()
        for cut in cuts:
            part = NS_COEF[0] * wide_scr[:, cut] + dot_nn(poly_scr[...], low_scr[:, cut])
            wide_scr[:, cut] = part
            low_scr[:, cut] = part.astype(LOW)

    polynomial()
    rows = out_ref.shape[0]
    for i in range(0, half, 384):
        cut = slice(i, i + 384)
        out_ref[:, cut] = (
            NS_COEF[0] * wide_scr[:rows, cut] + dot_nn(poly_scr[:rows, :], low_scr[:, cut])
        ).astype(LOW)


def ns_kernel(spans, high, near_a, far_a, near_b, far_b, out_ref, *scratch):
    out_ref[...] = jnp.zeros(out_ref.shape, LOW)
    widest = max(spans)
    for span in sorted(set(spans)):
        wanted = jnp.bool_(False)
        for owner, own_span in enumerate(spans):
            if own_span == span:
                wanted = wanted | (high[0] == owner)

        @pl.when(wanted)
        def _():
            near, far = (near_a, far_a) if span == widest else (near_b, far_b)
            ns_matrix(span, near, far, out_ref, *scratch)


def orthogonal_rows(spans, high, wide_pair, short_pair, rows):
    size, half = wide_pair[0].shape
    kept = rows if rows % 16 == 0 else size
    out = pl.pallas_call(
        partial(ns_kernel, spans),
        in_specs=[smem()] + [vmem()] * 4,
        out_specs=vmem(),
        out_shape=jax.ShapeDtypeStruct((kept, half), LOW),
        scratch_shapes=[
            pltpu.VMEM((size, 2 * half), WIDE),
            pltpu.VMEM((size, 2 * half), LOW),
            pltpu.VMEM((size, size), WIDE),
            pltpu.VMEM((size, size), LOW),
        ],
        compiler_params=pltpu.CompilerParams(vmem_limit_bytes=VMEM_ASK),
        cost_estimate=pl.CostEstimate(
            flops=NS_STEPS * 10 * size * size * half,
            bytes_accessed=8 * size * half,
            transcendentals=0,
        ),
        name="orthogonal_rows",
    )(high, *wide_pair, *short_pair)
    return out[:rows]


def rotary_tables(places):
    half = ROT // 2
    exponent = jnp.arange(0, ROT, 2, dtype=WIDE) / ROT
    frequency = 1.0 / 10000.0**exponent
    angles = frequency[:, None] * places.astype(WIDE)[None, :]
    lane = jnp.arange(BLK) % HD
    picked = ((lane % half)[None, :] == jnp.arange(half)[:, None]) & (lane < ROT)[None, :]
    sign = jnp.where(lane < half, -1.0, 1.0)[None, :]
    spread = partial(
        jnp.einsum, "fn,fl->nl", precision=lax.Precision.HIGHEST, preferred_element_type=WIDE
    )
    cosine = spread(jnp.cos(angles), picked.astype(WIDE)) + (lane >= ROT)[None, :].astype(WIDE)
    return cosine, spread(jnp.sin(angles), picked * sign)


def body(
    tokens,
    cotangent,
    w_qkv,
    w_attn,
    w_up,
    w_down,
    norm_vectors,
    qkv_bias,
    up_bias,
    qkv_moment,
    attn_moment,
    up_moment,
    down_moment,
    norm_moment,
    qbias_moment,
    ubias_moment,
    seq_lengths,
    block_source,
):
    row_count, half = tokens.shape
    fsdp_count = lax.axis_size("fsdp")
    ctx_count = lax.axis_size("ctx")
    tp_index = lax.axis_index("tp")
    fsdp_index = lax.axis_index("fsdp")
    ctx_index = lax.axis_index("ctx")
    low_count = ctx_count // OWNERS
    ctx_low = ctx_index % low_count
    ctx_high = ctx_index // low_count
    width = 2 * half
    own_blocks = row_count // BLK
    pack = ctx_count * row_count
    first_tp = tp_index == 0
    block_row = block_source[0]
    length_row = seq_lengths[0]

    def both_halves(mine, other, dim):
        return jnp.concatenate(
            [jnp.where(first_tp, mine, other), jnp.where(first_tp, other, mine)], axis=dim
        )

    def own_half(array):
        return jnp.where(first_tp, array[:, :half], array[:, half:])

    def far_half(array):
        return jnp.where(first_tp, array[:, half:], array[:, :half])

    own_pair = jnp.concatenate([tokens, cotangent], axis=1)
    far_pair = partner(own_pair, "tp", 1)
    inputs_low = both_halves(tokens, far_pair[:, :half], 1)
    full_cotangent = both_halves(cotangent, far_pair[:, half:], 1)

    near = [own_pair] + [partner(own_pair, "ctx", s * low_count) for s in range(1, OWNERS)]
    near_parts = [jnp.concatenate(near, axis=0)]
    for s in range(1, low_count):
        near_parts.append(jnp.concatenate([partner(part, "ctx", s) for part in near], axis=0))
    far_parts = [partner(part, "tp", 1) for part in near_parts]

    joint_full = gather_axis(
        jnp.concatenate(
            [w_qkv.astype(LOW).reshape(w_qkv.shape[0], 3 * half), w_attn.astype(LOW).T], axis=1
        ),
        "fsdp",
        0,
    )
    up_down = lax.all_gather(
        jnp.concatenate([w_up.astype(LOW), w_down.astype(LOW).T], axis=1),
        "fsdp",
        axis=0,
        tiled=True,
    )

    def group_place(ctx):
        differs = ctx ^ ctx_index
        return (differs % low_count) * OWNERS + differs // low_count

    slot_blocks = jnp.arange(block_row.shape[0], dtype=jnp.int32)
    slot_places = group_place(slot_blocks // own_blocks) * own_blocks + slot_blocks % own_blocks
    inverse = jnp.sum(
        jnp.where(block_row[None, :] == slot_blocks[:, None], slot_places[None, :], 0), axis=1
    ).astype(jnp.int32)
    my_blocks = lax.dynamic_slice_in_dim(block_row, ctx_index * own_blocks, own_blocks)

    seq_ends = jnp.cumsum(length_row).astype(jnp.int32)
    seq_starts = seq_ends - length_row

    def bounds(packed):
        inside = (packed[:, None] >= seq_starts[None, :]) & (packed[:, None] < seq_ends[None, :])
        return (
            jnp.sum(jnp.where(inside, seq_starts[None, :], 0), axis=1).astype(jnp.int32),
            jnp.sum(jnp.where(inside, seq_ends[None, :], 0), axis=1).astype(jnp.int32),
        )

    group_blocks = jnp.sum(
        jnp.where(slot_places[None, :] == slot_blocks[:, None], block_row[None, :], 0), axis=1
    )
    offsets = jnp.arange(BLK, dtype=jnp.int32)
    packed = (group_blocks[:, None] * BLK + offsets[None, :]).reshape(-1)
    cosine, sine = rotary_tables(packed - bounds(packed)[0])
    my_starts, my_ends = bounds(
        (my_blocks[:, None] * BLK + offsets[None, :]).reshape(-1)
    )
    key_first = bounds(my_blocks * BLK)[0] // CHUNK
    key_last = (my_blocks * BLK + BLK - 1) // CHUNK + 1
    query_first = my_blocks * BLK // CHUNK
    query_last = (bounds(my_blocks * BLK + BLK - 1)[1] + CHUNK - 1) // CHUNK

    def own_first(array, dim):
        left, right = jnp.split(array, 2, axis=dim)
        return jnp.where(first_tp, left, right), jnp.where(first_tp, right, left)

    projections = (
        *own_first(joint_full, 0),
        qkv_bias.reshape(1, 3 * half),
        *own_first(norm_vectors, 1),
    )
    made = ()
    for part, (near_part, far_part) in enumerate(zip(near_parts, far_parts)):
        made = project_rows(
            part, pack, near_part, far_part, projections, cosine, sine, made
        )
    queries, keys, values, d_attended = made

    inputs = inputs_low.astype(WIDE)
    centered = inputs - jnp.mean(inputs, axis=1, keepdims=True)
    inv_std = lax.rsqrt(jnp.mean(centered * centered, axis=1, keepdims=True) + 1e-05)
    normed = centered * inv_std
    norm_out = (normed * norm_vectors[0] + norm_vectors[1]).astype(LOW)
    hidden_here = up_bias.shape[0]
    feed_out, feed_dx, grad_up, grad_down, grad_ubias = feed_forward(
        norm_out, full_cotangent, up_down, up_bias.reshape(1, hidden_here)
    )

    def outer(left, right):
        return jnp.einsum("na,nb->ab", left, right, preferred_element_type=WIDE).astype(LOW)

    def reduced_first(gradient):
        rows = gradient.shape[0] // fsdp_count
        return sum_scatter(
            gradient.reshape(fsdp_count, rows, gradient.shape[1]), "fsdp", 1, fsdp_index
        )

    def reduced_rest(part):
        piece = part.shape[0] // ctx_count
        part = part.reshape(OWNERS, low_count, piece, part.shape[1])
        part = sum_scatter(jnp.swapaxes(part, 0, 1), "ctx", 1, ctx_low)
        return sum_scatter(part, "ctx", low_count, ctx_high)

    sum_up = reduced_rest(reduced_first(grad_up))
    sum_down = reduced_rest(reduced_first(grad_down))
    piece = sum_up.shape[0]
    grad_outbias = jnp.sum(cotangent.astype(WIDE), axis=0)

    def all_rows(*sums):
        joined = jnp.concatenate(sums, axis=1).astype(LOW)
        return lax.all_gather(joined, "ctx", axis=0, tiled=True).astype(WIDE)

    all_up, all_down = jnp.split(all_rows(sum_up, sum_down), 2, axis=1)
    fresh_up = 0.95 * up_moment + all_up
    fresh_down = 0.95 * down_moment + all_down.T

    def my_rows(array, dim):
        return lax.dynamic_slice_in_dim(array, ctx_index * piece, piece, dim)

    def as_rows(up, attn, qkv, down):
        return (
            my_rows(up, 0),
            my_rows(attn, 1).T,
            my_rows(qkv, 0).reshape(piece, 3 * half),
            my_rows(down, 1).T,
        )

    spans = (2 * hidden_here, 2 * half, 6 * half, 2 * hidden_here)
    old_moments = as_rows(up_moment, attn_moment, qkv_moment, down_moment)

    def to_owners(pieces):
        owners = tuple(pieces)
        low, high = pieces[owners[0]].astype(LOW), pieces[owners[1]].astype(LOW)

        def wanted(index):
            return index // low_count in owners

        rows = [jnp.where(ctx_high == owners[0], low, high)]
        for s in range(1, OWNERS):
            sent = jnp.where(ctx_high ^ s == owners[0], low, high)
            rows.append(partner_among(sent, ("ctx",), (s * low_count,), lambda i: wanted(i[0])))
        parts = [jnp.concatenate(rows, axis=0)]
        for s in range(1, low_count):
            parts.append(partner_among(parts[0], ("ctx",), (s,), lambda i: wanted(i[0])))
        for s in range(1, fsdp_count):
            parts += [
                partner_among(part, ("fsdp", "ctx"), (s, 0), lambda i: wanted(i[1]))
                for part in parts[:low_count]
            ]
        others = [
            partner_among(part, ("ctx", "tp"), (0, 1), lambda i: wanted(i[0])) for part in parts
        ]
        return jnp.concatenate(parts, axis=0), jnp.concatenate(others, axis=0)

    wide_pair = to_owners(
        {0: 0.95 * old_moments[0] + sum_up, 3: 0.95 * old_moments[3] + sum_down}
    )

    attended, grad_q, stats = query_side(
        my_blocks,
        key_first,
        key_last,
        inverse,
        queries,
        keys,
        values,
        d_attended,
        cosine,
        sine,
        my_starts[:, None],
    )
    sum_early = reduced_rest(
        reduced_first(
            jnp.concatenate([outer(norm_out, grad_q), outer(full_cotangent, attended)], axis=1)
        )
    )
    near_stats = [stats] + [partner(stats, "ctx", s * low_count) for s in range(1, OWNERS)]
    all_stats = list(near_stats)
    for s in range(1, low_count):
        all_stats += [partner(part, "ctx", s) for part in near_stats]
    grad_k, grad_v = key_side(
        my_blocks,
        query_first,
        query_last,
        inverse,
        queries,
        keys,
        values,
        d_attended,
        cosine,
        sine,
        my_ends[:, None],
        jnp.concatenate(all_stats, axis=0),
    )
    grad_late = outer(norm_out, jnp.concatenate([grad_k, grad_v], axis=1))
    late_rows = reduced_first(grad_late)
    sum_late = reduced_rest(late_rows)
    grad_q, grad_k, grad_v, grad_late = lax.optimization_barrier(
        (grad_q, grad_k, grad_v, grad_late)
    )
    grad_proj = jnp.concatenate([grad_q, grad_k, grad_v], axis=1)
    grad_qbias = jnp.sum(grad_proj.astype(WIDE), axis=0)

    partial_out = dot_nt(attended, joint_full[:, 3 * half :]) + feed_out

    def sum_halves(array):
        return own_half(array) + partner(far_half(array).astype(LOW), "tp", 1).astype(WIDE)

    out_bias = own_half((norm_vectors[2] + norm_vectors[3])[None, :])
    mixed = (tokens.astype(WIDE) + sum_halves(partial_out) + out_bias).astype(LOW)

    grad_norm = sum_halves(dot_nt(grad_proj, joint_full[:, : 3 * half]) + feed_dx)
    my_normed = own_half(normed)
    scaled = grad_norm * own_half(norm_vectors[0:1])
    row_sums = jnp.stack([jnp.sum(scaled, axis=1), jnp.sum(scaled * my_normed, axis=1)])
    row_means = (row_sums + partner(row_sums, "tp", 1)) / width
    grad_tokens = cotangent.astype(WIDE) + inv_std * (
        scaled - row_means[0][:, None] - my_normed * row_means[1][:, None]
    )

    vector_parts = jnp.stack(
        [jnp.sum(grad_norm * my_normed, axis=0), jnp.sum(grad_norm, axis=0), grad_outbias]
    )
    small = jnp.concatenate([vector_parts.reshape(-1), grad_qbias, grad_ubias[0]])
    small = sum_everywhere(small, ("ctx",))
    small = sum_everywhere(lax.optimization_barrier((small, late_rows))[0], ("fsdp",))
    mine = small[: 3 * half].reshape(3, half)
    vectors = both_halves(mine, partner(mine, "tp", 1), 1)
    sum_vectors = jnp.concatenate([vectors, vectors[2:3]], axis=0)
    sum_qbias = small[3 * half : 6 * half].reshape(3, half)
    sum_ubias = small[6 * half :]

    sum_qkv = jnp.concatenate([sum_early[:, :half], sum_late], axis=1)
    sum_attn = sum_early[:, half:]
    gathered = all_rows(sum_qkv, sum_attn)
    fresh_qkv = 0.95 * qkv_moment + gathered[:, : 3 * half].reshape(qkv_moment.shape)
    fresh_attn = 0.95 * attn_moment + gathered[:, 3 * half :].T
    own_attn = jnp.pad(0.95 * old_moments[1] + sum_attn, ((0, 0), (0, 2 * half)))
    short_pair = to_owners({1: own_attn, 2: 0.95 * old_moments[2] + sum_qkv})
    rows_out = orthogonal_rows(
        spans, ctx_high.reshape(1), wide_pair, short_pair, OWNERS * piece
    ).reshape(OWNERS, piece, hidden_here)
    returned = jnp.stack(
        [rows_out[0]]
        + [partner(rows_out[s], "ctx", s * low_count) for s in range(1, OWNERS)]
    )
    orthogonal = [
        lax.dynamic_index_in_dim(returned, ctx_high ^ m, 0, keepdims=False).astype(WIDE)
        for m in range(OWNERS)
    ]
    full_hidden = hidden_here * 2
    olds = as_rows(w_up, w_attn, w_qkv, w_down)
    rates = (
        0.5 * math.sqrt(full_hidden / width),
        0.5 * math.sqrt(width / (width // HD)),
        0.5 * math.sqrt(3 * width / width),
        0.5 * math.sqrt(full_hidden / full_hidden),
    )
    new_up, new_attn, new_qkv, new_down = (
        old - rate * made[:, : old.shape[1]] for old, rate, made in zip(olds, rates, orthogonal)
    )

    vector_rate = 0.3 / math.sqrt(row_count * fsdp_count * ctx_count)
    mom_norm = 0.9 * norm_moment + sum_vectors
    mom_qbias = 0.9 * qbias_moment + sum_qbias
    mom_ubias = 0.9 * ubias_moment + sum_ubias
    return (
        mixed,
        grad_tokens,
        fresh_qkv,
        new_qkv.reshape(piece, 3, half),
        fresh_attn,
        new_attn.T,
        fresh_up,
        new_up,
        fresh_down,
        new_down.T,
        mom_norm,
        norm_vectors - vector_rate * mom_norm,
        mom_qbias,
        qkv_bias - vector_rate * mom_qbias,
        mom_ubias,
        up_bias - vector_rate * mom_ubias,
    )


def solution(mesh):
    return jax.shard_map(
        body,
        mesh=mesh,
        in_specs=(
            P(("fsdp", "ctx"), "tp"),
            P(("fsdp", "ctx"), "tp"),
            P("fsdp", None, "tp"),
            P("tp", "fsdp"),
            P("fsdp", "tp"),
            P("tp", "fsdp"),
            P(),
            P(None, "tp"),
            P("tp"),
            P("fsdp", None, "tp"),
            P("tp", "fsdp"),
            P("fsdp", "tp"),
            P("tp", "fsdp"),
            P(),
            P(None, "tp"),
            P("tp"),
            P("fsdp", None),
            P("fsdp", None),
        ),
        out_specs=(
            P(("fsdp", "ctx"), "tp"),
            P(("fsdp", "ctx"), "tp"),
            P("fsdp", None, "tp"),
            P(("fsdp", "ctx"), None, "tp"),
            P("tp", "fsdp"),
            P("tp", ("fsdp", "ctx")),
            P("fsdp", "tp"),
            P(("fsdp", "ctx"), "tp"),
            P("tp", "fsdp"),
            P("tp", ("fsdp", "ctx")),
            P(),
            P(),
            P(None, "tp"),
            P(None, "tp"),
            P("tp"),
            P("tp"),
        ),
        check_vma=False,
    )
```

```python
from functools import partial
import math

import jax
import jax.numpy as jnp
from jax import lax
from jax.experimental import pallas as pl
from jax.experimental.pallas import tpu as pltpu
from jax.sharding import PartitionSpec as P

HD = 64
ROT = 16
BLK = 128
NS_STEPS = 5
CHUNK = 512
MAX_LEN = 2048
SPAN = (MAX_LEN + BLK) // CHUNK + 2
OWNERS = 4
NS_COEF = (3.4445, -4.775, 2.0315)
NEG_BIG = -1e30
SCALE = HD**-0.5
LOW = jnp.bfloat16
WIDE = jnp.float32
NT = (((1,), (1,)), ((), ()))
VMEM_ASK = 56 * 1024 * 1024


def dot_nn(left, right):
    return jnp.dot(left, right, preferred_element_type=WIDE)


def dot_nt(left, right):
    return lax.dot_general(left, right, NT, preferred_element_type=WIDE)


def partner(value, axis, step):
    size = lax.axis_size(axis)
    return lax.ppermute(value, axis, [(i, i ^ step) for i in range(size)])


def partner_among(value, axes, strides, wanted):
    sizes = [lax.axis_size(axis) for axis in axes]
    pairs = []
    for flat in range(math.prod(sizes)):
        index, rest = [], flat
        for size in reversed(sizes):
            index.insert(0, rest % size)
            rest //= size
        if wanted(index):
            source = 0
            for size, i, stride in zip(sizes, index, strides):
                source = source * size + (i ^ stride)
            pairs.append((source, flat))
    return lax.ppermute(value, tuple(axes), pairs)


def sum_scatter(pieces, axis, stride, index):
    count = pieces.shape[0]
    total = lax.dynamic_index_in_dim(pieces, index, 0, keepdims=False).astype(WIDE)
    for step in range(1, count):
        piece = lax.dynamic_index_in_dim(pieces, index ^ step, 0, keepdims=False)
        total = total + partner(piece.astype(LOW), axis, step * stride).astype(WIDE)
    return total


def gather_axis(shard, axis, dim):
    if lax.axis_size(axis) != 2:
        return lax.all_gather(shard, axis, axis=dim, tiled=True)
    other = partner(shard, axis, 1)
    first = lax.axis_index(axis) == 0
    return jnp.concatenate(
        [jnp.where(first, shard, other), jnp.where(first, other, shard)], axis=dim
    )


def sum_everywhere(value, axes):
    for axis in axes:
        step = 1
        while step < lax.axis_size(axis):
            value = value + partner(value, axis, step)
            step *= 2
    return value


def turned(block, cosine, sine, lane):
    half = ROT // 2
    swapped = jnp.where(
        lane % HD < half, pltpu.roll(block, BLK - half, 1), pltpu.roll(block, half, 1)
    )
    return block * cosine + swapped * sine


def two_heads(block, lane):
    zero = jnp.zeros_like(block)
    return jnp.concatenate(
        [jnp.where(lane < HD, block, zero), jnp.where(lane < HD, zero, block)], axis=0
    )


def one_of_two(stacked, lane):
    return jnp.where(lane < HD, stacked[:BLK], stacked[BLK:])


def project_kernel(
    near, far, w_near, w_far, a_near, a_far, bias, vec_near, vec_far, cos_ref, sin_ref, *outs
):
    outs = outs[-4:]
    rows, half = outs[0].shape
    width = 2 * half
    own, other = near[:rows].astype(WIDE), far[:rows].astype(WIDE)
    mean = (
        jnp.sum(own, axis=1, keepdims=True) + jnp.sum(other, axis=1, keepdims=True)
    ) / width
    own, other = own - mean, other - mean
    var = (
        jnp.sum(own * own, axis=1, keepdims=True) + jnp.sum(other * other, axis=1, keepdims=True)
    ) / width
    inv_std = lax.rsqrt(var + 1e-5)
    own = (own * inv_std * vec_near[0:1] + vec_near[1:2]).astype(LOW)
    other = (other * inv_std * vec_far[0:1] + vec_far[1:2]).astype(LOW)
    lane = lax.broadcasted_iota(jnp.int32, (rows, BLK), 1)
    cosine, sine = cos_ref[...], sin_ref[...]
    for part, out in enumerate(outs[:3]):
        made = dot_nn(own, w_near[part]) + dot_nn(other, w_far[part]) + bias[part : part + 1]
        for pair in range(half // BLK):
            lanes = slice(pair * BLK, (pair + 1) * BLK)
            block = made[:, lanes]
            if part < 2:
                block = turned(block, cosine, sine, lane)
            out[:, lanes] = block.astype(LOW)
    outs[3][...] = (dot_nt(near[rows:], a_near[...]) + dot_nt(far[rows:], a_far[...])).astype(LOW)


def project_rows(place, count, near, far, weights, cosine, sine, made, after):
    rows, half = near.shape[0] // 2, near.shape[1]

    def fixed(array):
        return pl.BlockSpec(array.shape, lambda i: (0,) * array.ndim)

    def placed(width):
        return pl.BlockSpec((rows, width), lambda i: (place, 0))

    extra = tuple(made) + tuple(after)
    before = 4 + len(weights)
    return pl.pallas_call(
        project_kernel,
        grid=(1,),
        in_specs=[fixed(near), fixed(far)]
        + [fixed(w) for w in weights]
        + [placed(BLK)] * 2
        + [pl.BlockSpec(memory_space=pl.ANY)] * len(extra),
        out_specs=[placed(half)] * 4,
        out_shape=[jax.ShapeDtypeStruct((count * rows, half), LOW)] * 4,
        input_output_aliases={before + i: i for i in range(len(made))},
        compiler_params=pltpu.CompilerParams(vmem_limit_bytes=VMEM_ASK),
        cost_estimate=pl.CostEstimate(
            flops=60 * rows * half * half, bytes_accessed=20 * rows * half, transcendentals=0
        ),
        name="project_rows",
    )(near, far, *weights, cosine, sine, *extra)


def feed_kernel(
    x_ref,
    g_ref,
    up_ref,
    down_ref,
    bias_ref,
    out_ref,
    dx_ref,
    dup_ref,
    ddown_ref,
    dbias_ref,
    xt_ref,
    gt_ref,
):
    @pl.when(pl.program_id(0) == 0)
    def _():
        xt_ref[...] = x_ref[...].T
        gt_ref[...] = g_ref[...].T
        out_ref[...] = jnp.zeros(out_ref.shape, WIDE)
        dx_ref[...] = jnp.zeros(dx_ref.shape, WIDE)

    hidden = dot_nn(x_ref[...], up_ref[...]) + bias_ref[...]
    grad = dot_nt(g_ref[...], down_ref[...])
    below = 0.5 + 0.5 * lax.erf(hidden * math.sqrt(0.5))
    density = jnp.exp(-0.5 * hidden * hidden) * (1.0 / math.sqrt(2.0 * math.pi))
    active = (hidden * below).astype(LOW)
    grad = (grad * (below + hidden * density)).astype(LOW)
    dbias_ref[...] = jnp.sum(grad.astype(WIDE), axis=0, keepdims=True)
    out_ref[...] += dot_nn(active, down_ref[...])
    dx_ref[...] += dot_nt(grad, up_ref[...])
    dup_ref[...] = dot_nn(xt_ref[...], grad).astype(LOW)
    ddown_ref[...] = dot_nn(gt_ref[...], active).astype(LOW)


def feed_forward(x, g, up, down, bias):
    rows, width = x.shape
    hidden = bias.shape[1]
    step = 512
    steps = hidden // step

    def whole(shape):
        return pl.BlockSpec(shape, lambda i: (0, 0))

    column = pl.BlockSpec((width, step), lambda i: (0, i))
    line = pl.BlockSpec((1, step), lambda i: (0, i))
    return pl.pallas_call(
        feed_kernel,
        grid=(steps,),
        in_specs=[
            whole((rows, width)),
            whole((rows, width)),
            column,
            pl.BlockSpec((step, width), lambda i: (i, 0)),
            line,
        ],
        out_specs=[
            whole((rows, width)),
            whole((rows, width)),
            column,
            column,
            line,
            whole((width, rows)),
            whole((width, rows)),
        ],
        out_shape=[
            jax.ShapeDtypeStruct((rows, width), WIDE),
            jax.ShapeDtypeStruct((rows, width), WIDE),
            jax.ShapeDtypeStruct((width, hidden), LOW),
            jax.ShapeDtypeStruct((width, hidden), LOW),
            jax.ShapeDtypeStruct((1, hidden), WIDE),
            jax.ShapeDtypeStruct((width, rows), LOW),
            jax.ShapeDtypeStruct((width, rows), LOW),
        ],
        compiler_params=pltpu.CompilerParams(vmem_limit_bytes=VMEM_ASK),
        cost_estimate=pl.CostEstimate(
            flops=26 * rows * width * hidden, bytes_accessed=12 * width * hidden, transcendentals=0
        ),
        name="feed_forward",
    )(x, g, up, down, bias)


def outer_kernel(left_a, right_a, left_b, right_b, out_ref):
    half = right_a.shape[1]
    out_ref[:, :half] = dot_nn(left_a[...], right_a[...]).astype(LOW)
    out_ref[:, half:] = dot_nn(left_b[...], right_b[...]).astype(LOW)


def outer_pair(left_a, right_a, left_b, right_b):
    rows, depth = left_a.shape
    half = right_a.shape[1]
    return pl.pallas_call(
        outer_kernel,
        in_specs=[vmem()] * 4,
        out_specs=vmem(),
        out_shape=jax.ShapeDtypeStruct((rows, 2 * half), LOW),
        compiler_params=pltpu.CompilerParams(vmem_limit_bytes=VMEM_ASK),
        cost_estimate=pl.CostEstimate(
            flops=8 * rows * depth * half, bytes_accessed=6 * rows * depth, transcendentals=0
        ),
        name="outer_pair",
    )(left_a, right_a, left_b, right_b)


def lane_tiles(array, combine):
    total = array[:, :BLK]
    for i in range(1, array.shape[1] // BLK):
        total = combine(total, array[:, i * BLK : (i + 1) * BLK])
    return total


def gathered_blocks(ref, inverse, chunk, lanes):
    count = CHUNK // BLK
    return jnp.concatenate(
        [
            ref[pl.ds(pl.multiple_of(inverse[chunk * count + i] * BLK, BLK), BLK), lanes]
            for i in range(count)
        ],
        axis=0,
    )


def query_kernel(
    blocks,
    first,
    last,
    inverse,
    q_ref,
    k_ref,
    v_ref,
    d_ref,
    cos_ref,
    sin_ref,
    start_ref,
    att_out,
    dq_out,
    stat_out,
    s_scr,
    p_scr,
    q_scr,
    d_scr,
    m_scr,
    l_scr,
    e_scr,
    o_scr,
):
    pairs = q_ref.shape[1] // BLK
    own = att_out.shape[0] // BLK
    lane = lax.broadcasted_iota(jnp.int32, (BLK, BLK), 1)

    def lanes(pair):
        return slice(pair * BLK, (pair + 1) * BLK)

    @pl.loop(0, own)
    def _(j):
        row0 = pl.multiple_of(blocks[j] * BLK, BLK)
        out0 = pl.multiple_of(j * BLK, BLK)
        lo = first[j]
        hi = last[j]
        for g in range(pairs):
            q_scr[g] = two_heads(q_ref[pl.ds(out0, BLK), lanes(g)].astype(WIDE), lane).astype(
                LOW
            ) * LOW(SCALE)
            d_scr[g] = two_heads(d_ref[pl.ds(out0, BLK), lanes(g)].astype(WIDE), lane).astype(LOW)
        m_scr[...] = jnp.full(m_scr.shape, NEG_BIG, WIDE)
        l_scr[...] = jnp.zeros(l_scr.shape, WIDE)
        e_scr[...] = jnp.zeros(e_scr.shape, WIDE)
        o_scr[...] = jnp.zeros(o_scr.shape, WIDE)
        starts = start_ref[pl.ds(out0, BLK), :]
        places = row0 + lax.broadcasted_iota(jnp.int32, (BLK, 1), 0)
        starts = jnp.concatenate([starts, starts], axis=0)
        places = jnp.concatenate([places, places], axis=0)

        @pl.loop(lo, hi)
        def _(c):
            key0 = pl.multiple_of(c * CHUNK, CHUNK)
            key_place = key0 + lax.broadcasted_iota(jnp.int32, (2 * BLK, CHUNK), 1)
            allowed = (key_place >= starts) & (key_place <= places)
            for g in range(pairs):
                scores = dot_nt(q_scr[g], gathered_blocks(k_ref, inverse, c, lanes(g)))
                scores = jnp.where(allowed, scores, NEG_BIG)
                s_scr[g, c - lo] = scores
                m_scr[g] = jnp.maximum(m_scr[g], lane_tiles(scores, jnp.maximum))

        for g in range(pairs):
            m_scr[g] = jnp.broadcast_to(
                jnp.max(m_scr[g], axis=1, keepdims=True), (2 * BLK, BLK)
            )

        @pl.loop(lo, hi)
        def _(c):
            for g in range(pairs):
                values = gathered_blocks(v_ref, inverse, c, lanes(g))
                top = m_scr[g]
                weights = jnp.exp(s_scr[g, c - lo] - jnp.concatenate([top] * (CHUNK // BLK), 1))
                l_scr[g] += lane_tiles(weights, jnp.add)
                o_scr[g] += dot_nn(weights.astype(LOW), values)
                grad_prob = dot_nt(d_scr[g], values)
                e_scr[g] += lane_tiles(weights * grad_prob, jnp.add)
                s_scr[g, c - lo] = weights
                p_scr[g, c - lo] = grad_prob

        for g in range(pairs):
            total = jnp.sum(l_scr[g], axis=1, keepdims=True)
            share = 1.0 / total
            delta = jnp.sum(e_scr[g], axis=1, keepdims=True) * share
            att_out[pl.ds(out0, BLK), lanes(g)] = one_of_two(o_scr[g] * share, lane).astype(LOW)
            log_sum = m_scr[g] + jnp.log(total)
            stat_out[j, 2 * g : 2 * g + 1, :] = log_sum[:BLK].T[0:1]
            stat_out[j, 2 * g + 1 : 2 * g + 2, :] = log_sum[BLK:].T[0:1]
            wide = jnp.broadcast_to(delta, (2 * BLK, BLK))
            base = stat_out.shape[1] // 2 + 2 * g
            stat_out[j, base : base + 1, :] = wide[:BLK].T[0:1]
            stat_out[j, base + 1 : base + 2, :] = wide[BLK:].T[0:1]
            l_scr[g] = jnp.broadcast_to(share, (2 * BLK, BLK))
            e_scr[g] = wide
        o_scr[...] = jnp.zeros(o_scr.shape, WIDE)

        @pl.loop(lo, hi)
        def _(c):
            for g in range(pairs):
                wide = jnp.concatenate([e_scr[g]] * (CHUNK // BLK), 1)
                grad_score = s_scr[g, c - lo] * (p_scr[g, c - lo] - wide)
                o_scr[g] += dot_nn(
                    grad_score.astype(LOW), gathered_blocks(k_ref, inverse, c, lanes(g))
                )

        cosine = cos_ref[pl.ds(out0, BLK), :]
        sine = sin_ref[pl.ds(out0, BLK), :]
        for g in range(pairs):
            grad = one_of_two(o_scr[g] * l_scr[g], lane) * SCALE
            dq_out[pl.ds(out0, BLK), lanes(g)] = turned(grad, cosine, -sine, lane).astype(LOW)


def smem():
    return pl.BlockSpec(memory_space=pltpu.SMEM)


def vmem():
    return pl.BlockSpec(memory_space=pltpu.VMEM)


def query_side(blocks, first, last, inverse, queries, keys, values, grads, cosine, sine, starts):
    own = blocks.shape[0]
    width = queries.shape[1]
    pairs = width // BLK
    stat_rows = 16 * ((2 * pairs + 7) // 8)
    work = 2 * BLK * CHUNK
    return pl.pallas_call(
        query_kernel,
        in_specs=[smem()] * 4 + [vmem()] * 7,
        out_specs=[vmem()] * 3,
        out_shape=[
            jax.ShapeDtypeStruct((own * BLK, width), LOW),
            jax.ShapeDtypeStruct((own * BLK, width), LOW),
            jax.ShapeDtypeStruct((own, stat_rows, BLK), WIDE),
        ],
        scratch_shapes=[
            pltpu.VMEM((pairs, SPAN, 2 * BLK, CHUNK), WIDE),
            pltpu.VMEM((pairs, SPAN, 2 * BLK, CHUNK), WIDE),
            pltpu.VMEM((pairs, 2 * BLK, BLK), LOW),
            pltpu.VMEM((pairs, 2 * BLK, BLK), LOW),
            pltpu.VMEM((pairs, 2 * BLK, BLK), WIDE),
            pltpu.VMEM((pairs, 2 * BLK, BLK), WIDE),
            pltpu.VMEM((pairs, 2 * BLK, BLK), WIDE),
            pltpu.VMEM((pairs, 2 * BLK, BLK), WIDE),
        ],
        compiler_params=pltpu.CompilerParams(vmem_limit_bytes=VMEM_ASK),
        cost_estimate=pl.CostEstimate(
            flops=own * pairs * 12 * 4 * 2 * work * BLK,
            bytes_accessed=4 * keys.shape[0] * width * 2,
            transcendentals=own * pairs * 4 * work,
        ),
        name="query_side",
    )(blocks, first, last, inverse, queries, keys, values, grads, cosine, sine, starts)


def key_kernel(
    blocks,
    first,
    last,
    inverse,
    natural,
    q_ref,
    k_ref,
    v_ref,
    d_ref,
    cos_ref,
    sin_ref,
    end_ref,
    stat_ref,
    *rest,
):
    dk_out, dv_out, k_scr, v_scr, dk_scr, dv_scr = rest[-6:]
    pairs = q_ref.shape[1] // BLK
    own = dk_out.shape[0] // BLK
    half_stat = stat_ref.shape[1] // 2
    lane = lax.broadcasted_iota(jnp.int32, (BLK, BLK), 1)

    def lanes(pair):
        return slice(pair * BLK, (pair + 1) * BLK)

    @pl.loop(0, own)
    def _(j):
        row0 = pl.multiple_of(blocks[j] * BLK, BLK)
        out0 = pl.multiple_of(j * BLK, BLK)
        for g in range(pairs):
            k_scr[g] = two_heads(k_ref[pl.ds(out0, BLK), lanes(g)].astype(WIDE), lane).astype(
                LOW
            ) * LOW(SCALE)
            v_scr[g] = two_heads(v_ref[pl.ds(out0, BLK), lanes(g)].astype(WIDE), lane).astype(LOW)
        dk_scr[...] = jnp.zeros(dk_scr.shape, WIDE)
        dv_scr[...] = jnp.zeros(dv_scr.shape, WIDE)
        ends = end_ref[pl.ds(out0, BLK), :]
        places = row0 + lax.broadcasted_iota(jnp.int32, (BLK, 1), 0)

        @pl.loop(first[j], last[j])
        def _(c):
            query0 = pl.multiple_of(c * CHUNK, CHUNK)
            query_place = query0 + lax.broadcasted_iota(jnp.int32, (BLK, CHUNK), 1)
            allowed = (query_place >= places) & (query_place < ends)
            count = CHUNK // BLK
            slots = [natural[c * count + i] for i in range(count)]

            def stat(row):
                return jnp.concatenate([stat_ref[slot, row : row + 1, :] for slot in slots], 1)

            for g in range(pairs):
                queries = gathered_blocks(q_ref, inverse, c, lanes(g))
                grads = gathered_blocks(d_ref, inverse, c, lanes(g))
                scores = dot_nt(k_scr[g], queries)
                grad_prob = dot_nt(v_scr[g], grads)
                probs, grad_scores = [], []
                for h in range(2):
                    rows = slice(h * BLK, (h + 1) * BLK)
                    shifted = jnp.where(allowed, scores[rows] - stat(2 * g + h), NEG_BIG)
                    prob = jnp.exp(shifted)
                    probs.append(prob.astype(LOW))
                    grad_scores.append(
                        (prob * (grad_prob[rows] - stat(half_stat + 2 * g + h))).astype(LOW)
                    )
                dv_scr[g] += dot_nn(jnp.concatenate(probs, 0), grads)
                dk_scr[g] += dot_nn(jnp.concatenate(grad_scores, 0), queries)

        cosine = cos_ref[pl.ds(out0, BLK), :]
        sine = sin_ref[pl.ds(out0, BLK), :]
        for g in range(pairs):
            grad = one_of_two(dk_scr[g], lane) * SCALE
            dk_out[pl.ds(out0, BLK), lanes(g)] = turned(grad, cosine, -sine, lane).astype(LOW)
            dv_out[pl.ds(out0, BLK), lanes(g)] = one_of_two(dv_scr[g], lane).astype(LOW)


def key_side(
    blocks,
    first,
    last,
    inverse,
    natural,
    queries,
    keys,
    values,
    grads,
    cosine,
    sine,
    ends,
    stats,
    after,
):
    own = blocks.shape[0]
    width = queries.shape[1]
    pairs = width // BLK
    work = 2 * BLK * CHUNK
    return pl.pallas_call(
        key_kernel,
        in_specs=[smem()] * 5 + [vmem()] * 8 + [pl.BlockSpec(memory_space=pl.ANY)] * len(after),
        out_specs=[vmem()] * 2,
        out_shape=[jax.ShapeDtypeStruct((own * BLK, width), LOW)] * 2,
        scratch_shapes=[
            pltpu.VMEM((pairs, 2 * BLK, BLK), LOW),
            pltpu.VMEM((pairs, 2 * BLK, BLK), LOW),
            pltpu.VMEM((pairs, 2 * BLK, BLK), WIDE),
            pltpu.VMEM((pairs, 2 * BLK, BLK), WIDE),
        ],
        compiler_params=pltpu.CompilerParams(vmem_limit_bytes=VMEM_ASK),
        cost_estimate=pl.CostEstimate(
            flops=own * pairs * 12 * 4 * 2 * work * BLK,
            bytes_accessed=4 * keys.shape[0] * width * 2,
            transcendentals=own * pairs * 4 * work,
        ),
        name="key_side",
    )(
        blocks,
        first,
        last,
        inverse,
        natural,
        queries,
        keys,
        values,
        grads,
        cosine,
        sine,
        ends,
        stats,
        *after,
    )


TILE = 256


def symmetric_product(out_ref, left, right, depth):
    size = out_ref.shape[0]
    for i in range(0, size, TILE):
        out_ref[i : i + TILE, i:] = dot_nt(left[i : i + TILE, :depth], right[i:, :depth])
    for i in range(0, size, TILE):
        for j in range(i + TILE, size, TILE):
            out_ref[j : j + TILE, i : i + TILE] = out_ref[i : i + TILE, j : j + TILE].T


def ns_matrix(span, near, far, out_ref, wide_scr, low_scr, gram_scr, poly_scr):
    half = span // 2
    step = 768
    cuts = [slice(i, i + step) for i in range(0, span, step)]
    pltpu.sync_copy(near.at[:, pl.ds(0, half)], low_scr.at[:, pl.ds(0, half)])
    pltpu.sync_copy(far.at[:, pl.ds(0, half)], low_scr.at[:, pl.ds(half, half)])
    total = jnp.zeros((1, 1), WIDE)
    for cut in cuts:
        part = low_scr[:, cut].astype(WIDE)
        total = total + jnp.sum(part * part)
    factor = 1.0 / (jnp.sqrt(total) + 1e-7)
    for cut in cuts:
        part = low_scr[:, cut].astype(WIDE) * factor
        wide_scr[:, cut] = part
        low_scr[:, cut] = part.astype(LOW)

    def polynomial():
        symmetric_product(gram_scr, low_scr, low_scr, span)
        poly_scr[...] = gram_scr[...].astype(LOW)
        first = gram_scr[...] * NS_COEF[1]
        symmetric_product(gram_scr, poly_scr, poly_scr, poly_scr.shape[1])
        poly_scr[...] = (first + NS_COEF[2] * gram_scr[...]).astype(LOW)

    @pl.loop(0, NS_STEPS - 1)
    def _(_):
        polynomial()
        for cut in cuts:
            part = NS_COEF[0] * wide_scr[:, cut] + dot_nn(poly_scr[...], low_scr[:, cut])
            wide_scr[:, cut] = part
            low_scr[:, cut] = part.astype(LOW)

    polynomial()
    rows = out_ref.shape[0]
    if half < out_ref.shape[1]:
        out_ref[:, half:] = jnp.zeros((rows, out_ref.shape[1] - half), LOW)
    for i in range(0, half, 384):
        cut = slice(i, i + 384)
        out_ref[:, cut] = (
            NS_COEF[0] * wide_scr[:rows, cut] + dot_nn(poly_scr[:rows, :], low_scr[:, cut])
        ).astype(LOW)


def ns_kernel(spans, high, near_a, far_a, near_b, far_b, out_ref, *scratch):
    widest = max(spans)
    for span in sorted(set(spans)):
        wanted = jnp.bool_(False)
        for owner, own_span in enumerate(spans):
            if own_span == span:
                wanted = wanted | (high[0] == owner)

        @pl.when(wanted)
        def _():
            near, far = (near_a, far_a) if span == widest else (near_b, far_b)
            ns_matrix(span, near, far, out_ref, *scratch)


def orthogonal_rows(spans, high, wide_pair, short_pair, rows):
    size, half = wide_pair[0].shape
    kept = rows if rows % 16 == 0 else size
    out = pl.pallas_call(
        partial(ns_kernel, spans),
        in_specs=[smem()] + [pl.BlockSpec(memory_space=pl.ANY)] * 4,
        out_specs=vmem(),
        out_shape=jax.ShapeDtypeStruct((kept, half), LOW),
        scratch_shapes=[
            pltpu.VMEM((size, 2 * half), WIDE),
            pltpu.VMEM((size, 2 * half), LOW),
            pltpu.VMEM((size, size), WIDE),
            pltpu.VMEM((size, size), LOW),
        ],
        compiler_params=pltpu.CompilerParams(vmem_limit_bytes=VMEM_ASK),
        cost_estimate=pl.CostEstimate(
            flops=NS_STEPS * 10 * size * size * half,
            bytes_accessed=8 * size * half,
            transcendentals=0,
        ),
        name="orthogonal_rows",
    )(high, *wide_pair, *short_pair)
    return out[:rows]


def rotary_tables(places):
    half = ROT // 2
    exponent = jnp.arange(0, ROT, 2, dtype=WIDE) / ROT
    frequency = 1.0 / 10000.0**exponent
    angles = frequency[:, None] * places.astype(WIDE)[None, :]
    lane = jnp.arange(BLK) % HD
    picked = ((lane % half)[None, :] == jnp.arange(half)[:, None]) & (lane < ROT)[None, :]
    sign = jnp.where(lane < half, -1.0, 1.0)[None, :]
    spread = partial(
        jnp.einsum, "fn,fl->nl", precision=lax.Precision.HIGHEST, preferred_element_type=WIDE
    )
    cosine = spread(jnp.cos(angles), picked.astype(WIDE)) + (lane >= ROT)[None, :].astype(WIDE)
    return cosine, spread(jnp.sin(angles), picked * sign)


def body(
    tokens,
    cotangent,
    w_qkv,
    w_attn,
    w_up,
    w_down,
    norm_vectors,
    qkv_bias,
    up_bias,
    qkv_moment,
    attn_moment,
    up_moment,
    down_moment,
    norm_moment,
    qbias_moment,
    ubias_moment,
    seq_lengths,
    block_source,
):
    row_count, half = tokens.shape
    fsdp_count = lax.axis_size("fsdp")
    ctx_count = lax.axis_size("ctx")
    tp_index = lax.axis_index("tp")
    fsdp_index = lax.axis_index("fsdp")
    ctx_index = lax.axis_index("ctx")
    low_count = ctx_count // OWNERS
    ctx_low = ctx_index % low_count
    ctx_high = ctx_index // low_count
    width = 2 * half
    own_blocks = row_count // BLK
    pack = ctx_count * row_count
    first_tp = tp_index == 0
    block_row = block_source[0]
    length_row = seq_lengths[0]

    def both_halves(mine, other, dim):
        return jnp.concatenate(
            [jnp.where(first_tp, mine, other), jnp.where(first_tp, other, mine)], axis=dim
        )

    def own_half(array):
        return jnp.where(first_tp, array[:, :half], array[:, half:])

    def far_half(array):
        return jnp.where(first_tp, array[:, half:], array[:, :half])

    own_pair = jnp.concatenate([tokens, cotangent], axis=0)

    def send_high(value, pairs):
        return lax.ppermute(
            value,
            "ctx",
            [(a * low_count + i, b * low_count + i) for a, b in pairs for i in range(low_count)],
        )

    inner = (ctx_high == 1) | (ctx_high == 2)
    between, outward = [(1, 2), (2, 1)], [(1, 0), (2, 3)]
    beside = send_high(own_pair, [(0, 1), (1, 0), (2, 3), (3, 2)])
    middle = send_high(own_pair, between)
    lasting = send_high(beside, between)
    line = [
        own_pair,
        beside,
        jnp.where(inner, middle, send_high(middle, outward)),
        jnp.where(inner, lasting, send_high(lasting, outward)),
    ]
    order = sorted(
        ((low, slot) for low in range(low_count) for slot in range(OWNERS)),
        key=lambda item: (item[1] + (item[0] > 0), item[0]),
    )
    blocks_near = [
        line[slot] if low == 0 else partner(line[slot], "ctx", low) for low, slot in order
    ]
    blocks_far = [partner(block, "tp", 1) for block in blocks_near]
    far_pair = blocks_far[0]
    inputs_low = both_halves(tokens, far_pair[:row_count], 1)
    full_cotangent = both_halves(cotangent, far_pair[row_count:], 1)

    up_full = gather_axis(w_up.astype(LOW), "fsdp", 0)
    down_full = gather_axis(w_down.astype(LOW), "fsdp", 1)
    attn_full = gather_axis(w_attn.astype(LOW), "fsdp", 1)
    qkv_full = lax.all_gather(
        jnp.transpose(w_qkv, (1, 0, 2)).astype(LOW), "fsdp", axis=1, tiled=True
    )

    def group_place(ctx):
        high = ctx // low_count
        slot = jnp.where(
            high == ctx_high,
            0,
            jnp.where(high == ctx_high ^ 1, 1, jnp.where((high == 1) | (high == 2), 2, 3)),
        )
        low = (ctx % low_count) ^ ctx_low
        place = jnp.zeros_like(ctx)
        for k, (its_low, its_slot) in enumerate(order):
            place = jnp.where((low == its_low) & (slot == its_slot), k, place)
        return place

    slot_blocks = jnp.arange(block_row.shape[0], dtype=jnp.int32)
    slot_places = group_place(slot_blocks // own_blocks) * own_blocks + slot_blocks % own_blocks
    holds = block_row[None, :] == slot_blocks[:, None]
    inverse = jnp.sum(jnp.where(holds, slot_places[None, :], 0), axis=1).astype(jnp.int32)
    natural = jnp.sum(jnp.where(holds, slot_blocks[None, :], 0), axis=1).astype(jnp.int32)
    my_blocks = lax.dynamic_slice_in_dim(block_row, ctx_index * own_blocks, own_blocks)

    seq_ends = jnp.cumsum(length_row).astype(jnp.int32)
    seq_starts = seq_ends - length_row

    def bounds(packed):
        inside = (packed[:, None] >= seq_starts[None, :]) & (packed[:, None] < seq_ends[None, :])
        return (
            jnp.sum(jnp.where(inside, seq_starts[None, :], 0), axis=1).astype(jnp.int32),
            jnp.sum(jnp.where(inside, seq_ends[None, :], 0), axis=1).astype(jnp.int32),
        )

    group_blocks = jnp.sum(
        jnp.where(slot_places[None, :] == slot_blocks[:, None], block_row[None, :], 0), axis=1
    )
    offsets = jnp.arange(BLK, dtype=jnp.int32)
    packed = (group_blocks[:, None] * BLK + offsets[None, :]).reshape(-1)
    cosine, sine = rotary_tables(packed - bounds(packed)[0])
    my_starts, my_ends = bounds(
        (my_blocks[:, None] * BLK + offsets[None, :]).reshape(-1)
    )
    key_first = bounds(my_blocks * BLK)[0] // CHUNK
    key_last = (my_blocks * BLK + BLK - 1) // CHUNK + 1
    query_first = my_blocks * BLK // CHUNK
    query_last = (bounds(my_blocks * BLK + BLK - 1)[1] + CHUNK - 1) // CHUNK

    def own_first(array, dim):
        left, right = jnp.split(array, 2, axis=dim)
        return jnp.where(first_tp, left, right), jnp.where(first_tp, right, left)

    inputs = inputs_low.astype(WIDE)
    centered = inputs - jnp.mean(inputs, axis=1, keepdims=True)
    inv_std = lax.rsqrt(jnp.mean(centered * centered, axis=1, keepdims=True) + 1e-05)
    normed = centered * inv_std
    norm_out = (normed * norm_vectors[0] + norm_vectors[1]).astype(LOW)
    hidden_here = up_bias.shape[0]
    feed_out, feed_dx, grad_up, grad_down, grad_ubias, norm_t, cotangent_t = feed_forward(
        norm_out, full_cotangent, up_full, down_full, up_bias.reshape(1, hidden_here)
    )

    projections = (
        *own_first(qkv_full, 1),
        *own_first(attn_full, 1),
        qkv_bias,
        *own_first(norm_vectors, 1),
    )
    made = ()
    for place, (near, far) in enumerate(zip(blocks_near, blocks_far)):
        after = (grad_ubias,) if place == len(order) - 3 else ()
        made = project_rows(
            place, len(order), near, far, projections, cosine, sine, made, after
        )
    queries, keys, values, d_attended = made

    def reduced_first(gradient):
        rows = gradient.shape[0] // fsdp_count
        return sum_scatter(
            gradient.reshape(fsdp_count, rows, gradient.shape[1]), "fsdp", 1, fsdp_index
        )

    def reduced_rest(part):
        piece = part.shape[0] // ctx_count
        part = part.reshape(OWNERS, low_count, piece, part.shape[1])
        part = sum_scatter(jnp.swapaxes(part, 0, 1), "ctx", 1, ctx_low)
        return sum_scatter(part, "ctx", low_count, ctx_high)

    first_up, first_down = reduced_first(grad_up), reduced_first(grad_down)

    def scatter_low(part):
        piece = part.shape[0] // ctx_count
        part = part.reshape(OWNERS, low_count, piece, part.shape[1])
        return sum_scatter(jnp.swapaxes(part, 0, 1), "ctx", 1, ctx_low)

    sum_feed = sum_scatter(
        jnp.concatenate([scatter_low(first_up), scatter_low(first_down)], axis=2),
        "ctx",
        low_count,
        ctx_high,
    )
    sum_up, sum_down = sum_feed[:, :hidden_here], sum_feed[:, hidden_here:]
    piece = sum_up.shape[0]
    grad_outbias = jnp.sum(cotangent.astype(WIDE), axis=0)

    def all_rows(*sums):
        joined = jnp.concatenate(sums, axis=1).astype(LOW)
        return lax.all_gather(joined, "ctx", axis=0, tiled=True).astype(WIDE)

    all_up, all_down = jnp.split(all_rows(sum_up, sum_down), 2, axis=1)
    fresh_up = 0.95 * up_moment + all_up
    fresh_down = 0.95 * down_moment + all_down.T

    def my_rows(array, dim):
        return lax.dynamic_slice_in_dim(array, ctx_index * piece, piece, dim)

    def as_rows(up, attn, qkv, down):
        return (
            my_rows(up, 0),
            my_rows(attn, 1).T,
            jnp.concatenate([my_rows(qkv, 0)[:, i] for i in range(3)], axis=1),
            my_rows(down, 1).T,
        )

    spans = (2 * hidden_here, 2 * half, 6 * half, 2 * hidden_here)
    old_moments = as_rows(up_moment, attn_moment, qkv_moment, down_moment)

    def to_owners(pieces):
        owners = tuple(pieces)
        low, high = pieces[owners[0]].astype(LOW), pieces[owners[1]].astype(LOW)

        def wanted(index):
            return index // low_count in owners

        rows = [jnp.where(ctx_high == owners[0], low, high)]
        for s in range(1, OWNERS):
            sent = jnp.where(ctx_high ^ s == owners[0], low, high)
            rows.append(partner_among(sent, ("ctx",), (s * low_count,), lambda i: wanted(i[0])))
        parts = [jnp.concatenate(rows, axis=0)]
        for s in range(1, low_count):
            parts.append(partner_among(parts[0], ("ctx",), (s,), lambda i: wanted(i[0])))
        for s in range(1, fsdp_count):
            parts += [
                partner_among(part, ("fsdp", "ctx"), (s, 0), lambda i: wanted(i[1]))
                for part in parts[:low_count]
            ]
        joined = [
            jnp.concatenate(parts[i : i + low_count], axis=0)
            for i in range(0, len(parts), low_count)
        ]
        others = [
            partner_among(part, ("ctx", "tp"), (0, 1), lambda i: wanted(i[0])) for part in joined
        ]
        return jnp.concatenate(joined, axis=0), jnp.concatenate(others, axis=0)

    wide_pair = to_owners(
        {0: 0.95 * old_moments[0] + sum_up, 3: 0.95 * old_moments[3] + sum_down}
    )

    attended, grad_q, stats = query_side(
        my_blocks,
        key_first,
        key_last,
        inverse,
        queries,
        keys,
        values,
        d_attended,
        cosine,
        sine,
        my_starts[:, None],
    )
    sum_early = reduced_rest(
        reduced_first(outer_pair(norm_t, grad_q, cotangent_t, attended))
    )
    all_stats = lax.all_gather(stats, "ctx", axis=0, tiled=True)
    grad_k, grad_v = key_side(
        my_blocks,
        query_first,
        query_last,
        inverse,
        natural,
        queries,
        keys,
        values,
        d_attended,
        cosine,
        sine,
        my_ends[:, None],
        all_stats,
        (first_up, first_down),
    )
    grad_late = outer_pair(norm_t, grad_k, norm_t, grad_v)
    late_rows = reduced_first(grad_late)
    sum_late = reduced_rest(late_rows)
    grad_q, grad_k, grad_v, grad_late = lax.optimization_barrier(
        (grad_q, grad_k, grad_v, grad_late)
    )
    grad_proj = (grad_q, grad_k, grad_v)
    grad_qbias = jnp.concatenate([jnp.sum(grad.astype(WIDE), axis=0) for grad in grad_proj])

    partial_out = dot_nn(attended, attn_full) + feed_out

    def sum_halves(array):
        return own_half(array) + partner(far_half(array).astype(LOW), "tp", 1).astype(WIDE)

    out_bias = own_half((norm_vectors[2] + norm_vectors[3])[None, :])
    mixed = (tokens.astype(WIDE) + sum_halves(partial_out) + out_bias).astype(LOW)

    grad_norm = sum_halves(
        sum(dot_nt(grad, qkv_full[i]) for i, grad in enumerate(grad_proj)) + feed_dx
    )
    my_normed = own_half(normed)
    scaled = grad_norm * own_half(norm_vectors[0:1])
    row_sums = jnp.stack([jnp.sum(scaled, axis=1), jnp.sum(scaled * my_normed, axis=1)])
    row_means = (row_sums + partner(row_sums, "tp", 1)) / width
    grad_tokens = cotangent.astype(WIDE) + inv_std * (
        scaled - row_means[0][:, None] - my_normed * row_means[1][:, None]
    )

    vector_parts = jnp.stack(
        [jnp.sum(grad_norm * my_normed, axis=0), jnp.sum(grad_norm, axis=0), grad_outbias]
    )
    small = jnp.concatenate([vector_parts.reshape(-1), grad_qbias, grad_ubias[0]])
    small = sum_everywhere(small, ("ctx",))
    small = sum_everywhere(lax.optimization_barrier((small, late_rows))[0], ("fsdp",))
    mine = small[: 3 * half].reshape(3, half)
    vectors = both_halves(mine, partner(mine, "tp", 1), 1)
    sum_vectors = jnp.concatenate([vectors, vectors[2:3]], axis=0)
    sum_qbias = small[3 * half : 6 * half].reshape(3, half)
    sum_ubias = small[6 * half :]

    sum_qkv = jnp.concatenate([sum_early[:, :half], sum_late], axis=1)
    sum_attn = sum_early[:, half:]
    gathered = all_rows(sum_qkv, sum_attn)
    fresh_qkv = 0.95 * qkv_moment + jnp.stack(jnp.split(gathered[:, : 3 * half], 3, axis=1), axis=1)
    fresh_attn = 0.95 * attn_moment + gathered[:, 3 * half :].T
    own_attn = jnp.pad(0.95 * old_moments[1] + sum_attn, ((0, 0), (0, 2 * half)))
    short_pair = to_owners({1: own_attn, 2: 0.95 * old_moments[2] + sum_qkv})
    rows_out = orthogonal_rows(
        spans, ctx_high.reshape(1), wide_pair, short_pair, OWNERS * piece
    ).reshape(OWNERS, piece, hidden_here)
    returned = jnp.stack(
        [rows_out[0]]
        + [partner(rows_out[s], "ctx", s * low_count) for s in range(1, OWNERS)]
    )
    orthogonal = [
        lax.dynamic_index_in_dim(returned, ctx_high ^ m, 0, keepdims=False).astype(WIDE)
        for m in range(OWNERS)
    ]
    full_hidden = hidden_here * 2
    olds = as_rows(w_up, w_attn, w_qkv, w_down)
    rates = (
        0.5 * math.sqrt(full_hidden / width),
        0.5 * math.sqrt(width / (width // HD)),
        0.5 * math.sqrt(3 * width / width),
        0.5 * math.sqrt(full_hidden / full_hidden),
    )
    new_up, new_attn, new_qkv, new_down = (
        old - rate * made[:, : old.shape[1]] for old, rate, made in zip(olds, rates, orthogonal)
    )

    vector_rate = 0.3 / math.sqrt(row_count * fsdp_count * ctx_count)
    mom_norm = 0.9 * norm_moment + sum_vectors
    mom_qbias = 0.9 * qbias_moment + sum_qbias
    mom_ubias = 0.9 * ubias_moment + sum_ubias
    return (
        mixed,
        grad_tokens,
        fresh_qkv,
        jnp.stack(jnp.split(new_qkv, 3, axis=1), axis=1),
        fresh_attn,
        new_attn.T,
        fresh_up,
        new_up,
        fresh_down,
        new_down.T,
        mom_norm,
        norm_vectors - vector_rate * mom_norm,
        mom_qbias,
        qkv_bias - vector_rate * mom_qbias,
        mom_ubias,
        up_bias - vector_rate * mom_ubias,
    )


def solution(mesh):
    return jax.shard_map(
        body,
        mesh=mesh,
        in_specs=(
            P(("fsdp", "ctx"), "tp"),
            P(("fsdp", "ctx"), "tp"),
            P("fsdp", None, "tp"),
            P("tp", "fsdp"),
            P("fsdp", "tp"),
            P("tp", "fsdp"),
            P(),
            P(None, "tp"),
            P("tp"),
            P("fsdp", None, "tp"),
            P("tp", "fsdp"),
            P("fsdp", "tp"),
            P("tp", "fsdp"),
            P(),
            P(None, "tp"),
            P("tp"),
            P("fsdp", None),
            P("fsdp", None),
        ),
        out_specs=(
            P(("fsdp", "ctx"), "tp"),
            P(("fsdp", "ctx"), "tp"),
            P("fsdp", None, "tp"),
            P(("fsdp", "ctx"), None, "tp"),
            P("tp", "fsdp"),
            P("tp", ("fsdp", "ctx")),
            P("fsdp", "tp"),
            P(("fsdp", "ctx"), "tp"),
            P("tp", "fsdp"),
            P("tp", ("fsdp", "ctx")),
            P(),
            P(),
            P(None, "tp"),
            P(None, "tp"),
            P("tp"),
            P("tp"),
        ),
        check_vma=False,
    )
```

```python
from functools import partial
import math

import jax
import jax.numpy as jnp
from jax import lax
from jax.experimental import pallas as pl
from jax.experimental.pallas import tpu as pltpu
from jax.sharding import PartitionSpec as P

HD = 64
ROT = 16
BLK = 128
NS_STEPS = 5
CHUNK = 512
MAX_LEN = 2048
SPAN = (MAX_LEN + BLK) // CHUNK + 2
OWNERS = 4
NS_COEF = (3.4445, -4.775, 2.0315)
NEG_BIG = -1e30
SCALE = HD**-0.5
LOW = jnp.bfloat16
WIDE = jnp.float32
NT = (((1,), (1,)), ((), ()))
VMEM_ASK = 56 * 1024 * 1024


def dot_nn(left, right):
    return jnp.dot(left, right, preferred_element_type=WIDE)


def dot_nt(left, right):
    return lax.dot_general(left, right, NT, preferred_element_type=WIDE)


def partner(value, axis, step):
    size = lax.axis_size(axis)
    return lax.ppermute(value, axis, [(i, i ^ step) for i in range(size)])


def partner_among(value, axes, strides, wanted):
    sizes = [lax.axis_size(axis) for axis in axes]
    pairs = []
    for flat in range(math.prod(sizes)):
        index, rest = [], flat
        for size in reversed(sizes):
            index.insert(0, rest % size)
            rest //= size
        if wanted(index):
            source = 0
            for size, i, stride in zip(sizes, index, strides):
                source = source * size + (i ^ stride)
            pairs.append((source, flat))
    return lax.ppermute(value, tuple(axes), pairs)


def sum_scatter(pieces, axis, stride, index):
    count = pieces.shape[0]
    total = lax.dynamic_index_in_dim(pieces, index, 0, keepdims=False).astype(WIDE)
    for step in range(1, count):
        piece = lax.dynamic_index_in_dim(pieces, index ^ step, 0, keepdims=False)
        total = total + partner(piece.astype(LOW), axis, step * stride).astype(WIDE)
    return total


def sum_everywhere(value, axes):
    for axis in axes:
        step = 1
        while step < lax.axis_size(axis):
            value = value + partner(value, axis, step)
            step *= 2
    return value


def turned(block, cosine, sine, lane):
    half = ROT // 2
    swapped = jnp.where(
        lane % HD < half, pltpu.roll(block, BLK - half, 1), pltpu.roll(block, half, 1)
    )
    return block * cosine + swapped * sine


def two_heads(block, lane):
    zero = jnp.zeros_like(block)
    return jnp.concatenate(
        [jnp.where(lane < HD, block, zero), jnp.where(lane < HD, zero, block)], axis=0
    )


def one_of_two(stacked, lane):
    return jnp.where(lane < HD, stacked[:BLK], stacked[BLK:])


def project_kernel(
    near, far, w_near, w_far, bias, vec_near, vec_far, cos_ref, sin_ref, *outs
):
    rows, half = outs[0].shape
    width = 2 * half
    own, other = near[...].astype(WIDE), far[...].astype(WIDE)
    mean = (
        jnp.sum(own, axis=1, keepdims=True) + jnp.sum(other, axis=1, keepdims=True)
    ) / width
    own, other = own - mean, other - mean
    var = (
        jnp.sum(own * own, axis=1, keepdims=True) + jnp.sum(other * other, axis=1, keepdims=True)
    ) / width
    inv_std = lax.rsqrt(var + 1e-5)
    own = (own * inv_std * vec_near[0:1] + vec_near[1:2]).astype(LOW)
    other = (other * inv_std * vec_far[0:1] + vec_far[1:2]).astype(LOW)
    lane = lax.broadcasted_iota(jnp.int32, (rows, BLK), 1)
    cosine, sine = cos_ref[...], sin_ref[...]
    for part, out in enumerate(outs):
        span = slice(part * half, (part + 1) * half)
        made = dot_nn(own, w_near[span]) + dot_nn(other, w_far[span]) + bias[part : part + 1]
        for pair in range(half // BLK):
            lanes = slice(pair * BLK, (pair + 1) * BLK)
            block = made[:, lanes]
            if part < 2:
                block = turned(block, cosine, sine, lane)
            out[:, lanes] = block.astype(LOW)


def project_rows(near, far, weights, cosine, sine):
    rows, half = near.shape

    def fixed(array):
        return pl.BlockSpec(array.shape, lambda i: (0,) * array.ndim)

    def chunk(width):
        return pl.BlockSpec((CHUNK, width), lambda i: (i, 0))

    return pl.pallas_call(
        project_kernel,
        grid=(rows // CHUNK,),
        in_specs=[chunk(half)] * 2 + [fixed(w) for w in weights] + [chunk(BLK)] * 2,
        out_specs=[chunk(half)] * 3,
        out_shape=[jax.ShapeDtypeStruct((rows, half), LOW)] * 3,
        compiler_params=pltpu.CompilerParams(vmem_limit_bytes=VMEM_ASK),
        cost_estimate=pl.CostEstimate(
            flops=44 * rows * half * half, bytes_accessed=14 * rows * half, transcendentals=0
        ),
        name="project_rows",
    )(near, far, *weights, cosine, sine)


def feed_kernel(
    xa_ref,
    xb_ref,
    ga_ref,
    gb_ref,
    up_a,
    up_b,
    down_a,
    down_b,
    bias_ref,
    out_ref,
    dx_ref,
    dup_ref,
    ddown_ref,
    dbias_ref,
    xt_ref,
    gt_ref,
):
    half = xa_ref.shape[1]
    first, second = slice(0, half), slice(half, 2 * half)

    @pl.when(pl.program_id(0) == 0)
    def _():
        xt_ref[first] = xa_ref[...].T
        xt_ref[second] = xb_ref[...].T
        gt_ref[first] = ga_ref[...].T
        gt_ref[second] = gb_ref[...].T
        out_ref[...] = jnp.zeros(out_ref.shape, WIDE)
        dx_ref[...] = jnp.zeros(dx_ref.shape, WIDE)

    hidden = dot_nn(xa_ref[...], up_a[...]) + dot_nn(xb_ref[...], up_b[...]) + bias_ref[...]
    grad = dot_nt(ga_ref[...], down_a[...]) + dot_nt(gb_ref[...], down_b[...])
    below = 0.5 + 0.5 * lax.erf(hidden * math.sqrt(0.5))
    density = jnp.exp(-0.5 * hidden * hidden) * (1.0 / math.sqrt(2.0 * math.pi))
    active = (hidden * below).astype(LOW)
    grad = (grad * (below + hidden * density)).astype(LOW)
    dbias_ref[...] = jnp.sum(grad.astype(WIDE), axis=0, keepdims=True)
    out_ref[:, first] += dot_nn(active, down_a[...])
    out_ref[:, second] += dot_nn(active, down_b[...])
    dx_ref[:, first] += dot_nt(grad, up_a[...])
    dx_ref[:, second] += dot_nt(grad, up_b[...])
    dup_ref[...] = dot_nn(xt_ref[...], grad).astype(LOW)
    ddown_ref[...] = dot_nn(gt_ref[...], active).astype(LOW)


def feed_forward(x_halves, g_halves, stacks, bias):
    rows, half = x_halves[0].shape
    width = 2 * half
    hidden = bias.shape[1]
    steps = hidden // half

    def whole(shape):
        return pl.BlockSpec(shape, lambda i: (0, 0))

    up = pl.BlockSpec((half, half), lambda i: (i, 0))
    down = pl.BlockSpec((half, half), lambda i: (i + steps, 0))
    column = pl.BlockSpec((width, half), lambda i: (0, i))
    line = pl.BlockSpec((1, half), lambda i: (0, i))
    return pl.pallas_call(
        feed_kernel,
        grid=(steps,),
        in_specs=[whole((rows, half))] * 4 + [up, up, down, down, line],
        out_specs=[
            whole((rows, width)),
            whole((rows, width)),
            column,
            column,
            line,
            whole((width, rows)),
            whole((width, rows)),
        ],
        out_shape=[
            jax.ShapeDtypeStruct((rows, width), WIDE),
            jax.ShapeDtypeStruct((rows, width), WIDE),
            jax.ShapeDtypeStruct((width, hidden), LOW),
            jax.ShapeDtypeStruct((width, hidden), LOW),
            jax.ShapeDtypeStruct((1, hidden), WIDE),
            jax.ShapeDtypeStruct((width, rows), LOW),
            jax.ShapeDtypeStruct((width, rows), LOW),
        ],
        compiler_params=pltpu.CompilerParams(vmem_limit_bytes=VMEM_ASK),
        cost_estimate=pl.CostEstimate(
            flops=26 * rows * width * hidden, bytes_accessed=12 * width * hidden, transcendentals=0
        ),
        name="feed_forward",
    )(*x_halves, *g_halves, *stacks, *stacks, bias)


def outer_kernel(left_a, right_a, left_b, right_b, out_ref):
    half = right_a.shape[1]
    out_ref[:, :half] = dot_nn(left_a[...], right_a[...]).astype(LOW)
    out_ref[:, half:] = dot_nn(left_b[...], right_b[...]).astype(LOW)


def outer_pair(left_a, right_a, left_b, right_b):
    rows, depth = left_a.shape
    half = right_a.shape[1]
    return pl.pallas_call(
        outer_kernel,
        in_specs=[vmem()] * 4,
        out_specs=vmem(),
        out_shape=jax.ShapeDtypeStruct((rows, 2 * half), LOW),
        compiler_params=pltpu.CompilerParams(vmem_limit_bytes=VMEM_ASK),
        cost_estimate=pl.CostEstimate(
            flops=8 * rows * depth * half, bytes_accessed=6 * rows * depth, transcendentals=0
        ),
        name="outer_pair",
    )(left_a, right_a, left_b, right_b)


def lane_tiles(array, combine):
    total = array[:, :BLK]
    for i in range(1, array.shape[1] // BLK):
        total = combine(total, array[:, i * BLK : (i + 1) * BLK])
    return total


def gathered_blocks(ref, inverse, chunk, lanes):
    count = CHUNK // BLK
    return jnp.concatenate(
        [
            ref[pl.ds(pl.multiple_of(inverse[chunk * count + i] * BLK, BLK), BLK), lanes]
            for i in range(count)
        ],
        axis=0,
    )


def query_kernel(
    blocks,
    first,
    last,
    natural,
    base,
    q_ref,
    k_ref,
    v_ref,
    d_ref,
    cos_ref,
    sin_ref,
    start_ref,
    att_out,
    dq_out,
    stat_out,
    s_scr,
    p_scr,
    q_scr,
    d_scr,
    m_scr,
    l_scr,
    e_scr,
    o_scr,
):
    pairs = q_ref.shape[1] // BLK
    own = att_out.shape[0] // BLK
    lane = lax.broadcasted_iota(jnp.int32, (BLK, BLK), 1)

    def lanes(pair):
        return slice(pair * BLK, (pair + 1) * BLK)

    @pl.loop(0, own)
    def _(j):
        row0 = pl.multiple_of(blocks[j] * BLK, BLK)
        out0 = pl.multiple_of(j * BLK, BLK)
        here = pl.multiple_of(base[0] + out0, BLK)
        lo = first[j]
        hi = last[j]
        for g in range(pairs):
            q_scr[g] = two_heads(q_ref[pl.ds(here, BLK), lanes(g)].astype(WIDE), lane).astype(
                LOW
            ) * LOW(SCALE)
            d_scr[g] = two_heads(d_ref[pl.ds(out0, BLK), lanes(g)].astype(WIDE), lane).astype(LOW)
        m_scr[...] = jnp.full(m_scr.shape, NEG_BIG, WIDE)
        l_scr[...] = jnp.zeros(l_scr.shape, WIDE)
        e_scr[...] = jnp.zeros(e_scr.shape, WIDE)
        o_scr[...] = jnp.zeros(o_scr.shape, WIDE)
        starts = start_ref[pl.ds(out0, BLK), :]
        places = row0 + lax.broadcasted_iota(jnp.int32, (BLK, 1), 0)
        starts = jnp.concatenate([starts, starts], axis=0)
        places = jnp.concatenate([places, places], axis=0)

        @pl.loop(lo, hi)
        def _(c):
            key0 = pl.multiple_of(c * CHUNK, CHUNK)
            key_place = key0 + lax.broadcasted_iota(jnp.int32, (2 * BLK, CHUNK), 1)
            allowed = (key_place >= starts) & (key_place <= places)
            for g in range(pairs):
                scores = dot_nt(q_scr[g], gathered_blocks(k_ref, natural, c, lanes(g)))
                scores = jnp.where(allowed, scores, NEG_BIG)
                s_scr[g, c - lo] = scores
                m_scr[g] = jnp.maximum(m_scr[g], lane_tiles(scores, jnp.maximum))

        for g in range(pairs):
            m_scr[g] = jnp.broadcast_to(
                jnp.max(m_scr[g], axis=1, keepdims=True), (2 * BLK, BLK)
            )

        @pl.loop(lo, hi)
        def _(c):
            for g in range(pairs):
                values = gathered_blocks(v_ref, natural, c, lanes(g))
                top = m_scr[g]
                weights = jnp.exp(s_scr[g, c - lo] - jnp.concatenate([top] * (CHUNK // BLK), 1))
                l_scr[g] += lane_tiles(weights, jnp.add)
                o_scr[g] += dot_nn(weights.astype(LOW), values)
                grad_prob = dot_nt(d_scr[g], values)
                e_scr[g] += lane_tiles(weights * grad_prob, jnp.add)
                s_scr[g, c - lo] = weights
                p_scr[g, c - lo] = grad_prob

        for g in range(pairs):
            total = jnp.sum(l_scr[g], axis=1, keepdims=True)
            share = 1.0 / total
            delta = jnp.sum(e_scr[g], axis=1, keepdims=True) * share
            att_out[pl.ds(out0, BLK), lanes(g)] = one_of_two(o_scr[g] * share, lane).astype(LOW)
            log_sum = m_scr[g] + jnp.log(total)
            stat_out[j, 2 * g : 2 * g + 1, :] = log_sum[:BLK].T[0:1]
            stat_out[j, 2 * g + 1 : 2 * g + 2, :] = log_sum[BLK:].T[0:1]
            wide = jnp.broadcast_to(delta, (2 * BLK, BLK))
            line = stat_out.shape[1] // 2 + 2 * g
            stat_out[j, line : line + 1, :] = wide[:BLK].T[0:1]
            stat_out[j, line + 1 : line + 2, :] = wide[BLK:].T[0:1]
            l_scr[g] = jnp.broadcast_to(share, (2 * BLK, BLK))
            e_scr[g] = wide
        o_scr[...] = jnp.zeros(o_scr.shape, WIDE)

        @pl.loop(lo, hi)
        def _(c):
            for g in range(pairs):
                wide = jnp.concatenate([e_scr[g]] * (CHUNK // BLK), 1)
                grad_score = s_scr[g, c - lo] * (p_scr[g, c - lo] - wide)
                o_scr[g] += dot_nn(
                    grad_score.astype(LOW), gathered_blocks(k_ref, natural, c, lanes(g))
                )

        cosine = cos_ref[pl.ds(here, BLK), :]
        sine = sin_ref[pl.ds(here, BLK), :]
        for g in range(pairs):
            grad = one_of_two(o_scr[g] * l_scr[g], lane) * SCALE
            dq_out[pl.ds(out0, BLK), lanes(g)] = turned(grad, cosine, -sine, lane).astype(LOW)


def smem():
    return pl.BlockSpec(memory_space=pltpu.SMEM)


def vmem():
    return pl.BlockSpec(memory_space=pltpu.VMEM)


def query_side(blocks, first, last, natural, base, queries, keys, values, grads, cosine, sine, starts):
    own = blocks.shape[0]
    width = queries.shape[1]
    pairs = width // BLK
    stat_rows = 16 * ((2 * pairs + 7) // 8)
    work = 2 * BLK * CHUNK
    return pl.pallas_call(
        query_kernel,
        in_specs=[smem()] * 5 + [vmem()] * 7,
        out_specs=[vmem()] * 3,
        out_shape=[
            jax.ShapeDtypeStruct((own * BLK, width), LOW),
            jax.ShapeDtypeStruct((own * BLK, width), LOW),
            jax.ShapeDtypeStruct((own, stat_rows, BLK), WIDE),
        ],
        scratch_shapes=[
            pltpu.VMEM((pairs, SPAN, 2 * BLK, CHUNK), WIDE),
            pltpu.VMEM((pairs, SPAN, 2 * BLK, CHUNK), WIDE),
            pltpu.VMEM((pairs, 2 * BLK, BLK), LOW),
            pltpu.VMEM((pairs, 2 * BLK, BLK), LOW),
            pltpu.VMEM((pairs, 2 * BLK, BLK), WIDE),
            pltpu.VMEM((pairs, 2 * BLK, BLK), WIDE),
            pltpu.VMEM((pairs, 2 * BLK, BLK), WIDE),
            pltpu.VMEM((pairs, 2 * BLK, BLK), WIDE),
        ],
        compiler_params=pltpu.CompilerParams(vmem_limit_bytes=VMEM_ASK),
        cost_estimate=pl.CostEstimate(
            flops=own * pairs * 12 * 4 * 2 * work * BLK,
            bytes_accessed=4 * keys.shape[0] * width * 2,
            transcendentals=own * pairs * 4 * work,
        ),
        name="query_side",
    )(blocks, first, last, natural, base, queries, keys, values, grads, cosine, sine, starts)


def key_kernel(
    blocks,
    first,
    last,
    natural,
    by_partner,
    stat_place,
    base,
    q_ref,
    k_ref,
    v_ref,
    d_ref,
    cos_ref,
    sin_ref,
    end_ref,
    stat_ref,
    *rest,
):
    dk_out, dv_out, k_scr, v_scr, dk_scr, dv_scr = rest[-6:]
    pairs = q_ref.shape[1] // BLK
    own = dk_out.shape[0] // BLK
    half_stat = stat_ref.shape[1] // 2
    lane = lax.broadcasted_iota(jnp.int32, (BLK, BLK), 1)

    def lanes(pair):
        return slice(pair * BLK, (pair + 1) * BLK)

    @pl.loop(0, own)
    def _(j):
        row0 = pl.multiple_of(blocks[j] * BLK, BLK)
        out0 = pl.multiple_of(j * BLK, BLK)
        here = pl.multiple_of(base[0] + out0, BLK)
        for g in range(pairs):
            k_scr[g] = two_heads(k_ref[pl.ds(here, BLK), lanes(g)].astype(WIDE), lane).astype(
                LOW
            ) * LOW(SCALE)
            v_scr[g] = two_heads(v_ref[pl.ds(here, BLK), lanes(g)].astype(WIDE), lane).astype(LOW)
        dk_scr[...] = jnp.zeros(dk_scr.shape, WIDE)
        dv_scr[...] = jnp.zeros(dv_scr.shape, WIDE)
        ends = end_ref[pl.ds(out0, BLK), :]
        places = row0 + lax.broadcasted_iota(jnp.int32, (BLK, 1), 0)

        @pl.loop(first[j], last[j])
        def _(c):
            query0 = pl.multiple_of(c * CHUNK, CHUNK)
            query_place = query0 + lax.broadcasted_iota(jnp.int32, (BLK, CHUNK), 1)
            allowed = (query_place >= places) & (query_place < ends)
            count = CHUNK // BLK
            slots = [stat_place[c * count + i] for i in range(count)]

            def stat(row):
                return jnp.concatenate([stat_ref[slot, row : row + 1, :] for slot in slots], 1)

            for g in range(pairs):
                queries = gathered_blocks(q_ref, natural, c, lanes(g))
                grads = gathered_blocks(d_ref, by_partner, c, lanes(g))
                scores = dot_nt(k_scr[g], queries)
                grad_prob = dot_nt(v_scr[g], grads)
                probs, grad_scores = [], []
                for h in range(2):
                    rows = slice(h * BLK, (h + 1) * BLK)
                    shifted = jnp.where(allowed, scores[rows] - stat(2 * g + h), NEG_BIG)
                    prob = jnp.exp(shifted)
                    probs.append(prob.astype(LOW))
                    grad_scores.append(
                        (prob * (grad_prob[rows] - stat(half_stat + 2 * g + h))).astype(LOW)
                    )
                dv_scr[g] += dot_nn(jnp.concatenate(probs, 0), grads)
                dk_scr[g] += dot_nn(jnp.concatenate(grad_scores, 0), queries)

        cosine = cos_ref[pl.ds(here, BLK), :]
        sine = sin_ref[pl.ds(here, BLK), :]
        for g in range(pairs):
            grad = one_of_two(dk_scr[g], lane) * SCALE
            dk_out[pl.ds(out0, BLK), lanes(g)] = turned(grad, cosine, -sine, lane).astype(LOW)
            dv_out[pl.ds(out0, BLK), lanes(g)] = one_of_two(dv_scr[g], lane).astype(LOW)


def key_side(
    blocks,
    first,
    last,
    natural,
    by_partner,
    stat_place,
    base,
    queries,
    keys,
    values,
    grads,
    cosine,
    sine,
    ends,
    stats,
    after,
):
    own = blocks.shape[0]
    width = queries.shape[1]
    pairs = width // BLK
    work = 2 * BLK * CHUNK
    return pl.pallas_call(
        key_kernel,
        in_specs=[smem()] * 7 + [vmem()] * 8 + [pl.BlockSpec(memory_space=pl.ANY)] * len(after),
        out_specs=[vmem()] * 2,
        out_shape=[jax.ShapeDtypeStruct((own * BLK, width), LOW)] * 2,
        scratch_shapes=[
            pltpu.VMEM((pairs, 2 * BLK, BLK), LOW),
            pltpu.VMEM((pairs, 2 * BLK, BLK), LOW),
            pltpu.VMEM((pairs, 2 * BLK, BLK), WIDE),
            pltpu.VMEM((pairs, 2 * BLK, BLK), WIDE),
        ],
        compiler_params=pltpu.CompilerParams(vmem_limit_bytes=VMEM_ASK),
        cost_estimate=pl.CostEstimate(
            flops=own * pairs * 12 * 4 * 2 * work * BLK,
            bytes_accessed=4 * keys.shape[0] * width * 2,
            transcendentals=own * pairs * 4 * work,
        ),
        name="key_side",
    )(
        blocks,
        first,
        last,
        natural,
        by_partner,
        stat_place,
        base,
        queries,
        keys,
        values,
        grads,
        cosine,
        sine,
        ends,
        stats,
        *after,
    )


TILE = 256


def symmetric_product(out_ref, left, right, depth):
    size = out_ref.shape[0]
    for i in range(0, size, TILE):
        out_ref[i : i + TILE, i:] = dot_nt(left[i : i + TILE, :depth], right[i:, :depth])
    for i in range(0, size, TILE):
        for j in range(i + TILE, size, TILE):
            out_ref[j : j + TILE, i : i + TILE] = out_ref[i : i + TILE, j : j + TILE].T


def ns_matrix(span, near, far, out_ref, wide_scr, low_scr, gram_scr, poly_scr):
    half = span // 2
    step = 768
    cuts = [slice(i, i + step) for i in range(0, span, step)]
    pltpu.sync_copy(near.at[:, pl.ds(0, half)], low_scr.at[:, pl.ds(0, half)])
    pltpu.sync_copy(far.at[:, pl.ds(0, half)], low_scr.at[:, pl.ds(half, half)])
    total = jnp.zeros((1, 1), WIDE)
    for cut in cuts:
        part = low_scr[:, cut].astype(WIDE)
        total = total + jnp.sum(part * part)
    factor = 1.0 / (jnp.sqrt(total) + 1e-7)
    for cut in cuts:
        part = low_scr[:, cut].astype(WIDE) * factor
        wide_scr[:, cut] = part
        low_scr[:, cut] = part.astype(LOW)

    def polynomial():
        symmetric_product(gram_scr, low_scr, low_scr, span)
        poly_scr[...] = gram_scr[...].astype(LOW)
        first = gram_scr[...] * NS_COEF[1]
        symmetric_product(gram_scr, poly_scr, poly_scr, poly_scr.shape[1])
        poly_scr[...] = (first + NS_COEF[2] * gram_scr[...]).astype(LOW)

    @pl.loop(0, NS_STEPS - 1)
    def _(_):
        polynomial()
        for cut in cuts:
            part = NS_COEF[0] * wide_scr[:, cut] + dot_nn(poly_scr[...], low_scr[:, cut])
            wide_scr[:, cut] = part
            low_scr[:, cut] = part.astype(LOW)

    polynomial()
    rows = out_ref.shape[0]
    if half < out_ref.shape[1]:
        out_ref[:, half:] = jnp.zeros((rows, out_ref.shape[1] - half), LOW)
    for i in range(0, half, 384):
        cut = slice(i, i + 384)
        out_ref[:, cut] = (
            NS_COEF[0] * wide_scr[:rows, cut] + dot_nn(poly_scr[:rows, :], low_scr[:, cut])
        ).astype(LOW)


def ns_kernel(spans, high, near_a, far_a, near_b, far_b, out_ref, *scratch):
    widest = max(spans)
    for span in sorted(set(spans)):
        wanted = jnp.bool_(False)
        for owner, own_span in enumerate(spans):
            if own_span == span:
                wanted = wanted | (high[0] == owner)

        @pl.when(wanted)
        def _():
            near, far = (near_a, far_a) if span == widest else (near_b, far_b)
            ns_matrix(span, near, far, out_ref, *scratch)


def orthogonal_rows(spans, high, wide_pair, short_pair, rows):
    size, half = wide_pair[0].shape
    kept = rows if rows % 16 == 0 else size
    out = pl.pallas_call(
        partial(ns_kernel, spans),
        in_specs=[smem()] + [pl.BlockSpec(memory_space=pl.ANY)] * 4,
        out_specs=vmem(),
        out_shape=jax.ShapeDtypeStruct((kept, half), LOW),
        scratch_shapes=[
            pltpu.VMEM((size, 2 * half), WIDE),
            pltpu.VMEM((size, 2 * half), LOW),
            pltpu.VMEM((size, size), WIDE),
            pltpu.VMEM((size, size), LOW),
        ],
        compiler_params=pltpu.CompilerParams(vmem_limit_bytes=VMEM_ASK),
        cost_estimate=pl.CostEstimate(
            flops=NS_STEPS * 10 * size * size * half,
            bytes_accessed=8 * size * half,
            transcendentals=0,
        ),
        name="orthogonal_rows",
    )(high, *wide_pair, *short_pair)
    return out[:rows]


def rotary_tables(places):
    half = ROT // 2
    exponent = jnp.arange(0, ROT, 2, dtype=WIDE) / ROT
    frequency = 1.0 / 10000.0**exponent
    angles = frequency[:, None] * places.astype(WIDE)[None, :]
    lane = jnp.arange(BLK) % HD
    picked = ((lane % half)[None, :] == jnp.arange(half)[:, None]) & (lane < ROT)[None, :]
    sign = jnp.where(lane < half, -1.0, 1.0)[None, :]
    spread = partial(
        jnp.einsum, "fn,fl->nl", precision=lax.Precision.HIGHEST, preferred_element_type=WIDE
    )
    cosine = spread(jnp.cos(angles), picked.astype(WIDE)) + (lane >= ROT)[None, :].astype(WIDE)
    return cosine, spread(jnp.sin(angles), picked * sign)


def body(
    tokens,
    cotangent,
    w_qkv,
    w_attn,
    w_up,
    w_down,
    norm_vectors,
    qkv_bias,
    up_bias,
    qkv_moment,
    attn_moment,
    up_moment,
    down_moment,
    norm_moment,
    qbias_moment,
    ubias_moment,
    seq_lengths,
    block_source,
):
    row_count, half = tokens.shape
    fsdp_count = lax.axis_size("fsdp")
    ctx_count = lax.axis_size("ctx")
    tp_index = lax.axis_index("tp")
    fsdp_index = lax.axis_index("fsdp")
    ctx_index = lax.axis_index("ctx")
    low_count = ctx_count // OWNERS
    ctx_low = ctx_index % low_count
    ctx_high = ctx_index // low_count
    width = 2 * half
    own_blocks = row_count // BLK
    pack = ctx_count * row_count
    first_tp = tp_index == 0
    block_row = block_source[0]
    length_row = seq_lengths[0]

    def both_halves(mine, other, dim):
        return jnp.concatenate(
            [jnp.where(first_tp, mine, other), jnp.where(first_tp, other, mine)], axis=dim
        )

    def own_half(array):
        return jnp.where(first_tp, array[:, :half], array[:, half:])

    def far_half(array):
        return jnp.where(first_tp, array[:, half:], array[:, :half])

    own_pair = jnp.concatenate([tokens, cotangent], axis=0)
    far_pair = partner(own_pair, "tp", 1)

    g_near = [
        jnp.concatenate(
            [cotangent] + [partner(cotangent, "ctx", s * low_count) for s in range(1, OWNERS)],
            axis=0,
        )
    ]
    x_near = lax.all_gather(tokens, "ctx", axis=0, tiled=True)
    for s in range(1, low_count):
        g_near.append(partner(g_near[0], "ctx", s))
    g_far = [partner(part, "tp", 1) for part in g_near]
    x_far = partner(x_near, "tp", 1)

    def stacked(up, down, qkv, attn):
        cuts = range(0, up.shape[1], half)
        return jnp.concatenate(
            [up[:, i : i + half] for i in cuts] + [down] + [qkv[:, i] for i in range(3)] + [attn],
            axis=0,
        )

    low_weights = [w.astype(LOW) for w in (w_up, w_down, w_qkv, w_attn)]
    if fsdp_count == 2:
        stack = stacked(*low_weights)
        other = partner(stack, "fsdp", 1)
        first_fsdp = fsdp_index == 0
        stacks = (jnp.where(first_fsdp, stack, other), jnp.where(first_fsdp, other, stack))
    else:
        whole_up, whole_down, whole_qkv, whole_attn = (
            lax.all_gather(w, "fsdp", axis=dim, tiled=True)
            for w, dim in zip(low_weights, (0, 1, 0, 1))
        )
        stacks = tuple(
            stacked(whole_up[cut], whole_down[:, cut], whole_qkv[cut], whole_attn[:, cut])
            for cut in (slice(0, half), slice(half, 2 * half))
        )
    hidden_here = up_bias.shape[0]
    late_stacks = tuple(part[2 * hidden_here :] for part in stacks)
    attn_halves = tuple(part[3 * half :] for part in late_stacks)

    def by_partners(ctx):
        differs = ctx ^ ctx_index
        return (differs % low_count) * OWNERS + differs // low_count

    slot_blocks = jnp.arange(block_row.shape[0], dtype=jnp.int32)
    slot_ctx, slot_rest = slot_blocks // own_blocks, slot_blocks % own_blocks
    holds = block_row[None, :] == slot_blocks[:, None]

    def located(places):
        return jnp.sum(jnp.where(holds, places[None, :], 0), axis=1).astype(jnp.int32)

    natural = located(slot_blocks)
    by_partner = located(by_partners(slot_ctx) * own_blocks + slot_rest)
    stat_place = located((slot_ctx ^ ctx_index) * own_blocks + slot_rest)
    row_base = (ctx_index * row_count).reshape(1)
    my_blocks = lax.dynamic_slice_in_dim(block_row, ctx_index * own_blocks, own_blocks)

    seq_ends = jnp.cumsum(length_row).astype(jnp.int32)
    seq_starts = seq_ends - length_row

    def bounds(packed):
        inside = (packed[:, None] >= seq_starts[None, :]) & (packed[:, None] < seq_ends[None, :])
        return (
            jnp.sum(jnp.where(inside, seq_starts[None, :], 0), axis=1).astype(jnp.int32),
            jnp.sum(jnp.where(inside, seq_ends[None, :], 0), axis=1).astype(jnp.int32),
        )

    offsets = jnp.arange(BLK, dtype=jnp.int32)
    packed = (block_row[:, None] * BLK + offsets[None, :]).reshape(-1)
    cosine, sine = rotary_tables(packed - bounds(packed)[0])
    my_starts, my_ends = bounds(
        (my_blocks[:, None] * BLK + offsets[None, :]).reshape(-1)
    )
    key_first = bounds(my_blocks * BLK)[0] // CHUNK
    key_last = (my_blocks * BLK + BLK - 1) // CHUNK + 1
    query_first = my_blocks * BLK // CHUNK
    query_last = (bounds(my_blocks * BLK + BLK - 1)[1] + CHUNK - 1) // CHUNK

    def own_first(array, dim):
        left, right = jnp.split(array, 2, axis=dim)
        return jnp.where(first_tp, left, right), jnp.where(first_tp, right, left)

    def two_halves(mine, other):
        return jnp.where(first_tp, mine, other), jnp.where(first_tp, other, mine)

    x_halves = [half_x.astype(WIDE) for half_x in two_halves(tokens, far_pair[:row_count])]
    row_mean = sum(jnp.sum(x, axis=1, keepdims=True) for x in x_halves) / width
    centered = [x - row_mean for x in x_halves]
    inv_std = lax.rsqrt(sum(jnp.sum(x * x, axis=1, keepdims=True) for x in centered) / width + 1e-5)
    norm_halves = [
        (x * inv_std * vec[0] + vec[1]).astype(LOW)
        for x, vec in zip(centered, jnp.split(norm_vectors, 2, axis=1))
    ]
    feed_out, feed_dx, grad_up, grad_down, grad_ubias, norm_t, cotangent_t = feed_forward(
        norm_halves,
        two_halves(cotangent, far_pair[row_count:]),
        stacks,
        up_bias.reshape(1, hidden_here),
    )

    queries, keys, values = project_rows(
        x_near,
        x_far,
        (*two_halves(*late_stacks), qkv_bias, *own_first(norm_vectors, 1)),
        cosine,
        sine,
    )
    attn_near, attn_far = two_halves(*attn_halves)
    d_attended = jnp.concatenate(
        [
            (dot_nt(near, attn_near) + dot_nt(far, attn_far)).astype(LOW)
            for near, far in zip(g_near, g_far)
        ],
        axis=0,
    )

    def reduced_first(gradient):
        rows = gradient.shape[0] // fsdp_count
        return sum_scatter(
            gradient.reshape(fsdp_count, rows, gradient.shape[1]), "fsdp", 1, fsdp_index
        )

    def reduced_rest(part):
        piece = part.shape[0] // ctx_count
        part = part.reshape(OWNERS, low_count, piece, part.shape[1])
        part = sum_scatter(jnp.swapaxes(part, 0, 1), "ctx", 1, ctx_low)
        return sum_scatter(part, "ctx", low_count, ctx_high)

    first_up, first_down = reduced_first(grad_up), reduced_first(grad_down)
    sum_feed = lax.psum_scatter(
        jnp.concatenate([first_up, first_down], axis=1).astype(LOW),
        "ctx",
        scatter_dimension=0,
        tiled=True,
    ).astype(WIDE)
    sum_up, sum_down = sum_feed[:, :hidden_here], sum_feed[:, hidden_here:]
    piece = sum_up.shape[0]
    grad_outbias = jnp.sum(cotangent.astype(WIDE), axis=0)

    def all_rows(*sums):
        joined = jnp.concatenate(sums, axis=1).astype(LOW)
        return lax.all_gather(joined, "ctx", axis=0, tiled=True).astype(WIDE)

    all_up, all_down = jnp.split(all_rows(sum_up, sum_down), 2, axis=1)
    fresh_up = 0.95 * up_moment + all_up
    fresh_down = 0.95 * down_moment + all_down.T

    def my_rows(array, dim):
        return lax.dynamic_slice_in_dim(array, ctx_index * piece, piece, dim)

    def as_rows(up, attn, qkv, down):
        return (
            my_rows(up, 0),
            my_rows(attn, 1).T,
            jnp.concatenate([my_rows(qkv, 0)[:, i] for i in range(3)], axis=1),
            my_rows(down, 1).T,
        )

    spans = (2 * hidden_here, 2 * half, 6 * half, 2 * hidden_here)
    old_moments = as_rows(up_moment, attn_moment, qkv_moment, down_moment)

    def to_owners(pieces):
        owners = tuple(pieces)
        low, high = pieces[owners[0]].astype(LOW), pieces[owners[1]].astype(LOW)

        def wanted(index):
            return index // low_count in owners

        rows = [jnp.where(ctx_high == owners[0], low, high)]
        for s in range(1, OWNERS):
            sent = jnp.where(ctx_high ^ s == owners[0], low, high)
            rows.append(partner_among(sent, ("ctx",), (s * low_count,), lambda i: wanted(i[0])))
        parts = [jnp.concatenate(rows, axis=0)]
        for s in range(1, low_count):
            parts.append(partner_among(parts[0], ("ctx",), (s,), lambda i: wanted(i[0])))
        for s in range(1, fsdp_count):
            parts += [
                partner_among(part, ("fsdp", "ctx"), (s, 0), lambda i: wanted(i[1]))
                for part in parts[:low_count]
            ]
        joined = [
            jnp.concatenate(parts[i : i + low_count], axis=0)
            for i in range(0, len(parts), low_count)
        ]
        others = [
            partner_among(part, ("ctx", "tp"), (0, 1), lambda i: wanted(i[0])) for part in joined
        ]
        return jnp.concatenate(joined, axis=0), jnp.concatenate(others, axis=0)

    wide_pair = to_owners(
        {0: 0.95 * old_moments[0] + sum_up, 3: 0.95 * old_moments[3] + sum_down}
    )

    attended, grad_q, stats = query_side(
        my_blocks,
        key_first,
        key_last,
        natural,
        row_base,
        queries,
        keys,
        values,
        d_attended,
        cosine,
        sine,
        my_starts[:, None],
    )
    early_rows = reduced_first(outer_pair(norm_t, grad_q, cotangent_t, attended))
    all_stats = stats
    step = 1
    while step < ctx_count:
        all_stats = jnp.concatenate([all_stats, partner(all_stats, "ctx", step)], axis=0)
        step *= 2
    grad_k, grad_v = key_side(
        my_blocks,
        query_first,
        query_last,
        natural,
        by_partner,
        stat_place,
        row_base,
        queries,
        keys,
        values,
        d_attended,
        cosine,
        sine,
        my_ends[:, None],
        all_stats,
        (first_up, first_down),
    )
    grad_late = outer_pair(norm_t, grad_k, norm_t, grad_v)
    late_rows = reduced_first(grad_late)
    joint_rows = jnp.concatenate([early_rows, late_rows], axis=1)
    sum_joint = reduced_rest(lax.optimization_barrier((joint_rows, sum_feed))[0])
    grad_q, grad_k, grad_v, grad_late = lax.optimization_barrier(
        (grad_q, grad_k, grad_v, grad_late)
    )
    grad_proj = (grad_q, grad_k, grad_v)
    grad_qbias = jnp.concatenate([jnp.sum(grad.astype(WIDE), axis=0) for grad in grad_proj])

    def joined(pair):
        return jnp.concatenate(pair, axis=1)

    partial_out = joined([dot_nn(attended, attn) for attn in attn_halves]) + feed_out

    def sum_halves(array):
        return own_half(array) + partner(far_half(array).astype(LOW), "tp", 1).astype(WIDE)

    out_bias = own_half((norm_vectors[2] + norm_vectors[3])[None, :])
    mixed = (tokens.astype(WIDE) + sum_halves(partial_out) + out_bias).astype(LOW)

    grad_norm = sum_halves(
        joined(
            [
                sum(
                    dot_nt(grad, stack[i * half : (i + 1) * half])
                    for i, grad in enumerate(grad_proj)
                )
                for stack in late_stacks
            ]
        )
        + feed_dx
    )
    my_normed = jnp.where(first_tp, *centered) * inv_std
    scaled = grad_norm * own_half(norm_vectors[0:1])
    row_sums = jnp.stack([jnp.sum(scaled, axis=1), jnp.sum(scaled * my_normed, axis=1)])
    row_means = (row_sums + partner(row_sums, "tp", 1)) / width
    grad_tokens = cotangent.astype(WIDE) + inv_std * (
        scaled - row_means[0][:, None] - my_normed * row_means[1][:, None]
    )

    vector_parts = jnp.stack(
        [jnp.sum(grad_norm * my_normed, axis=0), jnp.sum(grad_norm, axis=0), grad_outbias]
    )
    small = jnp.concatenate([vector_parts.reshape(-1), grad_qbias, grad_ubias[0]])
    small = sum_everywhere(small, ("ctx",))
    small = sum_everywhere(lax.optimization_barrier((small, late_rows))[0], ("fsdp",))
    mine = small[: 3 * half].reshape(3, half)
    vectors = both_halves(mine, partner(mine, "tp", 1), 1)
    sum_vectors = jnp.concatenate([vectors, vectors[2:3]], axis=0)
    sum_qbias = small[3 * half : 6 * half].reshape(3, half)
    sum_ubias = small[6 * half :]

    sum_qkv = jnp.concatenate([sum_joint[:, :half], sum_joint[:, 2 * half :]], axis=1)
    sum_attn = sum_joint[:, half : 2 * half]
    gathered = all_rows(sum_qkv, sum_attn)
    fresh_qkv = 0.95 * qkv_moment + jnp.stack(jnp.split(gathered[:, : 3 * half], 3, axis=1), axis=1)
    fresh_attn = 0.95 * attn_moment + gathered[:, 3 * half :].T
    own_attn = jnp.pad(0.95 * old_moments[1] + sum_attn, ((0, 0), (0, 2 * half)))
    short_pair = to_owners({1: own_attn, 2: 0.95 * old_moments[2] + sum_qkv})
    rows_out = orthogonal_rows(
        spans, ctx_high.reshape(1), wide_pair, short_pair, OWNERS * piece
    ).reshape(OWNERS, piece, hidden_here)
    returned = jnp.stack(
        [rows_out[0]]
        + [partner(rows_out[s], "ctx", s * low_count) for s in range(1, OWNERS)]
    )
    orthogonal = [
        lax.dynamic_index_in_dim(returned, ctx_high ^ m, 0, keepdims=False).astype(WIDE)
        for m in range(OWNERS)
    ]
    full_hidden = hidden_here * 2
    olds = as_rows(w_up, w_attn, w_qkv, w_down)
    rates = (
        0.5 * math.sqrt(full_hidden / width),
        0.5 * math.sqrt(width / (width // HD)),
        0.5 * math.sqrt(3 * width / width),
        0.5 * math.sqrt(full_hidden / full_hidden),
    )
    new_up, new_attn, new_qkv, new_down = (
        old - rate * made[:, : old.shape[1]] for old, rate, made in zip(olds, rates, orthogonal)
    )

    vector_rate = 0.3 / math.sqrt(row_count * fsdp_count * ctx_count)
    mom_norm = 0.9 * norm_moment + sum_vectors
    mom_qbias = 0.9 * qbias_moment + sum_qbias
    mom_ubias = 0.9 * ubias_moment + sum_ubias
    return (
        mixed,
        grad_tokens,
        fresh_qkv,
        jnp.stack(jnp.split(new_qkv, 3, axis=1), axis=1),
        fresh_attn,
        new_attn.T,
        fresh_up,
        new_up,
        fresh_down,
        new_down.T,
        mom_norm,
        norm_vectors - vector_rate * mom_norm,
        mom_qbias,
        qkv_bias - vector_rate * mom_qbias,
        mom_ubias,
        up_bias - vector_rate * mom_ubias,
    )


def solution(mesh):
    return jax.shard_map(
        body,
        mesh=mesh,
        in_specs=(
            P(("fsdp", "ctx"), "tp"),
            P(("fsdp", "ctx"), "tp"),
            P("fsdp", None, "tp"),
            P("tp", "fsdp"),
            P("fsdp", "tp"),
            P("tp", "fsdp"),
            P(),
            P(None, "tp"),
            P("tp"),
            P("fsdp", None, "tp"),
            P("tp", "fsdp"),
            P("fsdp", "tp"),
            P("tp", "fsdp"),
            P(),
            P(None, "tp"),
            P("tp"),
            P("fsdp", None),
            P("fsdp", None),
        ),
        out_specs=(
            P(("fsdp", "ctx"), "tp"),
            P(("fsdp", "ctx"), "tp"),
            P("fsdp", None, "tp"),
            P(("fsdp", "ctx"), None, "tp"),
            P("tp", "fsdp"),
            P("tp", ("fsdp", "ctx")),
            P("fsdp", "tp"),
            P(("fsdp", "ctx"), "tp"),
            P("tp", "fsdp"),
            P("tp", ("fsdp", "ctx")),
            P(),
            P(),
            P(None, "tp"),
            P(None, "tp"),
            P("tp"),
            P("tp"),
        ),
        check_vma=False,
    )
```

```python
from functools import partial
import math

import jax
import jax.numpy as jnp
from jax import lax
from jax.experimental import pallas as pl
from jax.experimental.pallas import tpu as pltpu
from jax.sharding import PartitionSpec as P

HD = 64
ROT = 16
BLK = 128
NS_STEPS = 5
CHUNK = 512
MAX_LEN = 2048
SPAN = (MAX_LEN + BLK) // CHUNK + 2
OWNERS = 4
NS_COEF = (3.4445, -4.775, 2.0315)
NEG_BIG = -1e30
SCALE = HD**-0.5
LOW = jnp.bfloat16
WIDE = jnp.float32
NT = (((1,), (1,)), ((), ()))
VMEM_ASK = 56 * 1024 * 1024


def dot_nn(left, right):
    return jnp.dot(left, right, preferred_element_type=WIDE)


def dot_nt(left, right):
    return lax.dot_general(left, right, NT, preferred_element_type=WIDE)


def partner(value, axis, step):
    size = lax.axis_size(axis)
    return lax.ppermute(value, axis, [(i, i ^ step) for i in range(size)])


def sum_scatter(pieces, axis, stride, index, *earlier):
    count = pieces.shape[0]
    total = lax.dynamic_index_in_dim(pieces, index, 0, keepdims=False)
    total = after(total, *earlier).astype(WIDE)
    for step in range(1, count):
        piece = lax.dynamic_index_in_dim(pieces, index ^ step, 0, keepdims=False)
        total = total + partner(piece.astype(LOW), axis, step * stride).astype(WIDE)
    return total


def after(value, *earlier):
    return lax.optimization_barrier((value, *earlier))[0]


def sum_everywhere(value, axes):
    for axis in axes:
        step = 1
        while step < lax.axis_size(axis):
            value = value + partner(value, axis, step)
            step *= 2
    return value


def turned(block, cosine, sine, lane):
    half = ROT // 2
    swapped = jnp.where(
        lane % HD < half, pltpu.roll(block, BLK - half, 1), pltpu.roll(block, half, 1)
    )
    return block * cosine + swapped * sine


def two_heads(block, lane):
    zero = jnp.zeros_like(block)
    return jnp.concatenate(
        [jnp.where(lane < HD, block, zero), jnp.where(lane < HD, zero, block)], axis=0
    )


def one_of_two(stacked, lane):
    return jnp.where(lane < HD, stacked[:BLK], stacked[BLK:])


def project_kernel(
    near, far, w_near, w_far, bias, vec_near, vec_far, cos_ref, sin_ref, *outs
):
    rows, half = outs[0].shape
    width = 2 * half
    own, other = near[...].astype(WIDE), far[...].astype(WIDE)
    mean = (
        jnp.sum(own, axis=1, keepdims=True) + jnp.sum(other, axis=1, keepdims=True)
    ) / width
    own, other = own - mean, other - mean
    var = (
        jnp.sum(own * own, axis=1, keepdims=True) + jnp.sum(other * other, axis=1, keepdims=True)
    ) / width
    inv_std = lax.rsqrt(var + 1e-5)
    own = (own * inv_std * vec_near[0:1] + vec_near[1:2]).astype(LOW)
    other = (other * inv_std * vec_far[0:1] + vec_far[1:2]).astype(LOW)
    lane = lax.broadcasted_iota(jnp.int32, (rows, BLK), 1)
    cosine, sine = cos_ref[...], sin_ref[...]
    for part, out in enumerate(outs):
        span = slice(part * half, (part + 1) * half)
        made = dot_nn(own, w_near[span]) + dot_nn(other, w_far[span]) + bias[part : part + 1]
        for pair in range(half // BLK):
            lanes = slice(pair * BLK, (pair + 1) * BLK)
            block = made[:, lanes]
            if part < 2:
                block = turned(block, cosine, sine, lane)
            out[:, lanes] = block.astype(LOW)


def project_rows(near, far, weights, cosine, sine):
    rows, half = near.shape

    def fixed(array):
        return pl.BlockSpec(array.shape, lambda i: (0,) * array.ndim)

    def chunk(width):
        return pl.BlockSpec((CHUNK, width), lambda i: (i, 0))

    return pl.pallas_call(
        project_kernel,
        grid=(rows // CHUNK,),
        in_specs=[chunk(half)] * 2 + [fixed(w) for w in weights] + [chunk(BLK)] * 2,
        out_specs=[chunk(half)] * 3,
        out_shape=[jax.ShapeDtypeStruct((rows, half), LOW)] * 3,
        compiler_params=pltpu.CompilerParams(vmem_limit_bytes=VMEM_ASK),
        cost_estimate=pl.CostEstimate(
            flops=44 * rows * half * half, bytes_accessed=14 * rows * half, transcendentals=0
        ),
        name="project_rows",
    )(near, far, *weights, cosine, sine)


def feed_kernel(
    xa_ref,
    xb_ref,
    ga_ref,
    gb_ref,
    up_a,
    up_b,
    down_a,
    down_b,
    bias_ref,
    *refs,
):
    out_ref, dx_ref, dup_ref, ddown_ref, dbias_ref, xt_ref, gt_ref = refs[-7:]
    half = xa_ref.shape[1]
    first, second = slice(0, half), slice(half, 2 * half)

    @pl.when(pl.program_id(0) == 0)
    def _():
        xt_ref[first] = xa_ref[...].T
        xt_ref[second] = xb_ref[...].T
        gt_ref[first] = ga_ref[...].T
        gt_ref[second] = gb_ref[...].T
        out_ref[...] = jnp.zeros(out_ref.shape, WIDE)
        dx_ref[...] = jnp.zeros(dx_ref.shape, WIDE)

    hidden = dot_nn(xa_ref[...], up_a[...]) + dot_nn(xb_ref[...], up_b[...]) + bias_ref[...]
    grad = dot_nt(ga_ref[...], down_a[...]) + dot_nt(gb_ref[...], down_b[...])
    below = 0.5 + 0.5 * lax.erf(hidden * math.sqrt(0.5))
    density = jnp.exp(-0.5 * hidden * hidden) * (1.0 / math.sqrt(2.0 * math.pi))
    active = (hidden * below).astype(LOW)
    grad = (grad * (below + hidden * density)).astype(LOW)
    dbias_ref[...] = jnp.sum(grad.astype(WIDE), axis=0, keepdims=True)
    out_ref[:, first] += dot_nn(active, down_a[...])
    out_ref[:, second] += dot_nn(active, down_b[...])
    dx_ref[:, first] += dot_nt(grad, up_a[...])
    dx_ref[:, second] += dot_nt(grad, up_b[...])
    dup_ref[...] = dot_nn(xt_ref[...], grad).astype(LOW)
    ddown_ref[...] = dot_nn(gt_ref[...], active).astype(LOW)


def feed_forward(x_halves, g_halves, stacks, bias, earlier):
    rows, half = x_halves[0].shape
    width = 2 * half
    hidden = bias.shape[1]
    steps = hidden // half

    def whole(shape):
        return pl.BlockSpec(shape, lambda i: (0, 0))

    up = pl.BlockSpec((half, half), lambda i: (i, 0))
    down = pl.BlockSpec((half, half), lambda i: (i + steps, 0))
    column = pl.BlockSpec((width, half), lambda i: (0, i))
    line = pl.BlockSpec((1, half), lambda i: (0, i))
    return pl.pallas_call(
        feed_kernel,
        grid=(steps,),
        in_specs=[whole((rows, half))] * 4
        + [up, up, down, down, line]
        + [pl.BlockSpec(memory_space=pl.ANY)] * len(earlier),
        out_specs=[
            whole((rows, width)),
            whole((rows, width)),
            column,
            column,
            line,
            whole((width, rows)),
            whole((width, rows)),
        ],
        out_shape=[
            jax.ShapeDtypeStruct((rows, width), WIDE),
            jax.ShapeDtypeStruct((rows, width), WIDE),
            jax.ShapeDtypeStruct((width, hidden), LOW),
            jax.ShapeDtypeStruct((width, hidden), LOW),
            jax.ShapeDtypeStruct((1, hidden), WIDE),
            jax.ShapeDtypeStruct((width, rows), LOW),
            jax.ShapeDtypeStruct((width, rows), LOW),
        ],
        compiler_params=pltpu.CompilerParams(vmem_limit_bytes=VMEM_ASK),
        cost_estimate=pl.CostEstimate(
            flops=26 * rows * width * hidden, bytes_accessed=12 * width * hidden, transcendentals=0
        ),
        name="feed_forward",
    )(*x_halves, *g_halves, *stacks, *stacks, bias, *earlier)


def outer_kernel(left_a, right_a, left_b, right_b, out_ref):
    half = right_a.shape[1]
    out_ref[:, :half] = dot_nn(left_a[...], right_a[...]).astype(LOW)
    out_ref[:, half:] = dot_nn(left_b[...], right_b[...]).astype(LOW)


def outer_pair(left_a, right_a, left_b, right_b):
    rows, depth = left_a.shape
    half = right_a.shape[1]
    return pl.pallas_call(
        outer_kernel,
        in_specs=[vmem()] * 4,
        out_specs=vmem(),
        out_shape=jax.ShapeDtypeStruct((rows, 2 * half), LOW),
        compiler_params=pltpu.CompilerParams(vmem_limit_bytes=VMEM_ASK),
        cost_estimate=pl.CostEstimate(
            flops=8 * rows * depth * half, bytes_accessed=6 * rows * depth, transcendentals=0
        ),
        name="outer_pair",
    )(left_a, right_a, left_b, right_b)


def lane_tiles(array, combine):
    total = array[:, :BLK]
    for i in range(1, array.shape[1] // BLK):
        total = combine(total, array[:, i * BLK : (i + 1) * BLK])
    return total


def gathered_blocks(ref, inverse, chunk, lanes):
    count = CHUNK // BLK
    return jnp.concatenate(
        [
            ref[pl.ds(pl.multiple_of(inverse[chunk * count + i] * BLK, BLK), BLK), lanes]
            for i in range(count)
        ],
        axis=0,
    )


def query_kernel(
    blocks,
    first,
    last,
    natural,
    base,
    q_ref,
    k_ref,
    v_ref,
    d_ref,
    cos_ref,
    sin_ref,
    start_ref,
    att_out,
    dq_out,
    stat_out,
    s_scr,
    p_scr,
    q_scr,
    d_scr,
    m_scr,
    l_scr,
    e_scr,
    o_scr,
):
    pairs = q_ref.shape[1] // BLK
    own = att_out.shape[0] // BLK
    lane = lax.broadcasted_iota(jnp.int32, (BLK, BLK), 1)

    def lanes(pair):
        return slice(pair * BLK, (pair + 1) * BLK)

    @pl.loop(0, own)
    def _(j):
        row0 = pl.multiple_of(blocks[j] * BLK, BLK)
        out0 = pl.multiple_of(j * BLK, BLK)
        here = pl.multiple_of(base[0] + out0, BLK)
        lo = first[j]
        hi = last[j]
        for g in range(pairs):
            q_scr[g] = two_heads(q_ref[pl.ds(here, BLK), lanes(g)].astype(WIDE), lane).astype(
                LOW
            ) * LOW(SCALE)
            d_scr[g] = two_heads(d_ref[pl.ds(out0, BLK), lanes(g)].astype(WIDE), lane).astype(LOW)
        m_scr[...] = jnp.full(m_scr.shape, NEG_BIG, WIDE)
        l_scr[...] = jnp.zeros(l_scr.shape, WIDE)
        e_scr[...] = jnp.zeros(e_scr.shape, WIDE)
        o_scr[...] = jnp.zeros(o_scr.shape, WIDE)
        starts = start_ref[pl.ds(out0, BLK), :]
        places = row0 + lax.broadcasted_iota(jnp.int32, (BLK, 1), 0)
        starts = jnp.concatenate([starts, starts], axis=0)
        places = jnp.concatenate([places, places], axis=0)

        @pl.loop(lo, hi)
        def _(c):
            key0 = pl.multiple_of(c * CHUNK, CHUNK)
            key_place = key0 + lax.broadcasted_iota(jnp.int32, (2 * BLK, CHUNK), 1)
            allowed = (key_place >= starts) & (key_place <= places)
            for g in range(pairs):
                scores = dot_nt(q_scr[g], gathered_blocks(k_ref, natural, c, lanes(g)))
                scores = jnp.where(allowed, scores, NEG_BIG)
                s_scr[g, c - lo] = scores
                m_scr[g] = jnp.maximum(m_scr[g], lane_tiles(scores, jnp.maximum))

        for g in range(pairs):
            m_scr[g] = jnp.broadcast_to(
                jnp.max(m_scr[g], axis=1, keepdims=True), (2 * BLK, BLK)
            )

        @pl.loop(lo, hi)
        def _(c):
            for g in range(pairs):
                values = gathered_blocks(v_ref, natural, c, lanes(g))
                top = m_scr[g]
                weights = jnp.exp(s_scr[g, c - lo] - jnp.concatenate([top] * (CHUNK // BLK), 1))
                l_scr[g] += lane_tiles(weights, jnp.add)
                o_scr[g] += dot_nn(weights.astype(LOW), values)
                grad_prob = dot_nt(d_scr[g], values)
                e_scr[g] += lane_tiles(weights * grad_prob, jnp.add)
                s_scr[g, c - lo] = weights
                p_scr[g, c - lo] = grad_prob

        for g in range(pairs):
            total = jnp.sum(l_scr[g], axis=1, keepdims=True)
            share = 1.0 / total
            delta = jnp.sum(e_scr[g], axis=1, keepdims=True) * share
            att_out[pl.ds(out0, BLK), lanes(g)] = one_of_two(o_scr[g] * share, lane).astype(LOW)
            log_sum = m_scr[g] + jnp.log(total)
            stat_out[j, 2 * g : 2 * g + 1, :] = log_sum[:BLK].T[0:1]
            stat_out[j, 2 * g + 1 : 2 * g + 2, :] = log_sum[BLK:].T[0:1]
            wide = jnp.broadcast_to(delta, (2 * BLK, BLK))
            line = stat_out.shape[1] // 2 + 2 * g
            stat_out[j, line : line + 1, :] = wide[:BLK].T[0:1]
            stat_out[j, line + 1 : line + 2, :] = wide[BLK:].T[0:1]
            l_scr[g] = jnp.broadcast_to(share, (2 * BLK, BLK))
            e_scr[g] = wide
        o_scr[...] = jnp.zeros(o_scr.shape, WIDE)

        @pl.loop(lo, hi)
        def _(c):
            for g in range(pairs):
                wide = jnp.concatenate([e_scr[g]] * (CHUNK // BLK), 1)
                grad_score = s_scr[g, c - lo] * (p_scr[g, c - lo] - wide)
                o_scr[g] += dot_nn(
                    grad_score.astype(LOW), gathered_blocks(k_ref, natural, c, lanes(g))
                )

        cosine = cos_ref[pl.ds(here, BLK), :]
        sine = sin_ref[pl.ds(here, BLK), :]
        for g in range(pairs):
            grad = one_of_two(o_scr[g] * l_scr[g], lane) * SCALE
            dq_out[pl.ds(out0, BLK), lanes(g)] = turned(grad, cosine, -sine, lane).astype(LOW)


def smem():
    return pl.BlockSpec(memory_space=pltpu.SMEM)


def vmem():
    return pl.BlockSpec(memory_space=pltpu.VMEM)


def query_side(blocks, first, last, natural, base, queries, keys, values, grads, cosine, sine, starts):
    own = blocks.shape[0]
    width = queries.shape[1]
    pairs = width // BLK
    stat_rows = 16 * ((2 * pairs + 7) // 8)
    work = 2 * BLK * CHUNK
    return pl.pallas_call(
        query_kernel,
        in_specs=[smem()] * 5 + [vmem()] * 7,
        out_specs=[vmem()] * 3,
        out_shape=[
            jax.ShapeDtypeStruct((own * BLK, width), LOW),
            jax.ShapeDtypeStruct((own * BLK, width), LOW),
            jax.ShapeDtypeStruct((own, stat_rows, BLK), WIDE),
        ],
        scratch_shapes=[
            pltpu.VMEM((pairs, SPAN, 2 * BLK, CHUNK), WIDE),
            pltpu.VMEM((pairs, SPAN, 2 * BLK, CHUNK), WIDE),
            pltpu.VMEM((pairs, 2 * BLK, BLK), LOW),
            pltpu.VMEM((pairs, 2 * BLK, BLK), LOW),
            pltpu.VMEM((pairs, 2 * BLK, BLK), WIDE),
            pltpu.VMEM((pairs, 2 * BLK, BLK), WIDE),
            pltpu.VMEM((pairs, 2 * BLK, BLK), WIDE),
            pltpu.VMEM((pairs, 2 * BLK, BLK), WIDE),
        ],
        compiler_params=pltpu.CompilerParams(vmem_limit_bytes=VMEM_ASK),
        cost_estimate=pl.CostEstimate(
            flops=own * pairs * 12 * 4 * 2 * work * BLK,
            bytes_accessed=4 * keys.shape[0] * width * 2,
            transcendentals=own * pairs * 4 * work,
        ),
        name="query_side",
    )(blocks, first, last, natural, base, queries, keys, values, grads, cosine, sine, starts)


def key_kernel(
    blocks,
    first,
    last,
    natural,
    by_partner,
    stat_place,
    base,
    q_ref,
    k_ref,
    v_ref,
    d_ref,
    cos_ref,
    sin_ref,
    end_ref,
    stat_ref,
    *rest,
):
    dk_out, dv_out, k_scr, v_scr, dk_scr, dv_scr = rest[-6:]
    pairs = q_ref.shape[1] // BLK
    own = dk_out.shape[0] // BLK
    half_stat = stat_ref.shape[1] // 2
    lane = lax.broadcasted_iota(jnp.int32, (BLK, BLK), 1)

    def lanes(pair):
        return slice(pair * BLK, (pair + 1) * BLK)

    @pl.loop(0, own)
    def _(j):
        row0 = pl.multiple_of(blocks[j] * BLK, BLK)
        out0 = pl.multiple_of(j * BLK, BLK)
        here = pl.multiple_of(base[0] + out0, BLK)
        for g in range(pairs):
            k_scr[g] = two_heads(k_ref[pl.ds(here, BLK), lanes(g)].astype(WIDE), lane).astype(
                LOW
            ) * LOW(SCALE)
            v_scr[g] = two_heads(v_ref[pl.ds(here, BLK), lanes(g)].astype(WIDE), lane).astype(LOW)
        dk_scr[...] = jnp.zeros(dk_scr.shape, WIDE)
        dv_scr[...] = jnp.zeros(dv_scr.shape, WIDE)
        ends = end_ref[pl.ds(out0, BLK), :]
        places = row0 + lax.broadcasted_iota(jnp.int32, (BLK, 1), 0)

        @pl.loop(first[j], last[j])
        def _(c):
            query0 = pl.multiple_of(c * CHUNK, CHUNK)
            query_place = query0 + lax.broadcasted_iota(jnp.int32, (BLK, CHUNK), 1)
            allowed = (query_place >= places) & (query_place < ends)
            count = CHUNK // BLK
            slots = [stat_place[c * count + i] for i in range(count)]

            def stat(row):
                return jnp.concatenate([stat_ref[slot, row : row + 1, :] for slot in slots], 1)

            for g in range(pairs):
                queries = gathered_blocks(q_ref, natural, c, lanes(g))
                grads = gathered_blocks(d_ref, by_partner, c, lanes(g))
                scores = dot_nt(k_scr[g], queries)
                grad_prob = dot_nt(v_scr[g], grads)
                probs, grad_scores = [], []
                for h in range(2):
                    rows = slice(h * BLK, (h + 1) * BLK)
                    shifted = jnp.where(allowed, scores[rows] - stat(2 * g + h), NEG_BIG)
                    prob = jnp.exp(shifted)
                    probs.append(prob.astype(LOW))
                    grad_scores.append(
                        (prob * (grad_prob[rows] - stat(half_stat + 2 * g + h))).astype(LOW)
                    )
                dv_scr[g] += dot_nn(jnp.concatenate(probs, 0), grads)
                dk_scr[g] += dot_nn(jnp.concatenate(grad_scores, 0), queries)

        cosine = cos_ref[pl.ds(here, BLK), :]
        sine = sin_ref[pl.ds(here, BLK), :]
        for g in range(pairs):
            grad = one_of_two(dk_scr[g], lane) * SCALE
            dk_out[pl.ds(out0, BLK), lanes(g)] = turned(grad, cosine, -sine, lane).astype(LOW)
            dv_out[pl.ds(out0, BLK), lanes(g)] = one_of_two(dv_scr[g], lane).astype(LOW)


def key_side(
    blocks,
    first,
    last,
    natural,
    by_partner,
    stat_place,
    base,
    queries,
    keys,
    values,
    grads,
    cosine,
    sine,
    ends,
    stats,
    after,
):
    own = blocks.shape[0]
    width = queries.shape[1]
    pairs = width // BLK
    work = 2 * BLK * CHUNK
    return pl.pallas_call(
        key_kernel,
        in_specs=[smem()] * 7 + [vmem()] * 8 + [pl.BlockSpec(memory_space=pl.ANY)] * len(after),
        out_specs=[vmem()] * 2,
        out_shape=[jax.ShapeDtypeStruct((own * BLK, width), LOW)] * 2,
        scratch_shapes=[
            pltpu.VMEM((pairs, 2 * BLK, BLK), LOW),
            pltpu.VMEM((pairs, 2 * BLK, BLK), LOW),
            pltpu.VMEM((pairs, 2 * BLK, BLK), WIDE),
            pltpu.VMEM((pairs, 2 * BLK, BLK), WIDE),
        ],
        compiler_params=pltpu.CompilerParams(vmem_limit_bytes=VMEM_ASK),
        cost_estimate=pl.CostEstimate(
            flops=own * pairs * 12 * 4 * 2 * work * BLK,
            bytes_accessed=4 * keys.shape[0] * width * 2,
            transcendentals=own * pairs * 4 * work,
        ),
        name="key_side",
    )(
        blocks,
        first,
        last,
        natural,
        by_partner,
        stat_place,
        base,
        queries,
        keys,
        values,
        grads,
        cosine,
        sine,
        ends,
        stats,
        *after,
    )


TILE = 256


def symmetric_product(out_ref, left, right):
    size = out_ref.shape[0]
    for i in range(0, size, TILE):
        out_ref[i : i + TILE, i:] = dot_nt(left[i : i + TILE, :], right[i:, :])
    for i in range(0, size, TILE):
        for j in range(i + TILE, size, TILE):
            out_ref[j : j + TILE, i : i + TILE] = out_ref[i : i + TILE, j : j + TILE].T


def ns_kernel(near_ref, far_ref, *refs):
    out_ref, wide_scr, low_scr, gram_scr, poly_scr = refs[-5:]
    size, half = near_ref.shape
    span = 2 * half
    step = 768
    cuts = [slice(i, i + step) for i in range(0, span, step)]
    total = jnp.zeros((1, 1), WIDE)
    for source, base in ((near_ref, 0), (far_ref, half)):
        for i in range(0, half, step):
            part = source[:, i : i + step].astype(WIDE)
            wide_scr[:, base + i : base + i + step] = part
            total = total + jnp.sum(part * part)
    factor = 1.0 / (jnp.sqrt(total) + 1e-7)
    for cut in cuts:
        part = wide_scr[:, cut] * factor
        wide_scr[:, cut] = part
        low_scr[:, cut] = part.astype(LOW)

    def polynomial():
        symmetric_product(gram_scr, low_scr, low_scr)
        poly_scr[...] = gram_scr[...].astype(LOW)
        first = gram_scr[...] * NS_COEF[1]
        symmetric_product(gram_scr, poly_scr, poly_scr)
        poly_scr[...] = (first + NS_COEF[2] * gram_scr[...]).astype(LOW)

    @pl.loop(0, NS_STEPS - 1)
    def _(_):
        polynomial()
        for cut in cuts:
            part = NS_COEF[0] * wide_scr[:, cut] + dot_nn(poly_scr[...], low_scr[:, cut])
            wide_scr[:, cut] = part
            low_scr[:, cut] = part.astype(LOW)

    polynomial()
    rows = out_ref.shape[0]
    for i in range(0, half, step):
        cut = slice(i, i + step)
        out_ref[:, cut] = (
            NS_COEF[0] * wide_scr[:rows, cut] + dot_nn(poly_scr[:rows, :], low_scr[:, cut])
        ).astype(LOW)


def orthogonal_rows(near, far, rows, earlier):
    size, half = near.shape
    kept = rows if rows % 16 == 0 else size
    out = pl.pallas_call(
        ns_kernel,
        in_specs=[vmem()] * 2 + [pl.BlockSpec(memory_space=pl.ANY)] * len(earlier),
        out_specs=vmem(),
        out_shape=jax.ShapeDtypeStruct((kept, half), LOW),
        scratch_shapes=[
            pltpu.VMEM((size, 2 * half), WIDE),
            pltpu.VMEM((size, 2 * half), LOW),
            pltpu.VMEM((size, size), WIDE),
            pltpu.VMEM((size, size), LOW),
        ],
        compiler_params=pltpu.CompilerParams(vmem_limit_bytes=VMEM_ASK),
        cost_estimate=pl.CostEstimate(
            flops=NS_STEPS * 10 * size * size * half,
            bytes_accessed=4 * size * half,
            transcendentals=0,
        ),
        name="orthogonal_rows",
    )(near, far, *earlier)
    return out[:rows]


def rotary_tables(places):
    half = ROT // 2
    exponent = jnp.arange(0, ROT, 2, dtype=WIDE) / ROT
    frequency = 1.0 / 10000.0**exponent
    angles = frequency[:, None] * places.astype(WIDE)[None, :]
    lane = jnp.arange(BLK) % HD
    picked = ((lane % half)[None, :] == jnp.arange(half)[:, None]) & (lane < ROT)[None, :]
    sign = jnp.where(lane < half, -1.0, 1.0)[None, :]
    spread = partial(
        jnp.einsum, "fn,fl->nl", precision=lax.Precision.HIGHEST, preferred_element_type=WIDE
    )
    cosine = spread(jnp.cos(angles), picked.astype(WIDE)) + (lane >= ROT)[None, :].astype(WIDE)
    return cosine, spread(jnp.sin(angles), picked * sign)


def body(
    tokens,
    cotangent,
    w_qkv,
    w_attn,
    w_up,
    w_down,
    norm_vectors,
    qkv_bias,
    up_bias,
    qkv_moment,
    attn_moment,
    up_moment,
    down_moment,
    norm_moment,
    qbias_moment,
    ubias_moment,
    seq_lengths,
    block_source,
):
    row_count, half = tokens.shape
    fsdp_count = lax.axis_size("fsdp")
    ctx_count = lax.axis_size("ctx")
    tp_index = lax.axis_index("tp")
    fsdp_index = lax.axis_index("fsdp")
    ctx_index = lax.axis_index("ctx")
    low_count = ctx_count // OWNERS
    ctx_low = ctx_index % low_count
    ctx_high = ctx_index // low_count
    width = 2 * half
    own_blocks = row_count // BLK
    pack = ctx_count * row_count
    first_tp = tp_index == 0
    block_row = block_source[0]
    length_row = seq_lengths[0]

    def both_halves(mine, other, dim):
        return jnp.concatenate(
            [jnp.where(first_tp, mine, other), jnp.where(first_tp, other, mine)], axis=dim
        )

    def own_half(array):
        return jnp.where(first_tp, array[:, :half], array[:, half:])

    def far_half(array):
        return jnp.where(first_tp, array[:, half:], array[:, :half])

    own_pair = jnp.concatenate([tokens, cotangent], axis=0)
    far_pair = partner(own_pair, "tp", 1)

    g_near = [
        jnp.concatenate(
            [cotangent] + [partner(cotangent, "ctx", s * low_count) for s in range(1, OWNERS)],
            axis=0,
        )
    ]
    x_near = lax.all_gather(tokens, "ctx", axis=0, tiled=True)
    x_far = partner(x_near, "tp", 1)

    def feed_stack(up, down):
        cuts = range(0, up.shape[1], half)
        return jnp.concatenate([up[:, i : i + half] for i in cuts] + [down], axis=0)

    def late_stack(qkv, attn):
        return jnp.concatenate([qkv[:, i] for i in range(3)] + [attn], axis=0)

    low_weights = [w.astype(LOW) for w in (w_up, w_down, w_qkv, w_attn)]
    if fsdp_count == 2:

        def exchanged(stack):
            other = partner(stack, "fsdp", 1)
            first = fsdp_index == 0
            return jnp.where(first, stack, other), jnp.where(first, other, stack)

        feed_stacks = exchanged(feed_stack(*low_weights[:2]))
        late_stacks = exchanged(after(late_stack(*low_weights[2:]), feed_stacks[0]))
    else:
        whole_up, whole_down, whole_qkv, whole_attn = (
            lax.all_gather(w, "fsdp", axis=dim, tiled=True)
            for w, dim in zip(low_weights, (0, 1, 0, 1))
        )
        cuts = (slice(0, half), slice(half, 2 * half))
        feed_stacks = tuple(feed_stack(whole_up[cut], whole_down[:, cut]) for cut in cuts)
        late_stacks = tuple(late_stack(whole_qkv[cut], whole_attn[:, cut]) for cut in cuts)
    hidden_here = up_bias.shape[0]
    attn_halves = tuple(part[3 * half :] for part in late_stacks)

    def by_partners(ctx):
        differs = ctx ^ ctx_index
        return (differs % low_count) * OWNERS + differs // low_count

    slot_blocks = jnp.arange(block_row.shape[0], dtype=jnp.int32)
    slot_ctx, slot_rest = slot_blocks // own_blocks, slot_blocks % own_blocks
    holds = block_row[None, :] == slot_blocks[:, None]

    def located(places):
        return jnp.sum(jnp.where(holds, places[None, :], 0), axis=1).astype(jnp.int32)

    natural = located(slot_blocks)
    by_partner = located(by_partners(slot_ctx) * own_blocks + slot_rest)
    stat_place = located((slot_ctx ^ ctx_index) * own_blocks + slot_rest)
    row_base = (ctx_index * row_count).reshape(1)
    my_blocks = lax.dynamic_slice_in_dim(block_row, ctx_index * own_blocks, own_blocks)

    seq_ends = jnp.cumsum(length_row).astype(jnp.int32)
    seq_starts = seq_ends - length_row

    def bounds(packed):
        inside = (packed[:, None] >= seq_starts[None, :]) & (packed[:, None] < seq_ends[None, :])
        return (
            jnp.sum(jnp.where(inside, seq_starts[None, :], 0), axis=1).astype(jnp.int32),
            jnp.sum(jnp.where(inside, seq_ends[None, :], 0), axis=1).astype(jnp.int32),
        )

    offsets = jnp.arange(BLK, dtype=jnp.int32)
    packed = (block_row[:, None] * BLK + offsets[None, :]).reshape(-1)
    cosine, sine = rotary_tables(packed - bounds(packed)[0])
    my_starts, my_ends = bounds(
        (my_blocks[:, None] * BLK + offsets[None, :]).reshape(-1)
    )
    key_first = bounds(my_blocks * BLK)[0] // CHUNK
    key_last = (my_blocks * BLK + BLK - 1) // CHUNK + 1
    query_first = my_blocks * BLK // CHUNK
    query_last = (bounds(my_blocks * BLK + BLK - 1)[1] + CHUNK - 1) // CHUNK

    def own_first(array, dim):
        left, right = jnp.split(array, 2, axis=dim)
        return jnp.where(first_tp, left, right), jnp.where(first_tp, right, left)

    piece = width // (fsdp_count * ctx_count)

    def my_rows(array, dim):
        return lax.dynamic_slice_in_dim(array, ctx_index * piece, piece, dim)

    def as_rows(up, attn, qkv, down):
        rows = (
            my_rows(up, 0),
            my_rows(attn, 1).T,
            jnp.concatenate([my_rows(qkv, 0)[:, i] for i in range(3)], axis=1),
            my_rows(down, 1).T,
        )
        return jnp.stack([jnp.pad(r, ((0, 0), (0, hidden_here - r.shape[1]))) for r in rows])

    old_moments = as_rows(up_moment, attn_moment, qkv_moment, down_moment)
    old_weights = as_rows(w_up, w_attn, w_qkv, w_down)

    def two_halves(mine, other):
        return jnp.where(first_tp, mine, other), jnp.where(first_tp, other, mine)

    x_halves = [half_x.astype(WIDE) for half_x in two_halves(tokens, far_pair[:row_count])]
    row_mean = sum(jnp.sum(x, axis=1, keepdims=True) for x in x_halves) / width
    centered = [x - row_mean for x in x_halves]
    inv_std = lax.rsqrt(sum(jnp.sum(x * x, axis=1, keepdims=True) for x in centered) / width + 1e-5)
    norm_halves = [
        (x * inv_std * vec[0] + vec[1]).astype(LOW)
        for x, vec in zip(centered, jnp.split(norm_vectors, 2, axis=1))
    ]
    feed_out, feed_dx, grad_up, grad_down, grad_ubias, norm_t, cotangent_t = feed_forward(
        norm_halves,
        two_halves(cotangent, far_pair[row_count:]),
        feed_stacks,
        up_bias.reshape(1, hidden_here),
        (old_moments, old_weights, cosine, sine),
    )
    for s in range(1, low_count):
        g_near.append(partner(g_near[0], "ctx", s))
    g_far = [partner(part, "tp", 1) for part in [g_near[0]] + [after(p, grad_ubias) for p in g_near[1:]]]

    queries, keys, values = project_rows(
        x_near,
        x_far,
        (*two_halves(*late_stacks), qkv_bias, *own_first(norm_vectors, 1)),
        cosine,
        sine,
    )
    attn_near, attn_far = two_halves(*attn_halves)
    d_attended = jnp.concatenate(
        [
            (dot_nt(near, attn_near) + dot_nt(far, attn_far)).astype(LOW)
            for near, far in zip(g_near, g_far)
        ],
        axis=0,
    )

    def reduced_first(gradient, *earlier):
        rows = gradient.shape[0] // fsdp_count
        pieces = gradient.reshape(fsdp_count, rows, gradient.shape[1])
        return sum_scatter(pieces, "fsdp", 1, fsdp_index, *earlier)

    def reduced_rest(part):
        piece = part.shape[0] // ctx_count
        part = part.reshape(OWNERS, low_count, piece, part.shape[1])
        part = sum_scatter(jnp.swapaxes(part, 0, 1), "ctx", 1, ctx_low)
        return sum_scatter(part, "ctx", low_count, ctx_high)

    first_up, first_down = (reduced_first(grad, queries) for grad in (grad_up, grad_down))
    grad_outbias = jnp.sum(cotangent.astype(WIDE), axis=0)

    attended, grad_q, stats = query_side(
        my_blocks,
        key_first,
        key_last,
        natural,
        row_base,
        queries,
        keys,
        values,
        d_attended,
        cosine,
        sine,
        my_starts[:, None],
    )
    sum_feed = lax.psum_scatter(
        jnp.concatenate([first_up, first_down], axis=1).astype(LOW),
        "ctx",
        scatter_dimension=0,
        tiled=True,
    ).astype(WIDE)
    sum_up, sum_down = sum_feed[:, :hidden_here], sum_feed[:, hidden_here:]

    early_rows = reduced_first(outer_pair(norm_t, grad_q, cotangent_t, attended))
    all_stats = stats
    step = 1
    while step < ctx_count:
        all_stats = jnp.concatenate([all_stats, partner(all_stats, "ctx", step)], axis=0)
        step *= 2
    grad_k, grad_v = key_side(
        my_blocks,
        query_first,
        query_last,
        natural,
        by_partner,
        stat_place,
        row_base,
        queries,
        keys,
        values,
        d_attended,
        cosine,
        sine,
        my_ends[:, None],
        all_stats,
        (first_up, first_down),
    )
    grad_late = outer_pair(norm_t, after(grad_k, sum_feed), norm_t, grad_v)
    late_rows = reduced_first(grad_late)
    joint_rows = jnp.concatenate([early_rows, late_rows], axis=1)
    sum_joint = reduced_rest(joint_rows)
    grad_proj = [after(grad, late_rows) for grad in (grad_q, grad_k, grad_v)]
    grad_qbias = jnp.concatenate([jnp.sum(grad.astype(WIDE), axis=0) for grad in grad_proj])

    def joined(pair):
        return jnp.concatenate(pair, axis=1)

    partial_out = joined([dot_nn(attended, attn) for attn in attn_halves]) + feed_out

    def sum_halves(array):
        return own_half(array) + partner(far_half(array).astype(LOW), "tp", 1).astype(WIDE)

    out_bias = own_half((norm_vectors[2] + norm_vectors[3])[None, :])
    mixed = (tokens.astype(WIDE) + sum_halves(partial_out) + out_bias).astype(LOW)

    grad_norm = sum_halves(
        joined(
            [
                sum(
                    dot_nt(grad, stack[i * half : (i + 1) * half])
                    for i, grad in enumerate(grad_proj)
                )
                for stack in late_stacks
            ]
        )
        + feed_dx
    )
    my_normed = jnp.where(first_tp, *centered) * inv_std
    scaled = grad_norm * own_half(norm_vectors[0:1])
    row_sums = jnp.stack([jnp.sum(scaled, axis=1), jnp.sum(scaled * my_normed, axis=1)])
    row_means = (row_sums + partner(row_sums, "tp", 1)) / width
    grad_tokens = cotangent.astype(WIDE) + inv_std * (
        scaled - row_means[0][:, None] - my_normed * row_means[1][:, None]
    )

    vector_parts = jnp.stack(
        [jnp.sum(grad_norm * my_normed, axis=0), jnp.sum(grad_norm, axis=0), grad_outbias]
    )
    small = jnp.concatenate([vector_parts.reshape(-1), grad_qbias, grad_ubias[0]])
    small = sum_everywhere(small, ("ctx",))
    small = sum_everywhere(after(small, sum_joint), ("fsdp",))
    mine = small[: 3 * half].reshape(3, half)
    vectors = both_halves(mine, partner(mine, "tp", 1), 1)
    sum_vectors = jnp.concatenate([vectors, vectors[2:3]], axis=0)
    sum_qbias = small[3 * half : 6 * half].reshape(3, half)
    sum_ubias = small[6 * half :]

    def all_rows(sums):
        return lax.all_gather(sums, "ctx", axis=0, tiled=True)

    feed_rows = all_rows(sum_feed.astype(LOW))
    joint_all = all_rows(after(sum_joint.astype(LOW), feed_rows)).astype(WIDE)
    all_up, all_down = jnp.split(feed_rows.astype(WIDE), 2, axis=1)
    fresh_up = 0.95 * up_moment + all_up
    fresh_down = 0.95 * down_moment + all_down.T
    all_q, all_attn, all_k, all_v = jnp.split(joint_all, 4, axis=1)
    fresh_qkv = 0.95 * qkv_moment + jnp.stack([all_q, all_k, all_v], axis=1)
    fresh_attn = 0.95 * attn_moment + all_attn.T

    own_q, own_attn, own_k, own_v = jnp.split(sum_joint, 4, axis=1)
    sums = (sum_up, own_attn, jnp.concatenate([own_q, own_k, own_v], axis=1), sum_down)
    pieces = jnp.stack(
        [
            (
                0.95 * moment + jnp.pad(total, ((0, 0), (0, hidden_here - total.shape[1])))
            ).astype(LOW)
            for moment, total in zip(old_moments, sums)
        ]
    )

    def to_owner(step):
        picked = lax.dynamic_index_in_dim(pieces, ctx_high ^ step, 0, keepdims=False)
        return partner(picked, "ctx", step * low_count) if step else picked

    matrix = jnp.concatenate([to_owner(s) for s in range(OWNERS)], axis=0)
    parts = [matrix] + [partner(matrix, "ctx", s) for s in range(1, low_count)]
    for s in range(1, fsdp_count):
        parts += [partner(part, "fsdp", s) for part in parts[:low_count]]
    groups = [
        jnp.concatenate(parts[i : i + low_count], axis=0) for i in range(0, len(parts), low_count)
    ]
    near_cols = jnp.concatenate(groups, axis=0)
    far_cols = jnp.concatenate([partner(group, "tp", 1) for group in groups], axis=0)
    rows_out = orthogonal_rows(
        near_cols, far_cols, OWNERS * piece, (fresh_up, fresh_down)
    ).reshape(OWNERS, piece, hidden_here)
    returned = [rows_out[0]] + [
        partner(rows_out[s], "ctx", s * low_count) for s in range(1, OWNERS)
    ]
    returned = jnp.stack([after(part, fresh_qkv, fresh_attn) for part in returned])
    full_hidden = hidden_here * 2
    rates = (
        0.5 * math.sqrt(full_hidden / width),
        0.5 * math.sqrt(width / (width // HD)),
        0.5 * math.sqrt(3 * width / width),
        0.5 * math.sqrt(full_hidden / full_hidden),
    )
    new_up, new_attn, new_qkv, new_down = (
        old_weights[m]
        - rate * lax.dynamic_index_in_dim(returned, ctx_high ^ m, 0, keepdims=False).astype(WIDE)
        for m, rate in enumerate(rates)
    )
    new_attn, new_qkv = new_attn[:, :half], new_qkv[:, : 3 * half]

    vector_rate = 0.3 / math.sqrt(row_count * fsdp_count * ctx_count)
    mom_norm = 0.9 * norm_moment + sum_vectors
    mom_qbias = 0.9 * qbias_moment + sum_qbias
    mom_ubias = 0.9 * ubias_moment + sum_ubias
    return (
        mixed,
        grad_tokens,
        fresh_qkv,
        jnp.stack(jnp.split(new_qkv, 3, axis=1), axis=1),
        fresh_attn,
        new_attn.T,
        fresh_up,
        new_up,
        fresh_down,
        new_down.T,
        mom_norm,
        norm_vectors - vector_rate * mom_norm,
        mom_qbias,
        qkv_bias - vector_rate * mom_qbias,
        mom_ubias,
        up_bias - vector_rate * mom_ubias,
    )


def solution(mesh):
    return jax.shard_map(
        body,
        mesh=mesh,
        in_specs=(
            P(("fsdp", "ctx"), "tp"),
            P(("fsdp", "ctx"), "tp"),
            P("fsdp", None, "tp"),
            P("tp", "fsdp"),
            P("fsdp", "tp"),
            P("tp", "fsdp"),
            P(),
            P(None, "tp"),
            P("tp"),
            P("fsdp", None, "tp"),
            P("tp", "fsdp"),
            P("fsdp", "tp"),
            P("tp", "fsdp"),
            P(),
            P(None, "tp"),
            P("tp"),
            P("fsdp", None),
            P("fsdp", None),
        ),
        out_specs=(
            P(("fsdp", "ctx"), "tp"),
            P(("fsdp", "ctx"), "tp"),
            P("fsdp", None, "tp"),
            P(("fsdp", "ctx"), None, "tp"),
            P("tp", "fsdp"),
            P("tp", ("fsdp", "ctx")),
            P("fsdp", "tp"),
            P(("fsdp", "ctx"), "tp"),
            P("tp", "fsdp"),
            P("tp", ("fsdp", "ctx")),
            P(),
            P(),
            P(None, "tp"),
            P(None, "tp"),
            P("tp"),
            P("tp"),
        ),
        check_vma=False,
    )
```

```python
from functools import partial
import math

import jax
import jax.numpy as jnp
from jax import lax
from jax.experimental import pallas as pl
from jax.experimental.pallas import tpu as pltpu
from jax.sharding import PartitionSpec as P

HD = 64
ROT = 16
BLK = 128
NS_STEPS = 5
CHUNK = 512
MAX_LEN = 2048
SPAN = (MAX_LEN + BLK) // CHUNK + 2
OWNERS = 4
NS_COEF = (3.4445, -4.775, 2.0315)
NEG_BIG = -1e30
SCALE = HD**-0.5
LOW = jnp.bfloat16
WIDE = jnp.float32
NT = (((1,), (1,)), ((), ()))
VMEM_ASK = 56 * 1024 * 1024


def dot_nn(left, right):
    return jnp.dot(left, right, preferred_element_type=WIDE)


def dot_nt(left, right):
    return lax.dot_general(left, right, NT, preferred_element_type=WIDE)


def partner(value, axis, step):
    size = lax.axis_size(axis)
    return lax.ppermute(value, axis, [(i, i ^ step) for i in range(size)])


def sum_scatter(pieces, axis, stride, index, *earlier):
    count = pieces.shape[0]
    total = lax.dynamic_index_in_dim(pieces, index, 0, keepdims=False)
    total = after(total, *earlier).astype(WIDE)
    for step in range(1, count):
        piece = lax.dynamic_index_in_dim(pieces, index ^ step, 0, keepdims=False)
        total = total + partner(piece.astype(LOW), axis, step * stride).astype(WIDE)
    return total


def after(value, *earlier):
    return lax.optimization_barrier((value, *earlier))[0]


def sum_everywhere(value, axes):
    for axis in axes:
        step = 1
        while step < lax.axis_size(axis):
            value = value + partner(value, axis, step)
            step *= 2
    return value


def turned(block, cosine, sine, lane):
    half = ROT // 2
    swapped = jnp.where(
        lane % HD < half, pltpu.roll(block, BLK - half, 1), pltpu.roll(block, half, 1)
    )
    return block * cosine + swapped * sine


def two_heads(block, lane):
    zero = jnp.zeros_like(block)
    return jnp.concatenate(
        [jnp.where(lane < HD, block, zero), jnp.where(lane < HD, zero, block)], axis=0
    )


def one_of_two(stacked, lane):
    return jnp.where(lane < HD, stacked[:BLK], stacked[BLK:])


def project_kernel(
    near, far, w_near, w_far, bias, vec_near, vec_far, cos_ref, sin_ref, *outs
):
    rows, half = outs[0].shape
    width = 2 * half
    own, other = near[...].astype(WIDE), far[...].astype(WIDE)
    mean = (
        jnp.sum(own, axis=1, keepdims=True) + jnp.sum(other, axis=1, keepdims=True)
    ) / width
    own, other = own - mean, other - mean
    var = (
        jnp.sum(own * own, axis=1, keepdims=True) + jnp.sum(other * other, axis=1, keepdims=True)
    ) / width
    inv_std = lax.rsqrt(var + 1e-5)
    own = (own * inv_std * vec_near[0:1] + vec_near[1:2]).astype(LOW)
    other = (other * inv_std * vec_far[0:1] + vec_far[1:2]).astype(LOW)
    lane = lax.broadcasted_iota(jnp.int32, (rows, BLK), 1)
    cosine, sine = cos_ref[...], sin_ref[...]
    for part, out in enumerate(outs):
        span = slice(part * half, (part + 1) * half)
        made = dot_nn(own, w_near[span]) + dot_nn(other, w_far[span]) + bias[part : part + 1]
        for pair in range(half // BLK):
            lanes = slice(pair * BLK, (pair + 1) * BLK)
            block = made[:, lanes]
            if part < 2:
                block = turned(block, cosine, sine, lane)
            out[:, lanes] = block.astype(LOW)


def project_rows(near, far, weights, cosine, sine):
    rows, half = near.shape

    def fixed(array):
        return pl.BlockSpec(array.shape, lambda i: (0,) * array.ndim)

    def chunk(width):
        return pl.BlockSpec((CHUNK, width), lambda i: (i, 0))

    return pl.pallas_call(
        project_kernel,
        grid=(rows // CHUNK,),
        in_specs=[chunk(half)] * 2 + [fixed(w) for w in weights] + [chunk(BLK)] * 2,
        out_specs=[chunk(half)] * 3,
        out_shape=[jax.ShapeDtypeStruct((rows, half), LOW)] * 3,
        compiler_params=pltpu.CompilerParams(vmem_limit_bytes=VMEM_ASK),
        cost_estimate=pl.CostEstimate(
            flops=44 * rows * half * half, bytes_accessed=14 * rows * half, transcendentals=0
        ),
        name="project_rows",
    )(near, far, *weights, cosine, sine)


def feed_kernel(
    xa_ref,
    xb_ref,
    ga_ref,
    gb_ref,
    up_a,
    up_b,
    down_a,
    down_b,
    bias_ref,
    *refs,
):
    out_ref, dx_ref, dup_ref, ddown_ref, dbias_ref, xt_ref, gt_ref = refs[-7:]
    half = xa_ref.shape[1]
    first, second = slice(0, half), slice(half, 2 * half)

    @pl.when(pl.program_id(0) == 0)
    def _():
        xt_ref[first] = xa_ref[...].T
        xt_ref[second] = xb_ref[...].T
        gt_ref[first] = ga_ref[...].T
        gt_ref[second] = gb_ref[...].T
        out_ref[...] = jnp.zeros(out_ref.shape, WIDE)
        dx_ref[...] = jnp.zeros(dx_ref.shape, WIDE)

    hidden = dot_nn(xa_ref[...], up_a[...]) + dot_nn(xb_ref[...], up_b[...]) + bias_ref[...]
    grad = dot_nt(ga_ref[...], down_a[...]) + dot_nt(gb_ref[...], down_b[...])
    below = 0.5 + 0.5 * lax.erf(hidden * math.sqrt(0.5))
    density = jnp.exp(-0.5 * hidden * hidden) * (1.0 / math.sqrt(2.0 * math.pi))
    active = (hidden * below).astype(LOW)
    grad = (grad * (below + hidden * density)).astype(LOW)
    dbias_ref[...] = jnp.sum(grad.astype(WIDE), axis=0, keepdims=True)
    out_ref[:, first] += dot_nn(active, down_a[...])
    out_ref[:, second] += dot_nn(active, down_b[...])
    dx_ref[:, first] += dot_nt(grad, up_a[...])
    dx_ref[:, second] += dot_nt(grad, up_b[...])
    dup_ref[...] = dot_nn(xt_ref[...], grad).astype(LOW)
    ddown_ref[...] = dot_nn(gt_ref[...], active).astype(LOW)


def feed_forward(x_halves, g_halves, stacks, bias, earlier):
    rows, half = x_halves[0].shape
    width = 2 * half
    hidden = bias.shape[1]
    steps = hidden // half

    def whole(shape):
        return pl.BlockSpec(shape, lambda i: (0, 0))

    up = pl.BlockSpec((half, half), lambda i: (i, 0))
    down = pl.BlockSpec((half, half), lambda i: (i + steps, 0))
    column = pl.BlockSpec((width, half), lambda i: (0, i))
    line = pl.BlockSpec((1, half), lambda i: (0, i))
    return pl.pallas_call(
        feed_kernel,
        grid=(steps,),
        in_specs=[whole((rows, half))] * 4
        + [up, up, down, down, line]
        + [pl.BlockSpec(memory_space=pl.ANY)] * len(earlier),
        out_specs=[
            whole((rows, width)),
            whole((rows, width)),
            column,
            column,
            line,
            whole((width, rows)),
            whole((width, rows)),
        ],
        out_shape=[
            jax.ShapeDtypeStruct((rows, width), WIDE),
            jax.ShapeDtypeStruct((rows, width), WIDE),
            jax.ShapeDtypeStruct((width, hidden), LOW),
            jax.ShapeDtypeStruct((width, hidden), LOW),
            jax.ShapeDtypeStruct((1, hidden), WIDE),
            jax.ShapeDtypeStruct((width, rows), LOW),
            jax.ShapeDtypeStruct((width, rows), LOW),
        ],
        compiler_params=pltpu.CompilerParams(vmem_limit_bytes=VMEM_ASK),
        cost_estimate=pl.CostEstimate(
            flops=26 * rows * width * hidden, bytes_accessed=12 * width * hidden, transcendentals=0
        ),
        name="feed_forward",
    )(*x_halves, *g_halves, *stacks, *stacks, bias, *earlier)


def outer_kernel(left_a, right_a, left_b, right_b, out_ref):
    half = right_a.shape[1]
    out_ref[:, :half] = dot_nn(left_a[...], right_a[...]).astype(LOW)
    out_ref[:, half:] = dot_nn(left_b[...], right_b[...]).astype(LOW)


def outer_pair(left_a, right_a, left_b, right_b):
    rows, depth = left_a.shape
    half = right_a.shape[1]
    return pl.pallas_call(
        outer_kernel,
        in_specs=[vmem()] * 4,
        out_specs=vmem(),
        out_shape=jax.ShapeDtypeStruct((rows, 2 * half), LOW),
        compiler_params=pltpu.CompilerParams(vmem_limit_bytes=VMEM_ASK),
        cost_estimate=pl.CostEstimate(
            flops=8 * rows * depth * half, bytes_accessed=6 * rows * depth, transcendentals=0
        ),
        name="outer_pair",
    )(left_a, right_a, left_b, right_b)


def lane_tiles(array, combine):
    total = array[:, :BLK]
    for i in range(1, array.shape[1] // BLK):
        total = combine(total, array[:, i * BLK : (i + 1) * BLK])
    return total


def gathered_blocks(ref, inverse, chunk, lanes):
    count = CHUNK // BLK
    return jnp.concatenate(
        [
            ref[pl.ds(pl.multiple_of(inverse[chunk * count + i] * BLK, BLK), BLK), lanes]
            for i in range(count)
        ],
        axis=0,
    )


def query_kernel(
    blocks,
    first,
    last,
    natural,
    base,
    q_ref,
    k_ref,
    v_ref,
    d_ref,
    cos_ref,
    sin_ref,
    start_ref,
    att_out,
    dq_out,
    stat_out,
    s_scr,
    p_scr,
    q_scr,
    d_scr,
    m_scr,
    l_scr,
    e_scr,
    o_scr,
):
    pairs = q_ref.shape[1] // BLK
    own = att_out.shape[0] // BLK
    lane = lax.broadcasted_iota(jnp.int32, (BLK, BLK), 1)

    def lanes(pair):
        return slice(pair * BLK, (pair + 1) * BLK)

    @pl.loop(0, own)
    def _(j):
        row0 = pl.multiple_of(blocks[j] * BLK, BLK)
        out0 = pl.multiple_of(j * BLK, BLK)
        here = pl.multiple_of(base[0] + out0, BLK)
        lo = first[j]
        hi = last[j]
        for g in range(pairs):
            q_scr[g] = two_heads(q_ref[pl.ds(here, BLK), lanes(g)].astype(WIDE), lane).astype(
                LOW
            ) * LOW(SCALE)
            d_scr[g] = two_heads(d_ref[pl.ds(out0, BLK), lanes(g)].astype(WIDE), lane).astype(LOW)
        m_scr[...] = jnp.full(m_scr.shape, NEG_BIG, WIDE)
        l_scr[...] = jnp.zeros(l_scr.shape, WIDE)
        e_scr[...] = jnp.zeros(e_scr.shape, WIDE)
        o_scr[...] = jnp.zeros(o_scr.shape, WIDE)
        starts = start_ref[pl.ds(out0, BLK), :]
        places = row0 + lax.broadcasted_iota(jnp.int32, (BLK, 1), 0)
        starts = jnp.concatenate([starts, starts], axis=0)
        places = jnp.concatenate([places, places], axis=0)

        @pl.loop(lo, hi)
        def _(c):
            key0 = pl.multiple_of(c * CHUNK, CHUNK)
            key_place = key0 + lax.broadcasted_iota(jnp.int32, (2 * BLK, CHUNK), 1)
            allowed = (key_place >= starts) & (key_place <= places)
            for g in range(pairs):
                scores = dot_nt(q_scr[g], gathered_blocks(k_ref, natural, c, lanes(g)))
                scores = jnp.where(allowed, scores, NEG_BIG)
                s_scr[g, c - lo] = scores
                m_scr[g] = jnp.maximum(m_scr[g], lane_tiles(scores, jnp.maximum))

        for g in range(pairs):
            m_scr[g] = jnp.broadcast_to(
                jnp.max(m_scr[g], axis=1, keepdims=True), (2 * BLK, BLK)
            )

        @pl.loop(lo, hi)
        def _(c):
            for g in range(pairs):
                values = gathered_blocks(v_ref, natural, c, lanes(g))
                top = m_scr[g]
                weights = jnp.exp(s_scr[g, c - lo] - jnp.concatenate([top] * (CHUNK // BLK), 1))
                l_scr[g] += lane_tiles(weights, jnp.add)
                o_scr[g] += dot_nn(weights.astype(LOW), values)
                grad_prob = dot_nt(d_scr[g], values)
                e_scr[g] += lane_tiles(weights * grad_prob, jnp.add)
                s_scr[g, c - lo] = weights
                p_scr[g, c - lo] = grad_prob

        for g in range(pairs):
            total = jnp.sum(l_scr[g], axis=1, keepdims=True)
            share = 1.0 / total
            delta = jnp.sum(e_scr[g], axis=1, keepdims=True) * share
            att_out[pl.ds(out0, BLK), lanes(g)] = one_of_two(o_scr[g] * share, lane).astype(LOW)
            log_sum = m_scr[g] + jnp.log(total)
            stat_out[j, 2 * g : 2 * g + 1, :] = log_sum[:BLK].T[0:1]
            stat_out[j, 2 * g + 1 : 2 * g + 2, :] = log_sum[BLK:].T[0:1]
            wide = jnp.broadcast_to(delta, (2 * BLK, BLK))
            line = stat_out.shape[1] // 2 + 2 * g
            stat_out[j, line : line + 1, :] = wide[:BLK].T[0:1]
            stat_out[j, line + 1 : line + 2, :] = wide[BLK:].T[0:1]
            l_scr[g] = jnp.broadcast_to(share, (2 * BLK, BLK))
            e_scr[g] = wide
        o_scr[...] = jnp.zeros(o_scr.shape, WIDE)

        @pl.loop(lo, hi)
        def _(c):
            for g in range(pairs):
                wide = jnp.concatenate([e_scr[g]] * (CHUNK // BLK), 1)
                grad_score = s_scr[g, c - lo] * (p_scr[g, c - lo] - wide)
                o_scr[g] += dot_nn(
                    grad_score.astype(LOW), gathered_blocks(k_ref, natural, c, lanes(g))
                )

        cosine = cos_ref[pl.ds(here, BLK), :]
        sine = sin_ref[pl.ds(here, BLK), :]
        for g in range(pairs):
            grad = one_of_two(o_scr[g] * l_scr[g], lane) * SCALE
            dq_out[pl.ds(out0, BLK), lanes(g)] = turned(grad, cosine, -sine, lane).astype(LOW)


def smem():
    return pl.BlockSpec(memory_space=pltpu.SMEM)


def vmem():
    return pl.BlockSpec(memory_space=pltpu.VMEM)


def query_side(blocks, first, last, natural, base, queries, keys, values, grads, cosine, sine, starts):
    own = blocks.shape[0]
    width = queries.shape[1]
    pairs = width // BLK
    stat_rows = 16 * ((2 * pairs + 7) // 8)
    work = 2 * BLK * CHUNK
    return pl.pallas_call(
        query_kernel,
        in_specs=[smem()] * 5 + [vmem()] * 7,
        out_specs=[vmem()] * 3,
        out_shape=[
            jax.ShapeDtypeStruct((own * BLK, width), LOW),
            jax.ShapeDtypeStruct((own * BLK, width), LOW),
            jax.ShapeDtypeStruct((own, stat_rows, BLK), WIDE),
        ],
        scratch_shapes=[
            pltpu.VMEM((pairs, SPAN, 2 * BLK, CHUNK), WIDE),
            pltpu.VMEM((pairs, SPAN, 2 * BLK, CHUNK), WIDE),
            pltpu.VMEM((pairs, 2 * BLK, BLK), LOW),
            pltpu.VMEM((pairs, 2 * BLK, BLK), LOW),
            pltpu.VMEM((pairs, 2 * BLK, BLK), WIDE),
            pltpu.VMEM((pairs, 2 * BLK, BLK), WIDE),
            pltpu.VMEM((pairs, 2 * BLK, BLK), WIDE),
            pltpu.VMEM((pairs, 2 * BLK, BLK), WIDE),
        ],
        compiler_params=pltpu.CompilerParams(vmem_limit_bytes=VMEM_ASK),
        cost_estimate=pl.CostEstimate(
            flops=own * pairs * 12 * 4 * 2 * work * BLK,
            bytes_accessed=4 * keys.shape[0] * width * 2,
            transcendentals=own * pairs * 4 * work,
        ),
        name="query_side",
    )(blocks, first, last, natural, base, queries, keys, values, grads, cosine, sine, starts)


def key_kernel(
    blocks,
    first,
    last,
    natural,
    by_partner,
    stat_place,
    base,
    q_ref,
    k_ref,
    v_ref,
    d_ref,
    cos_ref,
    sin_ref,
    end_ref,
    stat_ref,
    *rest,
):
    dk_out, dv_out, k_scr, v_scr, dk_scr, dv_scr = rest[-6:]
    pairs = q_ref.shape[1] // BLK
    own = dk_out.shape[0] // BLK
    half_stat = stat_ref.shape[1] // 2
    lane = lax.broadcasted_iota(jnp.int32, (BLK, BLK), 1)

    def lanes(pair):
        return slice(pair * BLK, (pair + 1) * BLK)

    @pl.loop(0, own)
    def _(j):
        row0 = pl.multiple_of(blocks[j] * BLK, BLK)
        out0 = pl.multiple_of(j * BLK, BLK)
        here = pl.multiple_of(base[0] + out0, BLK)
        for g in range(pairs):
            k_scr[g] = two_heads(k_ref[pl.ds(here, BLK), lanes(g)].astype(WIDE), lane).astype(
                LOW
            ) * LOW(SCALE)
            v_scr[g] = two_heads(v_ref[pl.ds(here, BLK), lanes(g)].astype(WIDE), lane).astype(LOW)
        dk_scr[...] = jnp.zeros(dk_scr.shape, WIDE)
        dv_scr[...] = jnp.zeros(dv_scr.shape, WIDE)
        ends = end_ref[pl.ds(out0, BLK), :]
        places = row0 + lax.broadcasted_iota(jnp.int32, (BLK, 1), 0)

        @pl.loop(first[j], last[j])
        def _(c):
            query0 = pl.multiple_of(c * CHUNK, CHUNK)
            query_place = query0 + lax.broadcasted_iota(jnp.int32, (BLK, CHUNK), 1)
            allowed = (query_place >= places) & (query_place < ends)
            count = CHUNK // BLK
            slots = [stat_place[c * count + i] for i in range(count)]

            def stat(row):
                return jnp.concatenate([stat_ref[slot, row : row + 1, :] for slot in slots], 1)

            for g in range(pairs):
                queries = gathered_blocks(q_ref, natural, c, lanes(g))
                grads = gathered_blocks(d_ref, by_partner, c, lanes(g))
                scores = dot_nt(k_scr[g], queries)
                grad_prob = dot_nt(v_scr[g], grads)
                probs, grad_scores = [], []
                for h in range(2):
                    rows = slice(h * BLK, (h + 1) * BLK)
                    shifted = jnp.where(allowed, scores[rows] - stat(2 * g + h), NEG_BIG)
                    prob = jnp.exp(shifted)
                    probs.append(prob.astype(LOW))
                    grad_scores.append(
                        (prob * (grad_prob[rows] - stat(half_stat + 2 * g + h))).astype(LOW)
                    )
                dv_scr[g] += dot_nn(jnp.concatenate(probs, 0), grads)
                dk_scr[g] += dot_nn(jnp.concatenate(grad_scores, 0), queries)

        cosine = cos_ref[pl.ds(here, BLK), :]
        sine = sin_ref[pl.ds(here, BLK), :]
        for g in range(pairs):
            grad = one_of_two(dk_scr[g], lane) * SCALE
            dk_out[pl.ds(out0, BLK), lanes(g)] = turned(grad, cosine, -sine, lane).astype(LOW)
            dv_out[pl.ds(out0, BLK), lanes(g)] = one_of_two(dv_scr[g], lane).astype(LOW)


def key_side(
    blocks,
    first,
    last,
    natural,
    by_partner,
    stat_place,
    base,
    queries,
    keys,
    values,
    grads,
    cosine,
    sine,
    ends,
    stats,
    after,
):
    own = blocks.shape[0]
    width = queries.shape[1]
    pairs = width // BLK
    work = 2 * BLK * CHUNK
    return pl.pallas_call(
        key_kernel,
        in_specs=[smem()] * 7 + [vmem()] * 8 + [pl.BlockSpec(memory_space=pl.ANY)] * len(after),
        out_specs=[vmem()] * 2,
        out_shape=[jax.ShapeDtypeStruct((own * BLK, width), LOW)] * 2,
        scratch_shapes=[
            pltpu.VMEM((pairs, 2 * BLK, BLK), LOW),
            pltpu.VMEM((pairs, 2 * BLK, BLK), LOW),
            pltpu.VMEM((pairs, 2 * BLK, BLK), WIDE),
            pltpu.VMEM((pairs, 2 * BLK, BLK), WIDE),
        ],
        compiler_params=pltpu.CompilerParams(vmem_limit_bytes=VMEM_ASK),
        cost_estimate=pl.CostEstimate(
            flops=own * pairs * 12 * 4 * 2 * work * BLK,
            bytes_accessed=4 * keys.shape[0] * width * 2,
            transcendentals=own * pairs * 4 * work,
        ),
        name="key_side",
    )(
        blocks,
        first,
        last,
        natural,
        by_partner,
        stat_place,
        base,
        queries,
        keys,
        values,
        grads,
        cosine,
        sine,
        ends,
        stats,
        *after,
    )


TILE = 256


def symmetric_product(out_ref, left, right):
    size = out_ref.shape[0]
    for i in range(0, size, TILE):
        out_ref[i : i + TILE, i:] = dot_nt(left[i : i + TILE, :], right[i:, :])
    for i in range(0, size, TILE):
        for j in range(i + TILE, size, TILE):
            out_ref[j : j + TILE, i : i + TILE] = out_ref[i : i + TILE, j : j + TILE].T


def ns_kernel(near_ref, far_ref, *refs):
    out_ref, wide_scr, low_scr, gram_scr, poly_scr = refs[-5:]
    size, half = near_ref.shape
    span = 2 * half
    step = 768
    cuts = [slice(i, i + step) for i in range(0, span, step)]
    total = jnp.zeros((1, 1), WIDE)
    for source, base in ((near_ref, 0), (far_ref, half)):
        for i in range(0, half, step):
            part = source[:, i : i + step].astype(WIDE)
            wide_scr[:, base + i : base + i + step] = part
            total = total + jnp.sum(part * part)
    factor = 1.0 / (jnp.sqrt(total) + 1e-7)
    for cut in cuts:
        part = wide_scr[:, cut] * factor
        wide_scr[:, cut] = part
        low_scr[:, cut] = part.astype(LOW)

    def polynomial():
        symmetric_product(gram_scr, low_scr, low_scr)
        poly_scr[...] = gram_scr[...].astype(LOW)
        first = gram_scr[...] * NS_COEF[1]
        symmetric_product(gram_scr, poly_scr, poly_scr)
        poly_scr[...] = (first + NS_COEF[2] * gram_scr[...]).astype(LOW)

    @pl.loop(0, NS_STEPS - 1)
    def _(_):
        polynomial()
        for cut in cuts:
            part = NS_COEF[0] * wide_scr[:, cut] + dot_nn(poly_scr[...], low_scr[:, cut])
            wide_scr[:, cut] = part
            low_scr[:, cut] = part.astype(LOW)

    polynomial()
    rows = out_ref.shape[0]
    for i in range(0, half, step):
        cut = slice(i, i + step)
        out_ref[:, cut] = (
            NS_COEF[0] * wide_scr[:rows, cut] + dot_nn(poly_scr[:rows, :], low_scr[:, cut])
        ).astype(LOW)


def orthogonal_rows(near, far, rows, earlier):
    size, half = near.shape
    kept = rows if rows % 16 == 0 else size
    out = pl.pallas_call(
        ns_kernel,
        in_specs=[vmem()] * 2 + [pl.BlockSpec(memory_space=pl.ANY)] * len(earlier),
        out_specs=vmem(),
        out_shape=jax.ShapeDtypeStruct((kept, half), LOW),
        scratch_shapes=[
            pltpu.VMEM((size, 2 * half), WIDE),
            pltpu.VMEM((size, 2 * half), LOW),
            pltpu.VMEM((size, size), WIDE),
            pltpu.VMEM((size, size), LOW),
        ],
        compiler_params=pltpu.CompilerParams(vmem_limit_bytes=VMEM_ASK),
        cost_estimate=pl.CostEstimate(
            flops=NS_STEPS * 10 * size * size * half,
            bytes_accessed=4 * size * half,
            transcendentals=0,
        ),
        name="orthogonal_rows",
    )(near, far, *earlier)
    return out[:rows]


def rotary_tables(places):
    half = ROT // 2
    exponent = jnp.arange(0, ROT, 2, dtype=WIDE) / ROT
    frequency = 1.0 / 10000.0**exponent
    angles = frequency[:, None] * places.astype(WIDE)[None, :]
    lane = jnp.arange(BLK) % HD
    picked = ((lane % half)[None, :] == jnp.arange(half)[:, None]) & (lane < ROT)[None, :]
    sign = jnp.where(lane < half, -1.0, 1.0)[None, :]
    spread = partial(
        jnp.einsum, "fn,fl->nl", precision=lax.Precision.HIGHEST, preferred_element_type=WIDE
    )
    cosine = spread(jnp.cos(angles), picked.astype(WIDE)) + (lane >= ROT)[None, :].astype(WIDE)
    return cosine, spread(jnp.sin(angles), picked * sign)


def body(
    tokens,
    cotangent,
    w_qkv,
    w_attn,
    w_up,
    w_down,
    norm_vectors,
    qkv_bias,
    up_bias,
    qkv_moment,
    attn_moment,
    up_moment,
    down_moment,
    norm_moment,
    qbias_moment,
    ubias_moment,
    seq_lengths,
    block_source,
):
    row_count, half = tokens.shape
    fsdp_count = lax.axis_size("fsdp")
    ctx_count = lax.axis_size("ctx")
    tp_index = lax.axis_index("tp")
    fsdp_index = lax.axis_index("fsdp")
    ctx_index = lax.axis_index("ctx")
    low_count = ctx_count // OWNERS
    ctx_low = ctx_index % low_count
    ctx_high = ctx_index // low_count
    width = 2 * half
    own_blocks = row_count // BLK
    pack = ctx_count * row_count
    first_tp = tp_index == 0
    block_row = block_source[0]
    length_row = seq_lengths[0]

    def both_halves(mine, other, dim):
        return jnp.concatenate(
            [jnp.where(first_tp, mine, other), jnp.where(first_tp, other, mine)], axis=dim
        )

    def own_half(array):
        return jnp.where(first_tp, array[:, :half], array[:, half:])

    def far_half(array):
        return jnp.where(first_tp, array[:, half:], array[:, :half])

    own_pair = jnp.concatenate([tokens, cotangent], axis=0)
    far_pair = partner(own_pair, "tp", 1)

    x_near = lax.all_gather(tokens, "ctx", axis=0, tiled=True)
    x_far = partner(x_near, "tp", 1)
    waiting = after(cotangent, x_near)
    g_line = [partner(waiting, "ctx", s * low_count) for s in range(1, OWNERS)]

    def feed_stack(up, down):
        cuts = range(0, up.shape[1], half)
        return jnp.concatenate([up[:, i : i + half] for i in cuts] + [down], axis=0)

    def late_stack(qkv, attn):
        return jnp.concatenate([qkv[:, i] for i in range(3)] + [attn], axis=0)

    low_weights = [w.astype(LOW) for w in (w_up, w_down, w_qkv, w_attn)]
    if fsdp_count == 2:

        def exchanged(stack):
            other = partner(stack, "fsdp", 1)
            first = fsdp_index == 0
            return jnp.where(first, stack, other), jnp.where(first, other, stack)

        feed_stacks = exchanged(feed_stack(*low_weights[:2]))
        late_stacks = exchanged(after(late_stack(*low_weights[2:]), feed_stacks[0]))
    else:
        whole_up, whole_down, whole_qkv, whole_attn = (
            lax.all_gather(w, "fsdp", axis=dim, tiled=True)
            for w, dim in zip(low_weights, (0, 1, 0, 1))
        )
        cuts = (slice(0, half), slice(half, 2 * half))
        feed_stacks = tuple(feed_stack(whole_up[cut], whole_down[:, cut]) for cut in cuts)
        late_stacks = tuple(late_stack(whole_qkv[cut], whole_attn[:, cut]) for cut in cuts)
    hidden_here = up_bias.shape[0]
    attn_halves = tuple(part[3 * half :] for part in late_stacks)

    def by_partners(ctx):
        differs = ctx ^ ctx_index
        return (differs % low_count) * OWNERS + differs // low_count

    slot_blocks = jnp.arange(block_row.shape[0], dtype=jnp.int32)
    slot_ctx, slot_rest = slot_blocks // own_blocks, slot_blocks % own_blocks
    holds = block_row[None, :] == slot_blocks[:, None]

    def located(places):
        return jnp.sum(jnp.where(holds, places[None, :], 0), axis=1).astype(jnp.int32)

    natural = located(slot_blocks)
    by_partner = located(by_partners(slot_ctx) * own_blocks + slot_rest)
    stat_place = located((slot_ctx ^ ctx_index) * own_blocks + slot_rest)
    row_base = (ctx_index * row_count).reshape(1)
    my_blocks = lax.dynamic_slice_in_dim(block_row, ctx_index * own_blocks, own_blocks)

    seq_ends = jnp.cumsum(length_row).astype(jnp.int32)
    seq_starts = seq_ends - length_row

    def bounds(packed):
        inside = (packed[:, None] >= seq_starts[None, :]) & (packed[:, None] < seq_ends[None, :])
        return (
            jnp.sum(jnp.where(inside, seq_starts[None, :], 0), axis=1).astype(jnp.int32),
            jnp.sum(jnp.where(inside, seq_ends[None, :], 0), axis=1).astype(jnp.int32),
        )

    offsets = jnp.arange(BLK, dtype=jnp.int32)
    packed = (block_row[:, None] * BLK + offsets[None, :]).reshape(-1)
    cosine, sine = rotary_tables(packed - bounds(packed)[0])
    my_starts, my_ends = bounds(
        (my_blocks[:, None] * BLK + offsets[None, :]).reshape(-1)
    )
    key_first = bounds(my_blocks * BLK)[0] // CHUNK
    key_last = (my_blocks * BLK + BLK - 1) // CHUNK + 1
    query_first = my_blocks * BLK // CHUNK
    query_last = (bounds(my_blocks * BLK + BLK - 1)[1] + CHUNK - 1) // CHUNK

    def own_first(array, dim):
        left, right = jnp.split(array, 2, axis=dim)
        return jnp.where(first_tp, left, right), jnp.where(first_tp, right, left)

    piece = width // (fsdp_count * ctx_count)

    def my_rows(array, dim):
        return lax.dynamic_slice_in_dim(array, ctx_index * piece, piece, dim)

    def as_rows(up, attn, qkv, down):
        rows = (
            my_rows(up, 0),
            my_rows(attn, 1).T,
            jnp.concatenate([my_rows(qkv, 0)[:, i] for i in range(3)], axis=1),
            my_rows(down, 1).T,
        )
        return jnp.stack([jnp.pad(r, ((0, 0), (0, hidden_here - r.shape[1]))) for r in rows])

    old_moments = as_rows(up_moment, attn_moment, qkv_moment, down_moment)
    old_weights = as_rows(w_up, w_attn, w_qkv, w_down)

    def two_halves(mine, other):
        return jnp.where(first_tp, mine, other), jnp.where(first_tp, other, mine)

    x_halves = [half_x.astype(WIDE) for half_x in two_halves(tokens, far_pair[:row_count])]
    row_mean = sum(jnp.sum(x, axis=1, keepdims=True) for x in x_halves) / width
    centered = [x - row_mean for x in x_halves]
    inv_std = lax.rsqrt(sum(jnp.sum(x * x, axis=1, keepdims=True) for x in centered) / width + 1e-5)
    norm_halves = [
        (x * inv_std * vec[0] + vec[1]).astype(LOW)
        for x, vec in zip(centered, jnp.split(norm_vectors, 2, axis=1))
    ]
    feed_out, feed_dx, grad_up, grad_down, grad_ubias, norm_t, cotangent_t = feed_forward(
        norm_halves,
        two_halves(cotangent, far_pair[row_count:]),
        feed_stacks,
        up_bias.reshape(1, hidden_here),
        (old_moments, old_weights, cosine, sine),
    )
    queries, keys, values = project_rows(
        x_near,
        x_far,
        (*two_halves(*late_stacks), qkv_bias, *own_first(norm_vectors, 1)),
        cosine,
        sine,
    )
    attn_near, attn_far = two_halves(*attn_halves)

    def attention_grads(near, far):
        return (dot_nt(near, attn_near) + dot_nt(far, attn_far)).astype(LOW)

    own_grads = attention_grads(cotangent, far_pair[row_count:])
    g_near = [
        jnp.concatenate([cotangent] + [after(block, queries) for block in g_line], axis=0)
    ]
    for s in range(1, low_count):
        g_near.append(partner(g_near[0], "ctx", s))
    g_far = [partner(part, "tp", 1) for part in g_near]

    def reduced_first(gradient, *earlier):
        rows = gradient.shape[0] // fsdp_count
        pieces = gradient.reshape(fsdp_count, rows, gradient.shape[1])
        return sum_scatter(pieces, "fsdp", 1, fsdp_index, *earlier)

    def reduced_rest(part):
        piece = part.shape[0] // ctx_count
        part = part.reshape(OWNERS, low_count, piece, part.shape[1])
        part = sum_scatter(jnp.swapaxes(part, 0, 1), "ctx", 1, ctx_low)
        return sum_scatter(part, "ctx", low_count, ctx_high)

    grad_outbias = jnp.sum(cotangent.astype(WIDE), axis=0)

    attended, grad_q, stats = query_side(
        my_blocks,
        key_first,
        key_last,
        natural,
        row_base,
        queries,
        keys,
        values,
        own_grads,
        cosine,
        sine,
        my_starts[:, None],
    )
    d_attended = jnp.concatenate(
        [
            attention_grads(after(near, stats), after(far, stats))
            for near, far in zip(g_near, g_far)
        ],
        axis=0,
    )
    first_up, first_down = (reduced_first(grad, stats) for grad in (grad_up, grad_down))
    sum_feed = lax.psum_scatter(
        jnp.concatenate([first_up, first_down], axis=1).astype(LOW),
        "ctx",
        scatter_dimension=0,
        tiled=True,
    ).astype(WIDE)
    sum_up, sum_down = sum_feed[:, :hidden_here], sum_feed[:, hidden_here:]

    early_rows = reduced_first(outer_pair(norm_t, grad_q, cotangent_t, attended))
    all_stats = stats
    step = 1
    while step < ctx_count:
        all_stats = jnp.concatenate([all_stats, partner(all_stats, "ctx", step)], axis=0)
        step *= 2
    grad_k, grad_v = key_side(
        my_blocks,
        query_first,
        query_last,
        natural,
        by_partner,
        stat_place,
        row_base,
        queries,
        keys,
        values,
        d_attended,
        cosine,
        sine,
        my_ends[:, None],
        all_stats,
        (),
    )
    grad_late = outer_pair(norm_t, grad_k, norm_t, grad_v)
    late_rows = reduced_first(grad_late)
    joint_rows = jnp.concatenate([early_rows, late_rows], axis=1)
    sum_joint = reduced_rest(after(joint_rows, sum_feed))
    grad_proj = [after(grad, late_rows) for grad in (grad_q, grad_k, grad_v)]
    grad_qbias = jnp.concatenate([jnp.sum(grad.astype(WIDE), axis=0) for grad in grad_proj])

    def joined(pair):
        return jnp.concatenate(pair, axis=1)

    partial_out = joined([dot_nn(attended, attn) for attn in attn_halves]) + feed_out

    def sum_halves(array):
        return own_half(array) + partner(far_half(array).astype(LOW), "tp", 1).astype(WIDE)

    out_bias = own_half((norm_vectors[2] + norm_vectors[3])[None, :])
    mixed = (tokens.astype(WIDE) + sum_halves(partial_out) + out_bias).astype(LOW)

    grad_norm = sum_halves(
        joined(
            [
                sum(
                    dot_nt(grad, stack[i * half : (i + 1) * half])
                    for i, grad in enumerate(grad_proj)
                )
                for stack in late_stacks
            ]
        )
        + feed_dx
    )
    my_normed = jnp.where(first_tp, *centered) * inv_std
    scaled = grad_norm * own_half(norm_vectors[0:1])
    row_sums = jnp.stack([jnp.sum(scaled, axis=1), jnp.sum(scaled * my_normed, axis=1)])
    row_means = (row_sums + partner(row_sums, "tp", 1)) / width
    grad_tokens = cotangent.astype(WIDE) + inv_std * (
        scaled - row_means[0][:, None] - my_normed * row_means[1][:, None]
    )

    vector_parts = jnp.stack(
        [jnp.sum(grad_norm * my_normed, axis=0), jnp.sum(grad_norm, axis=0), grad_outbias]
    )
    small = jnp.concatenate([vector_parts.reshape(-1), grad_qbias, grad_ubias[0]])
    small = sum_everywhere(small, ("ctx",))
    small = sum_everywhere(after(small, sum_joint), ("fsdp",))
    mine = small[: 3 * half].reshape(3, half)
    vectors = both_halves(mine, partner(mine, "tp", 1), 1)
    sum_vectors = jnp.concatenate([vectors, vectors[2:3]], axis=0)
    sum_qbias = small[3 * half : 6 * half].reshape(3, half)
    sum_ubias = small[6 * half :]

    own_q, own_attn, own_k, own_v = jnp.split(sum_joint, 4, axis=1)
    sums = (sum_up, own_attn, jnp.concatenate([own_q, own_k, own_v], axis=1), sum_down)
    pieces = jnp.stack(
        [
            (
                0.95 * moment + jnp.pad(total, ((0, 0), (0, hidden_here - total.shape[1])))
            ).astype(LOW)
            for moment, total in zip(old_moments, sums)
        ]
    )

    def to_owner(step):
        picked = lax.dynamic_index_in_dim(pieces, ctx_high ^ step, 0, keepdims=False)
        return partner(picked, "ctx", step * low_count) if step else picked

    matrix = jnp.concatenate([to_owner(s) for s in range(OWNERS)], axis=0)
    def all_rows(sums):
        return lax.all_gather(sums, "ctx", axis=0, tiled=True)

    feed_rows = all_rows(after(sum_feed.astype(LOW), matrix))
    joint_all = all_rows(after(sum_joint.astype(LOW), feed_rows)).astype(WIDE)
    all_up, all_down = jnp.split(feed_rows.astype(WIDE), 2, axis=1)
    fresh_up = 0.95 * up_moment + all_up
    fresh_down = 0.95 * down_moment + all_down.T
    all_q, all_attn, all_k, all_v = jnp.split(joint_all, 4, axis=1)
    fresh_qkv = 0.95 * qkv_moment + jnp.stack([all_q, all_k, all_v], axis=1)
    fresh_attn = 0.95 * attn_moment + all_attn.T

    parts = [matrix] + [partner(matrix, "ctx", s) for s in range(1, low_count)]
    for s in range(1, fsdp_count):
        parts += [partner(part, "fsdp", s) for part in parts[:low_count]]
    groups = [
        jnp.concatenate(parts[i : i + low_count], axis=0) for i in range(0, len(parts), low_count)
    ]
    near_cols = jnp.concatenate(groups, axis=0)
    far_cols = jnp.concatenate([partner(group, "tp", 1) for group in groups], axis=0)
    rows_out = orthogonal_rows(near_cols, far_cols, OWNERS * piece, ()).reshape(OWNERS, piece, hidden_here)
    returned = [rows_out[0]] + [
        partner(rows_out[s], "ctx", s * low_count) for s in range(1, OWNERS)
    ]
    returned = jnp.stack([after(part, fresh_up, fresh_down) for part in returned])
    full_hidden = hidden_here * 2
    rates = (
        0.5 * math.sqrt(full_hidden / width),
        0.5 * math.sqrt(width / (width // HD)),
        0.5 * math.sqrt(3 * width / width),
        0.5 * math.sqrt(full_hidden / full_hidden),
    )
    new_up, new_attn, new_qkv, new_down = (
        old_weights[m]
        - rate * lax.dynamic_index_in_dim(returned, ctx_high ^ m, 0, keepdims=False).astype(WIDE)
        for m, rate in enumerate(rates)
    )
    new_attn, new_qkv = new_attn[:, :half], new_qkv[:, : 3 * half]

    vector_rate = 0.3 / math.sqrt(row_count * fsdp_count * ctx_count)
    mom_norm = 0.9 * norm_moment + sum_vectors
    mom_qbias = 0.9 * qbias_moment + sum_qbias
    mom_ubias = 0.9 * ubias_moment + sum_ubias
    return (
        mixed,
        grad_tokens,
        fresh_qkv,
        jnp.stack(jnp.split(new_qkv, 3, axis=1), axis=1),
        fresh_attn,
        new_attn.T,
        fresh_up,
        new_up,
        fresh_down,
        new_down.T,
        mom_norm,
        norm_vectors - vector_rate * mom_norm,
        mom_qbias,
        qkv_bias - vector_rate * mom_qbias,
        mom_ubias,
        up_bias - vector_rate * mom_ubias,
    )


def solution(mesh):
    return jax.shard_map(
        body,
        mesh=mesh,
        in_specs=(
            P(("fsdp", "ctx"), "tp"),
            P(("fsdp", "ctx"), "tp"),
            P("fsdp", None, "tp"),
            P("tp", "fsdp"),
            P("fsdp", "tp"),
            P("tp", "fsdp"),
            P(),
            P(None, "tp"),
            P("tp"),
            P("fsdp", None, "tp"),
            P("tp", "fsdp"),
            P("fsdp", "tp"),
            P("tp", "fsdp"),
            P(),
            P(None, "tp"),
            P("tp"),
            P("fsdp", None),
            P("fsdp", None),
        ),
        out_specs=(
            P(("fsdp", "ctx"), "tp"),
            P(("fsdp", "ctx"), "tp"),
            P("fsdp", None, "tp"),
            P(("fsdp", "ctx"), None, "tp"),
            P("tp", "fsdp"),
            P("tp", ("fsdp", "ctx")),
            P("fsdp", "tp"),
            P(("fsdp", "ctx"), "tp"),
            P("tp", "fsdp"),
            P("tp", ("fsdp", "ctx")),
            P(),
            P(),
            P(None, "tp"),
            P(None, "tp"),
            P("tp"),
            P("tp"),
        ),
        check_vma=False,
    )
```

```python
from functools import partial
import math

import jax
import jax.numpy as jnp
from jax import lax
from jax.experimental import pallas as pl
from jax.experimental.pallas import tpu as pltpu
from jax.sharding import PartitionSpec as P

HD = 64
ROT = 16
BLK = 128
NS_STEPS = 5
CHUNK = 512
MAX_LEN = 2048
SPAN = (MAX_LEN + BLK) // CHUNK + 2
OWNERS = 4
NS_COEF = (3.4445, -4.775, 2.0315)
NEG_BIG = -1e30
SCALE = HD**-0.5
LOW = jnp.bfloat16
WIDE = jnp.float32
NT = (((1,), (1,)), ((), ()))
VMEM_ASK = 56 * 1024 * 1024


def dot_nn(left, right):
    return jnp.dot(left, right, preferred_element_type=WIDE)


def dot_nt(left, right):
    return lax.dot_general(left, right, NT, preferred_element_type=WIDE)


def partner(value, axis, step):
    size = lax.axis_size(axis)
    return lax.ppermute(value, axis, [(i, i ^ step) for i in range(size)])


def sum_scatter(pieces, axis, stride, index, *earlier):
    count = pieces.shape[0]
    total = lax.dynamic_index_in_dim(pieces, index, 0, keepdims=False)
    total = after(total, *earlier).astype(WIDE)
    for step in range(1, count):
        piece = lax.dynamic_index_in_dim(pieces, index ^ step, 0, keepdims=False)
        total = total + partner(piece.astype(LOW), axis, step * stride).astype(WIDE)
    return total


def after(value, *earlier):
    return lax.optimization_barrier((value, *earlier))[0]


def sum_everywhere(value, axes):
    for axis in axes:
        step = 1
        while step < lax.axis_size(axis):
            value = value + partner(value, axis, step)
            step *= 2
    return value


def turned(block, cosine, sine, lane):
    half = ROT // 2
    swapped = jnp.where(
        lane % HD < half, pltpu.roll(block, BLK - half, 1), pltpu.roll(block, half, 1)
    )
    return block * cosine + swapped * sine


def two_heads(block, lane):
    zero = jnp.zeros_like(block)
    return jnp.concatenate(
        [jnp.where(lane < HD, block, zero), jnp.where(lane < HD, zero, block)], axis=0
    )


def one_of_two(stacked, lane):
    return jnp.where(lane < HD, stacked[:BLK], stacked[BLK:])


def project_kernel(
    near, far, w_near, w_far, bias, vec_near, vec_far, cos_ref, sin_ref, *outs
):
    rows, half = outs[0].shape
    width = 2 * half
    own, other = near[...].astype(WIDE), far[...].astype(WIDE)
    mean = (
        jnp.sum(own, axis=1, keepdims=True) + jnp.sum(other, axis=1, keepdims=True)
    ) / width
    own, other = own - mean, other - mean
    var = (
        jnp.sum(own * own, axis=1, keepdims=True) + jnp.sum(other * other, axis=1, keepdims=True)
    ) / width
    inv_std = lax.rsqrt(var + 1e-5)
    own = (own * inv_std * vec_near[0:1] + vec_near[1:2]).astype(LOW)
    other = (other * inv_std * vec_far[0:1] + vec_far[1:2]).astype(LOW)
    lane = lax.broadcasted_iota(jnp.int32, (rows, BLK), 1)
    cosine, sine = cos_ref[...], sin_ref[...]
    for part, out in enumerate(outs):
        span = slice(part * half, (part + 1) * half)
        made = dot_nn(own, w_near[span]) + dot_nn(other, w_far[span]) + bias[part : part + 1]
        for pair in range(half // BLK):
            lanes = slice(pair * BLK, (pair + 1) * BLK)
            block = made[:, lanes]
            if part < 2:
                block = turned(block, cosine, sine, lane)
            out[:, lanes] = block.astype(LOW)


def project_rows(near, far, weights, cosine, sine):
    rows, half = near.shape

    def fixed(array):
        return pl.BlockSpec(array.shape, lambda i: (0,) * array.ndim)

    def chunk(width):
        return pl.BlockSpec((CHUNK, width), lambda i: (i, 0))

    return pl.pallas_call(
        project_kernel,
        grid=(rows // CHUNK,),
        in_specs=[chunk(half)] * 2 + [fixed(w) for w in weights] + [chunk(BLK)] * 2,
        out_specs=[chunk(half)] * 3,
        out_shape=[jax.ShapeDtypeStruct((rows, half), LOW)] * 3,
        compiler_params=pltpu.CompilerParams(vmem_limit_bytes=VMEM_ASK),
        cost_estimate=pl.CostEstimate(
            flops=44 * rows * half * half, bytes_accessed=14 * rows * half, transcendentals=0
        ),
        name="project_rows",
    )(near, far, *weights, cosine, sine)


def feed_kernel(
    xa_ref,
    xb_ref,
    ga_ref,
    gb_ref,
    up_a,
    up_b,
    down_a,
    down_b,
    bias_ref,
    *refs,
):
    out_ref, dx_ref, dup_ref, ddown_ref, dbias_ref, xt_ref, gt_ref = refs[-7:]
    half = xa_ref.shape[1]
    first, second = slice(0, half), slice(half, 2 * half)

    @pl.when(pl.program_id(0) == 0)
    def _():
        xt_ref[first] = xa_ref[...].T
        xt_ref[second] = xb_ref[...].T
        gt_ref[first] = ga_ref[...].T
        gt_ref[second] = gb_ref[...].T
        out_ref[...] = jnp.zeros(out_ref.shape, WIDE)
        dx_ref[...] = jnp.zeros(dx_ref.shape, WIDE)

    hidden = dot_nn(xa_ref[...], up_a[...]) + dot_nn(xb_ref[...], up_b[...]) + bias_ref[...]
    grad = dot_nt(ga_ref[...], down_a[...]) + dot_nt(gb_ref[...], down_b[...])
    below = 0.5 + 0.5 * lax.erf(hidden * math.sqrt(0.5))
    density = jnp.exp(-0.5 * hidden * hidden) * (1.0 / math.sqrt(2.0 * math.pi))
    active = (hidden * below).astype(LOW)
    grad = (grad * (below + hidden * density)).astype(LOW)
    dbias_ref[...] = jnp.sum(grad.astype(WIDE), axis=0, keepdims=True)
    out_ref[:, first] += dot_nn(active, down_a[...])
    out_ref[:, second] += dot_nn(active, down_b[...])
    dx_ref[:, first] += dot_nt(grad, up_a[...])
    dx_ref[:, second] += dot_nt(grad, up_b[...])
    dup_ref[...] = dot_nn(xt_ref[...], grad).astype(LOW)
    ddown_ref[...] = dot_nn(gt_ref[...], active).astype(LOW)


def feed_forward(x_halves, g_halves, stacks, bias, earlier):
    rows, half = x_halves[0].shape
    width = 2 * half
    hidden = bias.shape[1]
    steps = hidden // half

    def whole(shape):
        return pl.BlockSpec(shape, lambda i: (0, 0))

    up = pl.BlockSpec((half, half), lambda i: (i, 0))
    down = pl.BlockSpec((half, half), lambda i: (i + steps, 0))
    column = pl.BlockSpec((width, half), lambda i: (0, i))
    line = pl.BlockSpec((1, half), lambda i: (0, i))
    return pl.pallas_call(
        feed_kernel,
        grid=(steps,),
        in_specs=[whole((rows, half))] * 4
        + [up, up, down, down, line]
        + [pl.BlockSpec(memory_space=pl.ANY)] * len(earlier),
        out_specs=[
            whole((rows, width)),
            whole((rows, width)),
            column,
            column,
            line,
            whole((width, rows)),
            whole((width, rows)),
        ],
        out_shape=[
            jax.ShapeDtypeStruct((rows, width), WIDE),
            jax.ShapeDtypeStruct((rows, width), WIDE),
            jax.ShapeDtypeStruct((width, hidden), LOW),
            jax.ShapeDtypeStruct((width, hidden), LOW),
            jax.ShapeDtypeStruct((1, hidden), WIDE),
            jax.ShapeDtypeStruct((width, rows), LOW),
            jax.ShapeDtypeStruct((width, rows), LOW),
        ],
        compiler_params=pltpu.CompilerParams(vmem_limit_bytes=VMEM_ASK),
        cost_estimate=pl.CostEstimate(
            flops=26 * rows * width * hidden, bytes_accessed=12 * width * hidden, transcendentals=0
        ),
        name="feed_forward",
    )(*x_halves, *g_halves, *stacks, *stacks, bias, *earlier)


def outer_kernel(left_a, right_a, left_b, right_b, out_ref):
    half = right_a.shape[1]
    out_ref[:, :half] = dot_nn(left_a[...], right_a[...]).astype(LOW)
    out_ref[:, half:] = dot_nn(left_b[...], right_b[...]).astype(LOW)


def outer_pair(left_a, right_a, left_b, right_b):
    rows, depth = left_a.shape
    half = right_a.shape[1]
    return pl.pallas_call(
        outer_kernel,
        in_specs=[vmem()] * 4,
        out_specs=vmem(),
        out_shape=jax.ShapeDtypeStruct((rows, 2 * half), LOW),
        compiler_params=pltpu.CompilerParams(vmem_limit_bytes=VMEM_ASK),
        cost_estimate=pl.CostEstimate(
            flops=8 * rows * depth * half, bytes_accessed=6 * rows * depth, transcendentals=0
        ),
        name="outer_pair",
    )(left_a, right_a, left_b, right_b)


def lane_tiles(array, combine):
    total = array[:, :BLK]
    for i in range(1, array.shape[1] // BLK):
        total = combine(total, array[:, i * BLK : (i + 1) * BLK])
    return total


def gathered_blocks(ref, inverse, chunk, lanes):
    count = CHUNK // BLK
    return jnp.concatenate(
        [
            ref[pl.ds(pl.multiple_of(inverse[chunk * count + i] * BLK, BLK), BLK), lanes]
            for i in range(count)
        ],
        axis=0,
    )


def query_kernel(
    blocks,
    first,
    last,
    natural,
    base,
    q_ref,
    k_ref,
    v_ref,
    d_ref,
    cos_ref,
    sin_ref,
    start_ref,
    att_out,
    dq_out,
    stat_out,
    s_scr,
    p_scr,
    q_scr,
    d_scr,
    m_scr,
    l_scr,
    e_scr,
    o_scr,
):
    pairs = q_ref.shape[1] // BLK
    own = att_out.shape[0] // BLK
    lane = lax.broadcasted_iota(jnp.int32, (BLK, BLK), 1)

    def lanes(pair):
        return slice(pair * BLK, (pair + 1) * BLK)

    @pl.loop(0, own)
    def _(j):
        row0 = pl.multiple_of(blocks[j] * BLK, BLK)
        out0 = pl.multiple_of(j * BLK, BLK)
        here = pl.multiple_of(base[0] + out0, BLK)
        lo = first[j]
        hi = last[j]
        for g in range(pairs):
            q_scr[g] = two_heads(q_ref[pl.ds(here, BLK), lanes(g)].astype(WIDE), lane).astype(
                LOW
            ) * LOW(SCALE)
            d_scr[g] = two_heads(d_ref[pl.ds(out0, BLK), lanes(g)].astype(WIDE), lane).astype(LOW)
        m_scr[...] = jnp.full(m_scr.shape, NEG_BIG, WIDE)
        l_scr[...] = jnp.zeros(l_scr.shape, WIDE)
        e_scr[...] = jnp.zeros(e_scr.shape, WIDE)
        o_scr[...] = jnp.zeros(o_scr.shape, WIDE)
        starts = start_ref[pl.ds(out0, BLK), :]
        places = row0 + lax.broadcasted_iota(jnp.int32, (BLK, 1), 0)
        starts = jnp.concatenate([starts, starts], axis=0)
        places = jnp.concatenate([places, places], axis=0)

        @pl.loop(lo, hi)
        def _(c):
            key0 = pl.multiple_of(c * CHUNK, CHUNK)
            key_place = key0 + lax.broadcasted_iota(jnp.int32, (2 * BLK, CHUNK), 1)
            allowed = (key_place >= starts) & (key_place <= places)
            for g in range(pairs):
                scores = dot_nt(q_scr[g], gathered_blocks(k_ref, natural, c, lanes(g)))
                scores = jnp.where(allowed, scores, NEG_BIG)
                s_scr[g, c - lo] = scores
                m_scr[g] = jnp.maximum(m_scr[g], lane_tiles(scores, jnp.maximum))

        for g in range(pairs):
            m_scr[g] = jnp.broadcast_to(
                jnp.max(m_scr[g], axis=1, keepdims=True), (2 * BLK, BLK)
            )

        @pl.loop(lo, hi)
        def _(c):
            for g in range(pairs):
                values = gathered_blocks(v_ref, natural, c, lanes(g))
                top = m_scr[g]
                weights = jnp.exp(s_scr[g, c - lo] - jnp.concatenate([top] * (CHUNK // BLK), 1))
                l_scr[g] += lane_tiles(weights, jnp.add)
                o_scr[g] += dot_nn(weights.astype(LOW), values)
                grad_prob = dot_nt(d_scr[g], values)
                e_scr[g] += lane_tiles(weights * grad_prob, jnp.add)
                s_scr[g, c - lo] = weights
                p_scr[g, c - lo] = grad_prob

        for g in range(pairs):
            total = jnp.sum(l_scr[g], axis=1, keepdims=True)
            share = 1.0 / total
            delta = jnp.sum(e_scr[g], axis=1, keepdims=True) * share
            att_out[pl.ds(out0, BLK), lanes(g)] = one_of_two(o_scr[g] * share, lane).astype(LOW)
            log_sum = m_scr[g] + jnp.log(total)
            stat_out[j, 2 * g : 2 * g + 1, :] = log_sum[:BLK].T[0:1]
            stat_out[j, 2 * g + 1 : 2 * g + 2, :] = log_sum[BLK:].T[0:1]
            wide = jnp.broadcast_to(delta, (2 * BLK, BLK))
            line = stat_out.shape[1] // 2 + 2 * g
            stat_out[j, line : line + 1, :] = wide[:BLK].T[0:1]
            stat_out[j, line + 1 : line + 2, :] = wide[BLK:].T[0:1]
            l_scr[g] = jnp.broadcast_to(share, (2 * BLK, BLK))
            e_scr[g] = wide
        o_scr[...] = jnp.zeros(o_scr.shape, WIDE)

        @pl.loop(lo, hi)
        def _(c):
            for g in range(pairs):
                wide = jnp.concatenate([e_scr[g]] * (CHUNK // BLK), 1)
                grad_score = s_scr[g, c - lo] * (p_scr[g, c - lo] - wide)
                o_scr[g] += dot_nn(
                    grad_score.astype(LOW), gathered_blocks(k_ref, natural, c, lanes(g))
                )

        cosine = cos_ref[pl.ds(here, BLK), :]
        sine = sin_ref[pl.ds(here, BLK), :]
        for g in range(pairs):
            grad = one_of_two(o_scr[g] * l_scr[g], lane) * SCALE
            dq_out[pl.ds(out0, BLK), lanes(g)] = turned(grad, cosine, -sine, lane).astype(LOW)


def smem():
    return pl.BlockSpec(memory_space=pltpu.SMEM)


def vmem():
    return pl.BlockSpec(memory_space=pltpu.VMEM)


def query_side(blocks, first, last, natural, base, queries, keys, values, grads, cosine, sine, starts):
    own = blocks.shape[0]
    width = queries.shape[1]
    pairs = width // BLK
    stat_rows = 16 * ((2 * pairs + 7) // 8)
    work = 2 * BLK * CHUNK
    return pl.pallas_call(
        query_kernel,
        in_specs=[smem()] * 5 + [vmem()] * 7,
        out_specs=[vmem()] * 3,
        out_shape=[
            jax.ShapeDtypeStruct((own * BLK, width), LOW),
            jax.ShapeDtypeStruct((own * BLK, width), LOW),
            jax.ShapeDtypeStruct((own, stat_rows, BLK), WIDE),
        ],
        scratch_shapes=[
            pltpu.VMEM((pairs, SPAN, 2 * BLK, CHUNK), WIDE),
            pltpu.VMEM((pairs, SPAN, 2 * BLK, CHUNK), WIDE),
            pltpu.VMEM((pairs, 2 * BLK, BLK), LOW),
            pltpu.VMEM((pairs, 2 * BLK, BLK), LOW),
            pltpu.VMEM((pairs, 2 * BLK, BLK), WIDE),
            pltpu.VMEM((pairs, 2 * BLK, BLK), WIDE),
            pltpu.VMEM((pairs, 2 * BLK, BLK), WIDE),
            pltpu.VMEM((pairs, 2 * BLK, BLK), WIDE),
        ],
        compiler_params=pltpu.CompilerParams(vmem_limit_bytes=VMEM_ASK),
        cost_estimate=pl.CostEstimate(
            flops=own * pairs * 12 * 4 * 2 * work * BLK,
            bytes_accessed=4 * keys.shape[0] * width * 2,
            transcendentals=own * pairs * 4 * work,
        ),
        name="query_side",
    )(blocks, first, last, natural, base, queries, keys, values, grads, cosine, sine, starts)


def key_kernel(
    blocks,
    first,
    last,
    natural,
    by_partner,
    stat_place,
    base,
    q_ref,
    k_ref,
    v_ref,
    d_ref,
    cos_ref,
    sin_ref,
    end_ref,
    stat_ref,
    *rest,
):
    dk_out, dv_out, k_scr, v_scr, dk_scr, dv_scr = rest[-6:]
    pairs = q_ref.shape[1] // BLK
    own = dk_out.shape[0] // BLK
    half_stat = stat_ref.shape[1] // 2
    lane = lax.broadcasted_iota(jnp.int32, (BLK, BLK), 1)

    def lanes(pair):
        return slice(pair * BLK, (pair + 1) * BLK)

    @pl.loop(0, own)
    def _(j):
        row0 = pl.multiple_of(blocks[j] * BLK, BLK)
        out0 = pl.multiple_of(j * BLK, BLK)
        here = pl.multiple_of(base[0] + out0, BLK)
        for g in range(pairs):
            k_scr[g] = two_heads(k_ref[pl.ds(here, BLK), lanes(g)].astype(WIDE), lane).astype(
                LOW
            ) * LOW(SCALE)
            v_scr[g] = two_heads(v_ref[pl.ds(here, BLK), lanes(g)].astype(WIDE), lane).astype(LOW)
        dk_scr[...] = jnp.zeros(dk_scr.shape, WIDE)
        dv_scr[...] = jnp.zeros(dv_scr.shape, WIDE)
        ends = end_ref[pl.ds(out0, BLK), :]
        places = row0 + lax.broadcasted_iota(jnp.int32, (BLK, 1), 0)

        @pl.loop(first[j], last[j])
        def _(c):
            query0 = pl.multiple_of(c * CHUNK, CHUNK)
            query_place = query0 + lax.broadcasted_iota(jnp.int32, (BLK, CHUNK), 1)
            allowed = (query_place >= places) & (query_place < ends)
            count = CHUNK // BLK
            slots = [stat_place[c * count + i] for i in range(count)]

            def stat(row):
                return jnp.concatenate([stat_ref[slot, row : row + 1, :] for slot in slots], 1)

            for g in range(pairs):
                queries = gathered_blocks(q_ref, natural, c, lanes(g))
                grads = gathered_blocks(d_ref, by_partner, c, lanes(g))
                scores = dot_nt(k_scr[g], queries)
                grad_prob = dot_nt(v_scr[g], grads)
                probs, grad_scores = [], []
                for h in range(2):
                    rows = slice(h * BLK, (h + 1) * BLK)
                    shifted = jnp.where(allowed, scores[rows] - stat(2 * g + h), NEG_BIG)
                    prob = jnp.exp(shifted)
                    probs.append(prob.astype(LOW))
                    grad_scores.append(
                        (prob * (grad_prob[rows] - stat(half_stat + 2 * g + h))).astype(LOW)
                    )
                dv_scr[g] += dot_nn(jnp.concatenate(probs, 0), grads)
                dk_scr[g] += dot_nn(jnp.concatenate(grad_scores, 0), queries)

        cosine = cos_ref[pl.ds(here, BLK), :]
        sine = sin_ref[pl.ds(here, BLK), :]
        for g in range(pairs):
            grad = one_of_two(dk_scr[g], lane) * SCALE
            dk_out[pl.ds(out0, BLK), lanes(g)] = turned(grad, cosine, -sine, lane).astype(LOW)
            dv_out[pl.ds(out0, BLK), lanes(g)] = one_of_two(dv_scr[g], lane).astype(LOW)


def key_side(
    blocks,
    first,
    last,
    natural,
    by_partner,
    stat_place,
    base,
    queries,
    keys,
    values,
    grads,
    cosine,
    sine,
    ends,
    stats,
    after,
):
    own = blocks.shape[0]
    width = queries.shape[1]
    pairs = width // BLK
    work = 2 * BLK * CHUNK
    return pl.pallas_call(
        key_kernel,
        in_specs=[smem()] * 7 + [vmem()] * 8 + [pl.BlockSpec(memory_space=pl.ANY)] * len(after),
        out_specs=[vmem()] * 2,
        out_shape=[jax.ShapeDtypeStruct((own * BLK, width), LOW)] * 2,
        scratch_shapes=[
            pltpu.VMEM((pairs, 2 * BLK, BLK), LOW),
            pltpu.VMEM((pairs, 2 * BLK, BLK), LOW),
            pltpu.VMEM((pairs, 2 * BLK, BLK), WIDE),
            pltpu.VMEM((pairs, 2 * BLK, BLK), WIDE),
        ],
        compiler_params=pltpu.CompilerParams(vmem_limit_bytes=VMEM_ASK),
        cost_estimate=pl.CostEstimate(
            flops=own * pairs * 12 * 4 * 2 * work * BLK,
            bytes_accessed=4 * keys.shape[0] * width * 2,
            transcendentals=own * pairs * 4 * work,
        ),
        name="key_side",
    )(
        blocks,
        first,
        last,
        natural,
        by_partner,
        stat_place,
        base,
        queries,
        keys,
        values,
        grads,
        cosine,
        sine,
        ends,
        stats,
        *after,
    )


TILE = 256


def symmetric_product(out_ref, left, right):
    size = out_ref.shape[0]
    for i in range(0, size, TILE):
        out_ref[i : i + TILE, i:] = dot_nt(left[i : i + TILE, :], right[i:, :])
    for i in range(0, size, TILE):
        for j in range(i + TILE, size, TILE):
            out_ref[j : j + TILE, i : i + TILE] = out_ref[i : i + TILE, j : j + TILE].T


def ns_kernel(near_ref, far_ref, *refs):
    out_ref, wide_scr, low_scr, gram_scr, poly_scr = refs[-5:]
    size, half = near_ref.shape
    span = 2 * half
    step = 768
    cuts = [slice(i, i + step) for i in range(0, span, step)]
    total = jnp.zeros((1, 1), WIDE)
    for source, base in ((near_ref, 0), (far_ref, half)):
        for i in range(0, half, step):
            part = source[:, i : i + step].astype(WIDE)
            wide_scr[:, base + i : base + i + step] = part
            total = total + jnp.sum(part * part)
    factor = 1.0 / (jnp.sqrt(total) + 1e-7)
    for cut in cuts:
        part = wide_scr[:, cut] * factor
        wide_scr[:, cut] = part
        low_scr[:, cut] = part.astype(LOW)

    def polynomial():
        symmetric_product(gram_scr, low_scr, low_scr)
        poly_scr[...] = gram_scr[...].astype(LOW)
        first = gram_scr[...] * NS_COEF[1]
        symmetric_product(gram_scr, poly_scr, poly_scr)
        poly_scr[...] = (first + NS_COEF[2] * gram_scr[...]).astype(LOW)

    @pl.loop(0, NS_STEPS - 1)
    def _(_):
        polynomial()
        for cut in cuts:
            part = NS_COEF[0] * wide_scr[:, cut] + dot_nn(poly_scr[...], low_scr[:, cut])
            wide_scr[:, cut] = part
            low_scr[:, cut] = part.astype(LOW)

    polynomial()
    rows = out_ref.shape[0]
    for i in range(0, half, step):
        cut = slice(i, i + step)
        out_ref[:, cut] = (
            NS_COEF[0] * wide_scr[:rows, cut] + dot_nn(poly_scr[:rows, :], low_scr[:, cut])
        ).astype(LOW)


def orthogonal_rows(near, far, rows, earlier):
    size, half = near.shape
    kept = rows if rows % 16 == 0 else size
    out = pl.pallas_call(
        ns_kernel,
        in_specs=[vmem()] * 2 + [pl.BlockSpec(memory_space=pl.ANY)] * len(earlier),
        out_specs=vmem(),
        out_shape=jax.ShapeDtypeStruct((kept, half), LOW),
        scratch_shapes=[
            pltpu.VMEM((size, 2 * half), WIDE),
            pltpu.VMEM((size, 2 * half), LOW),
            pltpu.VMEM((size, size), WIDE),
            pltpu.VMEM((size, size), LOW),
        ],
        compiler_params=pltpu.CompilerParams(vmem_limit_bytes=VMEM_ASK),
        cost_estimate=pl.CostEstimate(
            flops=NS_STEPS * 10 * size * size * half,
            bytes_accessed=4 * size * half,
            transcendentals=0,
        ),
        name="orthogonal_rows",
    )(near, far, *earlier)
    return out[:rows]


def rotary_tables(places):
    half = ROT // 2
    exponent = jnp.arange(0, ROT, 2, dtype=WIDE) / ROT
    frequency = 1.0 / 10000.0**exponent
    angles = frequency[:, None] * places.astype(WIDE)[None, :]
    lane = jnp.arange(BLK) % HD
    picked = ((lane % half)[None, :] == jnp.arange(half)[:, None]) & (lane < ROT)[None, :]
    sign = jnp.where(lane < half, -1.0, 1.0)[None, :]
    spread = partial(
        jnp.einsum, "fn,fl->nl", precision=lax.Precision.HIGHEST, preferred_element_type=WIDE
    )
    cosine = spread(jnp.cos(angles), picked.astype(WIDE)) + (lane >= ROT)[None, :].astype(WIDE)
    return cosine, spread(jnp.sin(angles), picked * sign)


def body(
    tokens,
    cotangent,
    w_qkv,
    w_attn,
    w_up,
    w_down,
    norm_vectors,
    qkv_bias,
    up_bias,
    qkv_moment,
    attn_moment,
    up_moment,
    down_moment,
    norm_moment,
    qbias_moment,
    ubias_moment,
    seq_lengths,
    block_source,
):
    row_count, half = tokens.shape
    fsdp_count = lax.axis_size("fsdp")
    ctx_count = lax.axis_size("ctx")
    tp_index = lax.axis_index("tp")
    fsdp_index = lax.axis_index("fsdp")
    ctx_index = lax.axis_index("ctx")
    low_count = ctx_count // OWNERS
    ctx_low = ctx_index % low_count
    ctx_high = ctx_index // low_count
    width = 2 * half
    own_blocks = row_count // BLK
    pack = ctx_count * row_count
    first_tp = tp_index == 0
    block_row = block_source[0]
    length_row = seq_lengths[0]

    def both_halves(mine, other, dim):
        return jnp.concatenate(
            [jnp.where(first_tp, mine, other), jnp.where(first_tp, other, mine)], axis=dim
        )

    def own_half(array):
        return jnp.where(first_tp, array[:, :half], array[:, half:])

    def far_half(array):
        return jnp.where(first_tp, array[:, half:], array[:, :half])

    own_pair = jnp.concatenate([tokens, cotangent], axis=0)
    far_pair = partner(own_pair, "tp", 1)

    x_near = lax.all_gather(tokens, "ctx", axis=0, tiled=True)
    x_far = partner(x_near, "tp", 1)
    g_line = [partner(cotangent, "ctx", s * low_count) for s in range(1, OWNERS)]

    def feed_stack(up, down):
        cuts = range(0, up.shape[1], half)
        return jnp.concatenate([up[:, i : i + half] for i in cuts] + [down], axis=0)

    def late_stack(qkv, attn):
        return jnp.concatenate([qkv[:, i] for i in range(3)] + [attn], axis=0)

    low_weights = [w.astype(LOW) for w in (w_up, w_down, w_qkv, w_attn)]
    if fsdp_count == 2:

        def exchanged(stack):
            other = partner(stack, "fsdp", 1)
            first = fsdp_index == 0
            return jnp.where(first, stack, other), jnp.where(first, other, stack)

        feed_stacks = exchanged(feed_stack(*low_weights[:2]))
        late_stacks = exchanged(late_stack(*low_weights[2:]))
    else:
        whole_up, whole_down, whole_qkv, whole_attn = (
            lax.all_gather(w, "fsdp", axis=dim, tiled=True)
            for w, dim in zip(low_weights, (0, 1, 0, 1))
        )
        cuts = (slice(0, half), slice(half, 2 * half))
        feed_stacks = tuple(feed_stack(whole_up[cut], whole_down[:, cut]) for cut in cuts)
        late_stacks = tuple(late_stack(whole_qkv[cut], whole_attn[:, cut]) for cut in cuts)
    hidden_here = up_bias.shape[0]
    attn_halves = tuple(part[3 * half :] for part in late_stacks)

    def by_partners(ctx):
        differs = ctx ^ ctx_index
        return (differs % low_count) * OWNERS + differs // low_count

    slot_blocks = jnp.arange(block_row.shape[0], dtype=jnp.int32)
    slot_ctx, slot_rest = slot_blocks // own_blocks, slot_blocks % own_blocks
    holds = block_row[None, :] == slot_blocks[:, None]

    def located(places):
        return jnp.sum(jnp.where(holds, places[None, :], 0), axis=1).astype(jnp.int32)

    natural = located(slot_blocks)
    by_partner = located(by_partners(slot_ctx) * own_blocks + slot_rest)
    stat_place = located((slot_ctx ^ ctx_index) * own_blocks + slot_rest)
    row_base = (ctx_index * row_count).reshape(1)
    my_blocks = lax.dynamic_slice_in_dim(block_row, ctx_index * own_blocks, own_blocks)

    seq_ends = jnp.cumsum(length_row).astype(jnp.int32)
    seq_starts = seq_ends - length_row

    def bounds(packed):
        inside = (packed[:, None] >= seq_starts[None, :]) & (packed[:, None] < seq_ends[None, :])
        return (
            jnp.sum(jnp.where(inside, seq_starts[None, :], 0), axis=1).astype(jnp.int32),
            jnp.sum(jnp.where(inside, seq_ends[None, :], 0), axis=1).astype(jnp.int32),
        )

    offsets = jnp.arange(BLK, dtype=jnp.int32)
    packed = (block_row[:, None] * BLK + offsets[None, :]).reshape(-1)
    cosine, sine = rotary_tables(packed - bounds(packed)[0])
    my_starts, my_ends = bounds(
        (my_blocks[:, None] * BLK + offsets[None, :]).reshape(-1)
    )
    key_first = bounds(my_blocks * BLK)[0] // CHUNK
    key_last = (my_blocks * BLK + BLK - 1) // CHUNK + 1
    query_first = my_blocks * BLK // CHUNK
    query_last = (bounds(my_blocks * BLK + BLK - 1)[1] + CHUNK - 1) // CHUNK

    def own_first(array, dim):
        left, right = jnp.split(array, 2, axis=dim)
        return jnp.where(first_tp, left, right), jnp.where(first_tp, right, left)

    piece = width // (fsdp_count * ctx_count)

    def my_rows(array, dim):
        return lax.dynamic_slice_in_dim(array, ctx_index * piece, piece, dim)

    def as_rows(up, attn, qkv, down):
        rows = (
            my_rows(up, 0),
            my_rows(attn, 1).T,
            jnp.concatenate([my_rows(qkv, 0)[:, i] for i in range(3)], axis=1),
            my_rows(down, 1).T,
        )
        return jnp.stack([jnp.pad(r, ((0, 0), (0, hidden_here - r.shape[1]))) for r in rows])

    old_moments = as_rows(up_moment, attn_moment, qkv_moment, down_moment)
    old_weights = as_rows(w_up, w_attn, w_qkv, w_down)

    def two_halves(mine, other):
        return jnp.where(first_tp, mine, other), jnp.where(first_tp, other, mine)

    x_halves = [half_x.astype(WIDE) for half_x in two_halves(tokens, far_pair[:row_count])]
    row_mean = sum(jnp.sum(x, axis=1, keepdims=True) for x in x_halves) / width
    centered = [x - row_mean for x in x_halves]
    inv_std = lax.rsqrt(sum(jnp.sum(x * x, axis=1, keepdims=True) for x in centered) / width + 1e-5)
    norm_halves = [
        (x * inv_std * vec[0] + vec[1]).astype(LOW)
        for x, vec in zip(centered, jnp.split(norm_vectors, 2, axis=1))
    ]
    feed_out, feed_dx, grad_up, grad_down, grad_ubias, norm_t, cotangent_t = feed_forward(
        norm_halves,
        two_halves(cotangent, far_pair[row_count:]),
        feed_stacks,
        up_bias.reshape(1, hidden_here),
        (old_moments, old_weights, cosine, sine),
    )
    queries, keys, values = project_rows(
        x_near,
        x_far,
        (*two_halves(*late_stacks), qkv_bias, *own_first(norm_vectors, 1)),
        cosine,
        sine,
    )
    attn_near, attn_far = two_halves(*attn_halves)

    def attention_grads(near, far):
        return (dot_nt(near, attn_near) + dot_nt(far, attn_far)).astype(LOW)

    own_grads = attention_grads(cotangent, far_pair[row_count:])
    g_near = [
        jnp.concatenate([cotangent] + [after(block, x_near) for block in g_line], axis=0)
    ]
    for s in range(1, low_count):
        g_near.append(partner(g_near[0], "ctx", s))
    g_far = [partner(part, "tp", 1) for part in g_near]

    def reduced_first(gradient, *earlier):
        rows = gradient.shape[0] // fsdp_count
        pieces = gradient.reshape(fsdp_count, rows, gradient.shape[1])
        return sum_scatter(pieces, "fsdp", 1, fsdp_index, *earlier)

    def scatter_low(part):
        piece = part.shape[0] // ctx_count
        part = part.reshape(OWNERS, low_count, piece, part.shape[1])
        return sum_scatter(jnp.swapaxes(part, 0, 1), "ctx", 1, ctx_low)

    def scatter_high(part):
        return sum_scatter(part, "ctx", low_count, ctx_high)

    grad_outbias = jnp.sum(cotangent.astype(WIDE), axis=0)

    attended, grad_q, stats = query_side(
        my_blocks,
        key_first,
        key_last,
        natural,
        row_base,
        queries,
        keys,
        values,
        own_grads,
        cosine,
        sine,
        my_starts[:, None],
    )
    d_attended = jnp.concatenate(
        [
            attention_grads(after(near, stats), after(far, stats))
            for near, far in zip(g_near, g_far)
        ],
        axis=0,
    )
    first_up, first_down = (reduced_first(grad, stats) for grad in (grad_up, grad_down))
    low_feed = scatter_low(jnp.concatenate([first_up, first_down], axis=1))
    sum_feed = scatter_high(low_feed)
    sum_up, sum_down = sum_feed[:, :hidden_here], sum_feed[:, hidden_here:]

    early_rows = reduced_first(outer_pair(norm_t, grad_q, cotangent_t, attended))
    all_stats = stats
    step = 1
    while step < ctx_count:
        all_stats = jnp.concatenate([all_stats, partner(all_stats, "ctx", step)], axis=0)
        step *= 2
    grad_k, grad_v = key_side(
        my_blocks,
        query_first,
        query_last,
        natural,
        by_partner,
        stat_place,
        row_base,
        queries,
        keys,
        values,
        d_attended,
        cosine,
        sine,
        my_ends[:, None],
        all_stats,
        (early_rows,),
    )
    grad_late = outer_pair(norm_t, after(grad_k, low_feed), norm_t, grad_v)
    late_rows = reduced_first(grad_late)
    joint_rows = jnp.concatenate([early_rows, late_rows], axis=1)
    sum_joint = scatter_high(scatter_low(after(joint_rows, sum_feed)))
    grad_proj = [after(grad, late_rows) for grad in (grad_q, grad_k, grad_v)]
    grad_qbias = jnp.concatenate([jnp.sum(grad.astype(WIDE), axis=0) for grad in grad_proj])

    def joined(pair):
        return jnp.concatenate(pair, axis=1)

    partial_out = joined([dot_nn(attended, attn) for attn in attn_halves]) + feed_out

    def sum_halves(array):
        return own_half(array) + partner(far_half(array).astype(LOW), "tp", 1).astype(WIDE)

    out_bias = own_half((norm_vectors[2] + norm_vectors[3])[None, :])
    mixed = (tokens.astype(WIDE) + sum_halves(partial_out) + out_bias).astype(LOW)

    grad_norm = sum_halves(
        joined(
            [
                sum(
                    dot_nt(grad, stack[i * half : (i + 1) * half])
                    for i, grad in enumerate(grad_proj)
                )
                for stack in late_stacks
            ]
        )
        + feed_dx
    )
    my_normed = jnp.where(first_tp, *centered) * inv_std
    scaled = grad_norm * own_half(norm_vectors[0:1])
    row_sums = jnp.stack([jnp.sum(scaled, axis=1), jnp.sum(scaled * my_normed, axis=1)])
    row_means = (row_sums + partner(row_sums, "tp", 1)) / width
    grad_tokens = cotangent.astype(WIDE) + inv_std * (
        scaled - row_means[0][:, None] - my_normed * row_means[1][:, None]
    )

    vector_parts = jnp.stack(
        [jnp.sum(grad_norm * my_normed, axis=0), jnp.sum(grad_norm, axis=0), grad_outbias]
    )
    small = [vector_parts.reshape(-1), grad_qbias, grad_ubias[0]]
    small = jnp.concatenate([after(part, sum_joint) for part in small])
    small = sum_everywhere(small, ("ctx",))
    small = sum_everywhere(small, ("fsdp",))
    mine = small[: 3 * half].reshape(3, half)
    vectors = both_halves(mine, partner(mine, "tp", 1), 1)
    sum_vectors = jnp.concatenate([vectors, vectors[2:3]], axis=0)
    sum_qbias = small[3 * half : 6 * half].reshape(3, half)
    sum_ubias = small[6 * half :]

    own_q, own_attn, own_k, own_v = jnp.split(sum_joint, 4, axis=1)
    sums = (sum_up, own_attn, jnp.concatenate([own_q, own_k, own_v], axis=1), sum_down)
    pieces = jnp.stack(
        [
            (
                0.95 * moment + jnp.pad(total, ((0, 0), (0, hidden_here - total.shape[1])))
            ).astype(LOW)
            for moment, total in zip(old_moments, sums)
        ]
    )

    def to_owner(step):
        picked = lax.dynamic_index_in_dim(pieces, ctx_high ^ step, 0, keepdims=False)
        return partner(picked, "ctx", step * low_count) if step else picked

    matrix = jnp.concatenate([to_owner(s) for s in range(OWNERS)], axis=0)
    def all_rows(sums):
        return lax.all_gather(sums, "ctx", axis=0, tiled=True)

    feed_rows = all_rows(sum_feed.astype(LOW))
    joint_all = all_rows(after(sum_joint.astype(LOW), feed_rows)).astype(WIDE)
    all_up, all_down = jnp.split(feed_rows.astype(WIDE), 2, axis=1)
    fresh_up = 0.95 * up_moment + all_up
    fresh_down = 0.95 * down_moment + all_down.T
    all_q, all_attn, all_k, all_v = jnp.split(joint_all, 4, axis=1)
    fresh_qkv = 0.95 * qkv_moment + jnp.stack([all_q, all_k, all_v], axis=1)
    fresh_attn = 0.95 * attn_moment + all_attn.T

    parts = [matrix] + [partner(matrix, "ctx", s) for s in range(1, low_count)]
    for s in range(1, fsdp_count):
        parts += [partner(part, "fsdp", s) for part in parts[:low_count]]
    groups = [
        jnp.concatenate(parts[i : i + low_count], axis=0) for i in range(0, len(parts), low_count)
    ]
    near_cols = jnp.concatenate(groups, axis=0)
    far_cols = jnp.concatenate([partner(group, "tp", 1) for group in groups], axis=0)
    rows_out = orthogonal_rows(near_cols, far_cols, OWNERS * piece, ()).reshape(OWNERS, piece, hidden_here)
    returned = [rows_out[0]] + [
        partner(rows_out[s], "ctx", s * low_count) for s in range(1, OWNERS)
    ]
    returned = jnp.stack([after(part, fresh_up, fresh_down) for part in returned])
    full_hidden = hidden_here * 2
    rates = (
        0.5 * math.sqrt(full_hidden / width),
        0.5 * math.sqrt(width / (width // HD)),
        0.5 * math.sqrt(3 * width / width),
        0.5 * math.sqrt(full_hidden / full_hidden),
    )
    new_up, new_attn, new_qkv, new_down = (
        old_weights[m]
        - rate * lax.dynamic_index_in_dim(returned, ctx_high ^ m, 0, keepdims=False).astype(WIDE)
        for m, rate in enumerate(rates)
    )
    new_attn, new_qkv = new_attn[:, :half], new_qkv[:, : 3 * half]

    vector_rate = 0.3 / math.sqrt(row_count * fsdp_count * ctx_count)
    mom_norm = 0.9 * norm_moment + sum_vectors
    mom_qbias = 0.9 * qbias_moment + sum_qbias
    mom_ubias = 0.9 * ubias_moment + sum_ubias
    return (
        mixed,
        grad_tokens,
        fresh_qkv,
        jnp.stack(jnp.split(new_qkv, 3, axis=1), axis=1),
        fresh_attn,
        new_attn.T,
        fresh_up,
        new_up,
        fresh_down,
        new_down.T,
        mom_norm,
        norm_vectors - vector_rate * mom_norm,
        mom_qbias,
        qkv_bias - vector_rate * mom_qbias,
        mom_ubias,
        up_bias - vector_rate * mom_ubias,
    )


def solution(mesh):
    return jax.shard_map(
        body,
        mesh=mesh,
        in_specs=(
            P(("fsdp", "ctx"), "tp"),
            P(("fsdp", "ctx"), "tp"),
            P("fsdp", None, "tp"),
            P("tp", "fsdp"),
            P("fsdp", "tp"),
            P("tp", "fsdp"),
            P(),
            P(None, "tp"),
            P("tp"),
            P("fsdp", None, "tp"),
            P("tp", "fsdp"),
            P("fsdp", "tp"),
            P("tp", "fsdp"),
            P(),
            P(None, "tp"),
            P("tp"),
            P("fsdp", None),
            P("fsdp", None),
        ),
        out_specs=(
            P(("fsdp", "ctx"), "tp"),
            P(("fsdp", "ctx"), "tp"),
            P("fsdp", None, "tp"),
            P(("fsdp", "ctx"), None, "tp"),
            P("tp", "fsdp"),
            P("tp", ("fsdp", "ctx")),
            P("fsdp", "tp"),
            P(("fsdp", "ctx"), "tp"),
            P("tp", "fsdp"),
            P("tp", ("fsdp", "ctx")),
            P(),
            P(),
            P(None, "tp"),
            P(None, "tp"),
            P("tp"),
            P("tp"),
        ),
        check_vma=False,
    )
```

```python
from functools import partial
import math

import jax
import jax.numpy as jnp
from jax import lax
from jax.experimental import pallas as pl
from jax.experimental.pallas import tpu as pltpu
from jax.sharding import PartitionSpec as P

HD = 64
ROT = 16
BLK = 128
NS_STEPS = 5
CHUNK = 512
MAX_LEN = 2048
SPAN = (MAX_LEN + BLK) // CHUNK + 2
OWNERS = 4
NS_COEF = (3.4445, -4.775, 2.0315)
NEG_BIG = -1e30
SCALE = HD**-0.5
LOW = jnp.bfloat16
WIDE = jnp.float32
NT = (((1,), (1,)), ((), ()))
VMEM_ASK = 56 * 1024 * 1024


def dot_nn(left, right):
    return jnp.dot(left, right, preferred_element_type=WIDE)


def dot_nt(left, right):
    return lax.dot_general(left, right, NT, preferred_element_type=WIDE)


def partner(value, axis, step):
    size = lax.axis_size(axis)
    return lax.ppermute(value, axis, [(i, i ^ step) for i in range(size)])


def sum_scatter(pieces, axis, stride, index, *earlier):
    count = pieces.shape[0]
    total = lax.dynamic_index_in_dim(pieces, index, 0, keepdims=False)
    total = after(total, *earlier).astype(WIDE)
    for step in range(1, count):
        piece = lax.dynamic_index_in_dim(pieces, index ^ step, 0, keepdims=False)
        total = total + partner(piece.astype(LOW), axis, step * stride).astype(WIDE)
    return total


def after(value, *earlier):
    return lax.optimization_barrier((value, *earlier))[0]


def sum_everywhere(value, axes):
    for axis in axes:
        step = 1
        while step < lax.axis_size(axis):
            value = value + partner(value, axis, step)
            step *= 2
    return value


def turned(block, cosine, sine, lane):
    half = ROT // 2
    swapped = jnp.where(
        lane % HD < half, pltpu.roll(block, BLK - half, 1), pltpu.roll(block, half, 1)
    )
    return block * cosine + swapped * sine


def two_heads(block, lane):
    zero = jnp.zeros_like(block)
    return jnp.concatenate(
        [jnp.where(lane < HD, block, zero), jnp.where(lane < HD, zero, block)], axis=0
    )


def one_of_two(stacked, lane):
    return jnp.where(lane < HD, stacked[:BLK], stacked[BLK:])


def project_kernel(
    near, far, w_near, w_far, bias, vec_near, vec_far, cos_ref, sin_ref, *outs
):
    rows, half = outs[0].shape
    width = 2 * half
    own, other = near[...].astype(WIDE), far[...].astype(WIDE)
    mean = (
        jnp.sum(own, axis=1, keepdims=True) + jnp.sum(other, axis=1, keepdims=True)
    ) / width
    own, other = own - mean, other - mean
    var = (
        jnp.sum(own * own, axis=1, keepdims=True) + jnp.sum(other * other, axis=1, keepdims=True)
    ) / width
    inv_std = lax.rsqrt(var + 1e-5)
    own = (own * inv_std * vec_near[0:1] + vec_near[1:2]).astype(LOW)
    other = (other * inv_std * vec_far[0:1] + vec_far[1:2]).astype(LOW)
    lane = lax.broadcasted_iota(jnp.int32, (rows, BLK), 1)
    cosine, sine = cos_ref[...], sin_ref[...]
    for part, out in enumerate(outs):
        span = slice(part * half, (part + 1) * half)
        made = dot_nn(own, w_near[span]) + dot_nn(other, w_far[span]) + bias[part : part + 1]
        for pair in range(half // BLK):
            lanes = slice(pair * BLK, (pair + 1) * BLK)
            block = made[:, lanes]
            if part < 2:
                block = turned(block, cosine, sine, lane)
            out[:, lanes] = block.astype(LOW)


def project_rows(near, far, weights, cosine, sine):
    rows, half = near.shape

    def fixed(array):
        return pl.BlockSpec(array.shape, lambda i: (0,) * array.ndim)

    def chunk(width):
        return pl.BlockSpec((CHUNK, width), lambda i: (i, 0))

    return pl.pallas_call(
        project_kernel,
        grid=(rows // CHUNK,),
        in_specs=[chunk(half)] * 2 + [fixed(w) for w in weights] + [chunk(BLK)] * 2,
        out_specs=[chunk(half)] * 3,
        out_shape=[jax.ShapeDtypeStruct((rows, half), LOW)] * 3,
        compiler_params=pltpu.CompilerParams(vmem_limit_bytes=VMEM_ASK),
        cost_estimate=pl.CostEstimate(
            flops=44 * rows * half * half, bytes_accessed=14 * rows * half, transcendentals=0
        ),
        name="project_rows",
    )(near, far, *weights, cosine, sine)


def feed_kernel(
    xa_ref,
    xb_ref,
    ga_ref,
    gb_ref,
    up_a,
    up_b,
    down_a,
    down_b,
    bias_ref,
    *refs,
):
    out_ref, dx_ref, dup_ref, ddown_ref, dbias_ref, xt_ref, gt_ref = refs[-7:]
    half = xa_ref.shape[1]
    first, second = slice(0, half), slice(half, 2 * half)

    @pl.when(pl.program_id(0) == 0)
    def _():
        xt_ref[first] = xa_ref[...].T
        xt_ref[second] = xb_ref[...].T
        gt_ref[first] = ga_ref[...].T
        gt_ref[second] = gb_ref[...].T
        out_ref[...] = jnp.zeros(out_ref.shape, WIDE)
        dx_ref[...] = jnp.zeros(dx_ref.shape, WIDE)

    hidden = dot_nn(xa_ref[...], up_a[...]) + dot_nn(xb_ref[...], up_b[...]) + bias_ref[...]
    grad = dot_nt(ga_ref[...], down_a[...]) + dot_nt(gb_ref[...], down_b[...])
    below = 0.5 + 0.5 * lax.erf(hidden * math.sqrt(0.5))
    density = jnp.exp(-0.5 * hidden * hidden) * (1.0 / math.sqrt(2.0 * math.pi))
    active = (hidden * below).astype(LOW)
    grad = (grad * (below + hidden * density)).astype(LOW)
    dbias_ref[...] = jnp.sum(grad.astype(WIDE), axis=0, keepdims=True)
    out_ref[:, first] += dot_nn(active, down_a[...])
    out_ref[:, second] += dot_nn(active, down_b[...])
    dx_ref[:, first] += dot_nt(grad, up_a[...])
    dx_ref[:, second] += dot_nt(grad, up_b[...])
    dup_ref[...] = dot_nn(xt_ref[...], grad).astype(LOW)
    ddown_ref[...] = dot_nn(gt_ref[...], active).astype(LOW)


def feed_forward(x_halves, g_halves, stacks, bias, earlier):
    rows, half = x_halves[0].shape
    width = 2 * half
    hidden = bias.shape[1]
    steps = hidden // half

    def whole(shape):
        return pl.BlockSpec(shape, lambda i: (0, 0))

    up = pl.BlockSpec((half, half), lambda i: (i, 0))
    down = pl.BlockSpec((half, half), lambda i: (i + steps, 0))
    column = pl.BlockSpec((width, half), lambda i: (0, i))
    line = pl.BlockSpec((1, half), lambda i: (0, i))
    return pl.pallas_call(
        feed_kernel,
        grid=(steps,),
        in_specs=[whole((rows, half))] * 4
        + [up, up, down, down, line]
        + [pl.BlockSpec(memory_space=pl.ANY)] * len(earlier),
        out_specs=[
            whole((rows, width)),
            whole((rows, width)),
            column,
            column,
            line,
            whole((width, rows)),
            whole((width, rows)),
        ],
        out_shape=[
            jax.ShapeDtypeStruct((rows, width), WIDE),
            jax.ShapeDtypeStruct((rows, width), WIDE),
            jax.ShapeDtypeStruct((width, hidden), LOW),
            jax.ShapeDtypeStruct((width, hidden), LOW),
            jax.ShapeDtypeStruct((1, hidden), WIDE),
            jax.ShapeDtypeStruct((width, rows), LOW),
            jax.ShapeDtypeStruct((width, rows), LOW),
        ],
        compiler_params=pltpu.CompilerParams(vmem_limit_bytes=VMEM_ASK),
        cost_estimate=pl.CostEstimate(
            flops=26 * rows * width * hidden, bytes_accessed=12 * width * hidden, transcendentals=0
        ),
        name="feed_forward",
    )(*x_halves, *g_halves, *stacks, *stacks, bias, *earlier)


def outer_kernel(left_a, right_a, left_b, right_b, out_ref):
    half = right_a.shape[1]
    out_ref[:, :half] = dot_nn(left_a[...], right_a[...]).astype(LOW)
    out_ref[:, half:] = dot_nn(left_b[...], right_b[...]).astype(LOW)


def outer_pair(left_a, right_a, left_b, right_b):
    rows, depth = left_a.shape
    half = right_a.shape[1]
    return pl.pallas_call(
        outer_kernel,
        in_specs=[vmem()] * 4,
        out_specs=vmem(),
        out_shape=jax.ShapeDtypeStruct((rows, 2 * half), LOW),
        compiler_params=pltpu.CompilerParams(vmem_limit_bytes=VMEM_ASK),
        cost_estimate=pl.CostEstimate(
            flops=8 * rows * depth * half, bytes_accessed=6 * rows * depth, transcendentals=0
        ),
        name="outer_pair",
    )(left_a, right_a, left_b, right_b)


def lane_tiles(array, combine):
    total = array[:, :BLK]
    for i in range(1, array.shape[1] // BLK):
        total = combine(total, array[:, i * BLK : (i + 1) * BLK])
    return total


def gathered_blocks(ref, inverse, chunk, lanes):
    count = CHUNK // BLK
    return jnp.concatenate(
        [
            ref[pl.ds(pl.multiple_of(inverse[chunk * count + i] * BLK, BLK), BLK), lanes]
            for i in range(count)
        ],
        axis=0,
    )


def query_kernel(
    blocks,
    first,
    last,
    natural,
    base,
    q_ref,
    k_ref,
    v_ref,
    d_ref,
    cos_ref,
    sin_ref,
    start_ref,
    att_out,
    dq_out,
    stat_out,
    s_scr,
    p_scr,
    q_scr,
    d_scr,
    m_scr,
    l_scr,
    e_scr,
    o_scr,
):
    pairs = q_ref.shape[1] // BLK
    own = att_out.shape[0] // BLK
    lane = lax.broadcasted_iota(jnp.int32, (BLK, BLK), 1)

    def lanes(pair):
        return slice(pair * BLK, (pair + 1) * BLK)

    @pl.loop(0, own)
    def _(j):
        row0 = pl.multiple_of(blocks[j] * BLK, BLK)
        out0 = pl.multiple_of(j * BLK, BLK)
        here = pl.multiple_of(base[0] + out0, BLK)
        lo = first[j]
        hi = last[j]
        for g in range(pairs):
            q_scr[g] = two_heads(q_ref[pl.ds(here, BLK), lanes(g)].astype(WIDE), lane).astype(
                LOW
            ) * LOW(SCALE)
            d_scr[g] = two_heads(d_ref[pl.ds(out0, BLK), lanes(g)].astype(WIDE), lane).astype(LOW)
        m_scr[...] = jnp.full(m_scr.shape, NEG_BIG, WIDE)
        l_scr[...] = jnp.zeros(l_scr.shape, WIDE)
        e_scr[...] = jnp.zeros(e_scr.shape, WIDE)
        o_scr[...] = jnp.zeros(o_scr.shape, WIDE)
        starts = start_ref[pl.ds(out0, BLK), :]
        places = row0 + lax.broadcasted_iota(jnp.int32, (BLK, 1), 0)
        starts = jnp.concatenate([starts, starts], axis=0)
        places = jnp.concatenate([places, places], axis=0)

        @pl.loop(lo, hi)
        def _(c):
            key0 = pl.multiple_of(c * CHUNK, CHUNK)
            key_place = key0 + lax.broadcasted_iota(jnp.int32, (2 * BLK, CHUNK), 1)
            allowed = (key_place >= starts) & (key_place <= places)
            for g in range(pairs):
                scores = dot_nt(q_scr[g], gathered_blocks(k_ref, natural, c, lanes(g)))
                scores = jnp.where(allowed, scores, NEG_BIG)
                s_scr[g, c - lo] = scores
                m_scr[g] = jnp.maximum(m_scr[g], lane_tiles(scores, jnp.maximum))

        for g in range(pairs):
            m_scr[g] = jnp.broadcast_to(
                jnp.max(m_scr[g], axis=1, keepdims=True), (2 * BLK, BLK)
            )

        @pl.loop(lo, hi)
        def _(c):
            for g in range(pairs):
                values = gathered_blocks(v_ref, natural, c, lanes(g))
                top = m_scr[g]
                weights = jnp.exp(s_scr[g, c - lo] - jnp.concatenate([top] * (CHUNK // BLK), 1))
                l_scr[g] += lane_tiles(weights, jnp.add)
                o_scr[g] += dot_nn(weights.astype(LOW), values)
                grad_prob = dot_nt(d_scr[g], values)
                e_scr[g] += lane_tiles(weights * grad_prob, jnp.add)
                s_scr[g, c - lo] = weights
                p_scr[g, c - lo] = grad_prob

        for g in range(pairs):
            total = jnp.sum(l_scr[g], axis=1, keepdims=True)
            share = 1.0 / total
            delta = jnp.sum(e_scr[g], axis=1, keepdims=True) * share
            att_out[pl.ds(out0, BLK), lanes(g)] = one_of_two(o_scr[g] * share, lane).astype(LOW)
            log_sum = m_scr[g] + jnp.log(total)
            stat_out[j, 2 * g : 2 * g + 1, :] = log_sum[:BLK].T[0:1]
            stat_out[j, 2 * g + 1 : 2 * g + 2, :] = log_sum[BLK:].T[0:1]
            wide = jnp.broadcast_to(delta, (2 * BLK, BLK))
            line = stat_out.shape[1] // 2 + 2 * g
            stat_out[j, line : line + 1, :] = wide[:BLK].T[0:1]
            stat_out[j, line + 1 : line + 2, :] = wide[BLK:].T[0:1]
            l_scr[g] = jnp.broadcast_to(share, (2 * BLK, BLK))
            e_scr[g] = wide
        o_scr[...] = jnp.zeros(o_scr.shape, WIDE)

        @pl.loop(lo, hi)
        def _(c):
            for g in range(pairs):
                wide = jnp.concatenate([e_scr[g]] * (CHUNK // BLK), 1)
                grad_score = s_scr[g, c - lo] * (p_scr[g, c - lo] - wide)
                o_scr[g] += dot_nn(
                    grad_score.astype(LOW), gathered_blocks(k_ref, natural, c, lanes(g))
                )

        cosine = cos_ref[pl.ds(here, BLK), :]
        sine = sin_ref[pl.ds(here, BLK), :]
        for g in range(pairs):
            grad = one_of_two(o_scr[g] * l_scr[g], lane) * SCALE
            dq_out[pl.ds(out0, BLK), lanes(g)] = turned(grad, cosine, -sine, lane).astype(LOW)


def smem():
    return pl.BlockSpec(memory_space=pltpu.SMEM)


def vmem():
    return pl.BlockSpec(memory_space=pltpu.VMEM)


def query_side(blocks, first, last, natural, base, queries, keys, values, grads, cosine, sine, starts):
    own = blocks.shape[0]
    width = queries.shape[1]
    pairs = width // BLK
    stat_rows = 16 * ((2 * pairs + 7) // 8)
    work = 2 * BLK * CHUNK
    return pl.pallas_call(
        query_kernel,
        in_specs=[smem()] * 5 + [vmem()] * 7,
        out_specs=[vmem()] * 3,
        out_shape=[
            jax.ShapeDtypeStruct((own * BLK, width), LOW),
            jax.ShapeDtypeStruct((own * BLK, width), LOW),
            jax.ShapeDtypeStruct((own, stat_rows, BLK), WIDE),
        ],
        scratch_shapes=[
            pltpu.VMEM((pairs, SPAN, 2 * BLK, CHUNK), WIDE),
            pltpu.VMEM((pairs, SPAN, 2 * BLK, CHUNK), WIDE),
            pltpu.VMEM((pairs, 2 * BLK, BLK), LOW),
            pltpu.VMEM((pairs, 2 * BLK, BLK), LOW),
            pltpu.VMEM((pairs, 2 * BLK, BLK), WIDE),
            pltpu.VMEM((pairs, 2 * BLK, BLK), WIDE),
            pltpu.VMEM((pairs, 2 * BLK, BLK), WIDE),
            pltpu.VMEM((pairs, 2 * BLK, BLK), WIDE),
        ],
        compiler_params=pltpu.CompilerParams(vmem_limit_bytes=VMEM_ASK),
        cost_estimate=pl.CostEstimate(
            flops=own * pairs * 12 * 4 * 2 * work * BLK,
            bytes_accessed=4 * keys.shape[0] * width * 2,
            transcendentals=own * pairs * 4 * work,
        ),
        name="query_side",
    )(blocks, first, last, natural, base, queries, keys, values, grads, cosine, sine, starts)


def key_kernel(
    blocks,
    first,
    last,
    natural,
    by_partner,
    stat_place,
    base,
    q_ref,
    k_ref,
    v_ref,
    d_ref,
    cos_ref,
    sin_ref,
    end_ref,
    stat_ref,
    *rest,
):
    dk_out, dv_out, k_scr, v_scr, dk_scr, dv_scr = rest[-6:]
    pairs = q_ref.shape[1] // BLK
    own = dk_out.shape[0] // BLK
    half_stat = stat_ref.shape[1] // 2
    lane = lax.broadcasted_iota(jnp.int32, (BLK, BLK), 1)

    def lanes(pair):
        return slice(pair * BLK, (pair + 1) * BLK)

    @pl.loop(0, own)
    def _(j):
        row0 = pl.multiple_of(blocks[j] * BLK, BLK)
        out0 = pl.multiple_of(j * BLK, BLK)
        here = pl.multiple_of(base[0] + out0, BLK)
        for g in range(pairs):
            k_scr[g] = two_heads(k_ref[pl.ds(here, BLK), lanes(g)].astype(WIDE), lane).astype(
                LOW
            ) * LOW(SCALE)
            v_scr[g] = two_heads(v_ref[pl.ds(here, BLK), lanes(g)].astype(WIDE), lane).astype(LOW)
        dk_scr[...] = jnp.zeros(dk_scr.shape, WIDE)
        dv_scr[...] = jnp.zeros(dv_scr.shape, WIDE)
        ends = end_ref[pl.ds(out0, BLK), :]
        places = row0 + lax.broadcasted_iota(jnp.int32, (BLK, 1), 0)

        @pl.loop(first[j], last[j])
        def _(c):
            query0 = pl.multiple_of(c * CHUNK, CHUNK)
            query_place = query0 + lax.broadcasted_iota(jnp.int32, (BLK, CHUNK), 1)
            allowed = (query_place >= places) & (query_place < ends)
            count = CHUNK // BLK
            slots = [stat_place[c * count + i] for i in range(count)]

            def stat(row):
                return jnp.concatenate([stat_ref[slot, row : row + 1, :] for slot in slots], 1)

            for g in range(pairs):
                queries = gathered_blocks(q_ref, natural, c, lanes(g))
                grads = gathered_blocks(d_ref, by_partner, c, lanes(g))
                scores = dot_nt(k_scr[g], queries)
                grad_prob = dot_nt(v_scr[g], grads)
                probs, grad_scores = [], []
                for h in range(2):
                    rows = slice(h * BLK, (h + 1) * BLK)
                    shifted = jnp.where(allowed, scores[rows] - stat(2 * g + h), NEG_BIG)
                    prob = jnp.exp(shifted)
                    probs.append(prob.astype(LOW))
                    grad_scores.append(
                        (prob * (grad_prob[rows] - stat(half_stat + 2 * g + h))).astype(LOW)
                    )
                dv_scr[g] += dot_nn(jnp.concatenate(probs, 0), grads)
                dk_scr[g] += dot_nn(jnp.concatenate(grad_scores, 0), queries)

        cosine = cos_ref[pl.ds(here, BLK), :]
        sine = sin_ref[pl.ds(here, BLK), :]
        for g in range(pairs):
            grad = one_of_two(dk_scr[g], lane) * SCALE
            dk_out[pl.ds(out0, BLK), lanes(g)] = turned(grad, cosine, -sine, lane).astype(LOW)
            dv_out[pl.ds(out0, BLK), lanes(g)] = one_of_two(dv_scr[g], lane).astype(LOW)


def key_side(
    blocks,
    first,
    last,
    natural,
    by_partner,
    stat_place,
    base,
    queries,
    keys,
    values,
    grads,
    cosine,
    sine,
    ends,
    stats,
    after,
):
    own = blocks.shape[0]
    width = queries.shape[1]
    pairs = width // BLK
    work = 2 * BLK * CHUNK
    return pl.pallas_call(
        key_kernel,
        in_specs=[smem()] * 7 + [vmem()] * 8 + [pl.BlockSpec(memory_space=pl.ANY)] * len(after),
        out_specs=[vmem()] * 2,
        out_shape=[jax.ShapeDtypeStruct((own * BLK, width), LOW)] * 2,
        scratch_shapes=[
            pltpu.VMEM((pairs, 2 * BLK, BLK), LOW),
            pltpu.VMEM((pairs, 2 * BLK, BLK), LOW),
            pltpu.VMEM((pairs, 2 * BLK, BLK), WIDE),
            pltpu.VMEM((pairs, 2 * BLK, BLK), WIDE),
        ],
        compiler_params=pltpu.CompilerParams(vmem_limit_bytes=VMEM_ASK),
        cost_estimate=pl.CostEstimate(
            flops=own * pairs * 12 * 4 * 2 * work * BLK,
            bytes_accessed=4 * keys.shape[0] * width * 2,
            transcendentals=own * pairs * 4 * work,
        ),
        name="key_side",
    )(
        blocks,
        first,
        last,
        natural,
        by_partner,
        stat_place,
        base,
        queries,
        keys,
        values,
        grads,
        cosine,
        sine,
        ends,
        stats,
        *after,
    )


TILE = 256


def symmetric_product(out_ref, left, right):
    size = out_ref.shape[0]
    for i in range(0, size, TILE):
        out_ref[i : i + TILE, i:] = dot_nt(left[i : i + TILE, :], right[i:, :])
    for i in range(0, size, TILE):
        for j in range(i + TILE, size, TILE):
            out_ref[j : j + TILE, i : i + TILE] = out_ref[i : i + TILE, j : j + TILE].T


def ns_kernel(near_ref, far_ref, *refs):
    out_ref, wide_scr, low_scr, gram_scr, poly_scr = refs[-5:]
    size, half = near_ref.shape
    span = 2 * half
    step = 768
    cuts = [slice(i, i + step) for i in range(0, span, step)]
    total = jnp.zeros((1, 1), WIDE)
    for source, base in ((near_ref, 0), (far_ref, half)):
        for i in range(0, half, step):
            part = source[:, i : i + step].astype(WIDE)
            wide_scr[:, base + i : base + i + step] = part
            total = total + jnp.sum(part * part)
    factor = 1.0 / (jnp.sqrt(total) + 1e-7)
    for cut in cuts:
        part = wide_scr[:, cut] * factor
        wide_scr[:, cut] = part
        low_scr[:, cut] = part.astype(LOW)

    def polynomial():
        symmetric_product(gram_scr, low_scr, low_scr)
        poly_scr[...] = gram_scr[...].astype(LOW)
        first = gram_scr[...] * NS_COEF[1]
        symmetric_product(gram_scr, poly_scr, poly_scr)
        poly_scr[...] = (first + NS_COEF[2] * gram_scr[...]).astype(LOW)

    @pl.loop(0, NS_STEPS - 1)
    def _(_):
        polynomial()
        for cut in cuts:
            part = NS_COEF[0] * wide_scr[:, cut] + dot_nn(poly_scr[...], low_scr[:, cut])
            wide_scr[:, cut] = part
            low_scr[:, cut] = part.astype(LOW)

    polynomial()
    rows = out_ref.shape[0]
    for i in range(0, half, step):
        cut = slice(i, i + step)
        out_ref[:, cut] = (
            NS_COEF[0] * wide_scr[:rows, cut] + dot_nn(poly_scr[:rows, :], low_scr[:, cut])
        ).astype(LOW)


def orthogonal_rows(near, far, rows, earlier):
    size, half = near.shape
    kept = rows if rows % 16 == 0 else size
    out = pl.pallas_call(
        ns_kernel,
        in_specs=[vmem()] * 2 + [pl.BlockSpec(memory_space=pl.ANY)] * len(earlier),
        out_specs=vmem(),
        out_shape=jax.ShapeDtypeStruct((kept, half), LOW),
        scratch_shapes=[
            pltpu.VMEM((size, 2 * half), WIDE),
            pltpu.VMEM((size, 2 * half), LOW),
            pltpu.VMEM((size, size), WIDE),
            pltpu.VMEM((size, size), LOW),
        ],
        compiler_params=pltpu.CompilerParams(vmem_limit_bytes=VMEM_ASK),
        cost_estimate=pl.CostEstimate(
            flops=NS_STEPS * 10 * size * size * half,
            bytes_accessed=4 * size * half,
            transcendentals=0,
        ),
        name="orthogonal_rows",
    )(near, far, *earlier)
    return out[:rows]


def rotary_tables(places):
    half = ROT // 2
    exponent = jnp.arange(0, ROT, 2, dtype=WIDE) / ROT
    frequency = 1.0 / 10000.0**exponent
    angles = frequency[:, None] * places.astype(WIDE)[None, :]
    lane = jnp.arange(BLK) % HD
    picked = ((lane % half)[None, :] == jnp.arange(half)[:, None]) & (lane < ROT)[None, :]
    sign = jnp.where(lane < half, -1.0, 1.0)[None, :]
    spread = partial(
        jnp.einsum, "fn,fl->nl", precision=lax.Precision.HIGHEST, preferred_element_type=WIDE
    )
    cosine = spread(jnp.cos(angles), picked.astype(WIDE)) + (lane >= ROT)[None, :].astype(WIDE)
    return cosine, spread(jnp.sin(angles), picked * sign)


def body(
    tokens,
    cotangent,
    w_qkv,
    w_attn,
    w_up,
    w_down,
    norm_vectors,
    qkv_bias,
    up_bias,
    qkv_moment,
    attn_moment,
    up_moment,
    down_moment,
    norm_moment,
    qbias_moment,
    ubias_moment,
    seq_lengths,
    block_source,
):
    row_count, half = tokens.shape
    fsdp_count = lax.axis_size("fsdp")
    ctx_count = lax.axis_size("ctx")
    tp_index = lax.axis_index("tp")
    fsdp_index = lax.axis_index("fsdp")
    ctx_index = lax.axis_index("ctx")
    low_count = ctx_count // OWNERS
    ctx_low = ctx_index % low_count
    ctx_high = ctx_index // low_count
    width = 2 * half
    own_blocks = row_count // BLK
    pack = ctx_count * row_count
    first_tp = tp_index == 0
    block_row = block_source[0]
    length_row = seq_lengths[0]

    def both_halves(mine, other, dim):
        return jnp.concatenate(
            [jnp.where(first_tp, mine, other), jnp.where(first_tp, other, mine)], axis=dim
        )

    def own_half(array):
        return jnp.where(first_tp, array[:, :half], array[:, half:])

    def far_half(array):
        return jnp.where(first_tp, array[:, half:], array[:, :half])

    own_pair = jnp.concatenate([tokens, cotangent], axis=0)
    far_pair = partner(own_pair, "tp", 1)

    g_near = [
        jnp.concatenate(
            [cotangent] + [partner(cotangent, "ctx", s * low_count) for s in range(1, OWNERS)],
            axis=0,
        )
    ]
    x_near = lax.all_gather(tokens, "ctx", axis=0, tiled=True)
    x_far = partner(x_near, "tp", 1)

    def feed_stack(up, down):
        cuts = range(0, up.shape[1], half)
        return jnp.concatenate([up[:, i : i + half] for i in cuts] + [down], axis=0)

    def late_stack(qkv, attn):
        return jnp.concatenate([qkv[:, i] for i in range(3)] + [attn], axis=0)

    low_weights = [w.astype(LOW) for w in (w_up, w_down, w_qkv, w_attn)]
    if fsdp_count == 2:

        def exchanged(stack):
            other = partner(stack, "fsdp", 1)
            first = fsdp_index == 0
            return jnp.where(first, stack, other), jnp.where(first, other, stack)

        feed_stacks = exchanged(feed_stack(*low_weights[:2]))
        late_stacks = exchanged(after(late_stack(*low_weights[2:]), feed_stacks[0]))
    else:
        whole_up, whole_down, whole_qkv, whole_attn = (
            lax.all_gather(w, "fsdp", axis=dim, tiled=True)
            for w, dim in zip(low_weights, (0, 1, 0, 1))
        )
        cuts = (slice(0, half), slice(half, 2 * half))
        feed_stacks = tuple(feed_stack(whole_up[cut], whole_down[:, cut]) for cut in cuts)
        late_stacks = tuple(late_stack(whole_qkv[cut], whole_attn[:, cut]) for cut in cuts)
    hidden_here = up_bias.shape[0]
    attn_halves = tuple(part[3 * half :] for part in late_stacks)

    def by_partners(ctx):
        differs = ctx ^ ctx_index
        return (differs % low_count) * OWNERS + differs // low_count

    slot_blocks = jnp.arange(block_row.shape[0], dtype=jnp.int32)
    slot_ctx, slot_rest = slot_blocks // own_blocks, slot_blocks % own_blocks
    holds = block_row[None, :] == slot_blocks[:, None]

    def located(places):
        return jnp.sum(jnp.where(holds, places[None, :], 0), axis=1).astype(jnp.int32)

    natural = located(slot_blocks)
    by_partner = located(by_partners(slot_ctx) * own_blocks + slot_rest)
    stat_place = located((slot_ctx ^ ctx_index) * own_blocks + slot_rest)
    row_base = (ctx_index * row_count).reshape(1)
    my_blocks = lax.dynamic_slice_in_dim(block_row, ctx_index * own_blocks, own_blocks)

    seq_ends = jnp.cumsum(length_row).astype(jnp.int32)
    seq_starts = seq_ends - length_row

    def bounds(packed):
        inside = (packed[:, None] >= seq_starts[None, :]) & (packed[:, None] < seq_ends[None, :])
        return (
            jnp.sum(jnp.where(inside, seq_starts[None, :], 0), axis=1).astype(jnp.int32),
            jnp.sum(jnp.where(inside, seq_ends[None, :], 0), axis=1).astype(jnp.int32),
        )

    offsets = jnp.arange(BLK, dtype=jnp.int32)
    packed = (block_row[:, None] * BLK + offsets[None, :]).reshape(-1)
    cosine, sine = rotary_tables(packed - bounds(packed)[0])
    my_starts, my_ends = bounds(
        (my_blocks[:, None] * BLK + offsets[None, :]).reshape(-1)
    )
    key_first = bounds(my_blocks * BLK)[0] // CHUNK
    key_last = (my_blocks * BLK + BLK - 1) // CHUNK + 1
    query_first = my_blocks * BLK // CHUNK
    query_last = (bounds(my_blocks * BLK + BLK - 1)[1] + CHUNK - 1) // CHUNK

    def own_first(array, dim):
        left, right = jnp.split(array, 2, axis=dim)
        return jnp.where(first_tp, left, right), jnp.where(first_tp, right, left)

    piece = width // (fsdp_count * ctx_count)

    def my_rows(array, dim):
        return lax.dynamic_slice_in_dim(array, ctx_index * piece, piece, dim)

    def as_rows(up, attn, qkv, down):
        rows = (
            my_rows(up, 0),
            my_rows(attn, 1).T,
            jnp.concatenate([my_rows(qkv, 0)[:, i] for i in range(3)], axis=1),
            my_rows(down, 1).T,
        )
        return jnp.stack([jnp.pad(r, ((0, 0), (0, hidden_here - r.shape[1]))) for r in rows])

    old_moments = as_rows(up_moment, attn_moment, qkv_moment, down_moment)
    old_weights = as_rows(w_up, w_attn, w_qkv, w_down)

    def two_halves(mine, other):
        return jnp.where(first_tp, mine, other), jnp.where(first_tp, other, mine)

    x_halves = [half_x.astype(WIDE) for half_x in two_halves(tokens, far_pair[:row_count])]
    row_mean = sum(jnp.sum(x, axis=1, keepdims=True) for x in x_halves) / width
    centered = [x - row_mean for x in x_halves]
    inv_std = lax.rsqrt(sum(jnp.sum(x * x, axis=1, keepdims=True) for x in centered) / width + 1e-5)
    norm_halves = [
        (x * inv_std * vec[0] + vec[1]).astype(LOW)
        for x, vec in zip(centered, jnp.split(norm_vectors, 2, axis=1))
    ]
    feed_out, feed_dx, grad_up, grad_down, grad_ubias, norm_t, cotangent_t = feed_forward(
        norm_halves,
        two_halves(cotangent, far_pair[row_count:]),
        feed_stacks,
        up_bias.reshape(1, hidden_here),
        (old_moments, old_weights, cosine, sine),
    )
    for s in range(1, low_count):
        g_near.append(partner(g_near[0], "ctx", s))
    g_far = [partner(part, "tp", 1) for part in [g_near[0]] + [after(p, grad_ubias) for p in g_near[1:]]]

    queries, keys, values = project_rows(
        x_near,
        x_far,
        (*two_halves(*late_stacks), qkv_bias, *own_first(norm_vectors, 1)),
        cosine,
        sine,
    )
    attn_near, attn_far = two_halves(*attn_halves)
    d_attended = jnp.concatenate(
        [
            (dot_nt(near, attn_near) + dot_nt(far, attn_far)).astype(LOW)
            for near, far in zip(g_near, g_far)
        ],
        axis=0,
    )

    def reduced_first(gradient, *earlier):
        rows = gradient.shape[0] // fsdp_count
        pieces = gradient.reshape(fsdp_count, rows, gradient.shape[1])
        return sum_scatter(pieces, "fsdp", 1, fsdp_index, *earlier)

    def reduced_rest(part):
        piece = part.shape[0] // ctx_count
        part = part.reshape(OWNERS, low_count, piece, part.shape[1])
        part = sum_scatter(jnp.swapaxes(part, 0, 1), "ctx", 1, ctx_low)
        return sum_scatter(part, "ctx", low_count, ctx_high)

    first_up, first_down = (reduced_first(grad, queries) for grad in (grad_up, grad_down))
    grad_outbias = jnp.sum(cotangent.astype(WIDE), axis=0)

    attended, grad_q, stats = query_side(
        my_blocks,
        key_first,
        key_last,
        natural,
        row_base,
        queries,
        keys,
        values,
        d_attended,
        cosine,
        sine,
        my_starts[:, None],
    )
    sum_feed = lax.psum_scatter(
        jnp.concatenate([first_up, first_down], axis=1).astype(LOW),
        "ctx",
        scatter_dimension=0,
        tiled=True,
    ).astype(WIDE)
    sum_up, sum_down = sum_feed[:, :hidden_here], sum_feed[:, hidden_here:]

    early_rows = reduced_first(outer_pair(norm_t, grad_q, cotangent_t, attended))
    all_stats = stats
    step = 1
    while step < ctx_count:
        all_stats = jnp.concatenate([all_stats, partner(all_stats, "ctx", step)], axis=0)
        step *= 2
    grad_k, grad_v = key_side(
        my_blocks,
        query_first,
        query_last,
        natural,
        by_partner,
        stat_place,
        row_base,
        queries,
        keys,
        values,
        d_attended,
        cosine,
        sine,
        my_ends[:, None],
        all_stats,
        (first_up, first_down),
    )
    grad_late = outer_pair(norm_t, after(grad_k, sum_feed), norm_t, grad_v)
    late_rows = reduced_first(grad_late)
    joint_rows = jnp.concatenate([early_rows, late_rows], axis=1)
    sum_joint = reduced_rest(joint_rows)
    grad_proj = [after(grad, late_rows) for grad in (grad_q, grad_k, grad_v)]
    grad_qbias = jnp.concatenate([jnp.sum(grad.astype(WIDE), axis=0) for grad in grad_proj])

    def joined(pair):
        return jnp.concatenate(pair, axis=1)

    partial_out = joined([dot_nn(attended, attn) for attn in attn_halves]) + feed_out

    def sum_halves(array):
        return own_half(array) + partner(far_half(array).astype(LOW), "tp", 1).astype(WIDE)

    out_bias = own_half((norm_vectors[2] + norm_vectors[3])[None, :])
    mixed = (tokens.astype(WIDE) + sum_halves(partial_out) + out_bias).astype(LOW)

    grad_norm = sum_halves(
        joined(
            [
                sum(
                    dot_nt(grad, stack[i * half : (i + 1) * half])
                    for i, grad in enumerate(grad_proj)
                )
                for stack in late_stacks
            ]
        )
        + feed_dx
    )
    my_normed = jnp.where(first_tp, *centered) * inv_std
    scaled = grad_norm * own_half(norm_vectors[0:1])
    row_sums = jnp.stack([jnp.sum(scaled, axis=1), jnp.sum(scaled * my_normed, axis=1)])
    row_means = (row_sums + partner(row_sums, "tp", 1)) / width
    grad_tokens = cotangent.astype(WIDE) + inv_std * (
        scaled - row_means[0][:, None] - my_normed * row_means[1][:, None]
    )

    vector_parts = jnp.stack(
        [jnp.sum(grad_norm * my_normed, axis=0), jnp.sum(grad_norm, axis=0), grad_outbias]
    )
    small = jnp.concatenate([vector_parts.reshape(-1), grad_qbias, grad_ubias[0]])
    small = sum_everywhere(small, ("ctx",))
    small = sum_everywhere(after(small, sum_joint), ("fsdp",))
    mine = small[: 3 * half].reshape(3, half)
    vectors = both_halves(mine, partner(mine, "tp", 1), 1)
    sum_vectors = jnp.concatenate([vectors, vectors[2:3]], axis=0)
    sum_qbias = small[3 * half : 6 * half].reshape(3, half)
    sum_ubias = small[6 * half :]

    def all_rows(sums):
        return lax.all_gather(sums, "ctx", axis=0, tiled=True)

    feed_rows = all_rows(sum_feed.astype(LOW))
    joint_all = all_rows(after(sum_joint.astype(LOW), feed_rows)).astype(WIDE)
    all_up, all_down = jnp.split(feed_rows.astype(WIDE), 2, axis=1)
    fresh_up = 0.95 * up_moment + all_up
    fresh_down = 0.95 * down_moment + all_down.T
    all_q, all_attn, all_k, all_v = jnp.split(joint_all, 4, axis=1)
    fresh_qkv = 0.95 * qkv_moment + jnp.stack([all_q, all_k, all_v], axis=1)
    fresh_attn = 0.95 * attn_moment + all_attn.T

    own_q, own_attn, own_k, own_v = jnp.split(sum_joint, 4, axis=1)
    sums = (sum_up, own_attn, jnp.concatenate([own_q, own_k, own_v], axis=1), sum_down)
    pieces = jnp.stack(
        [
            (
                0.95 * moment + jnp.pad(total, ((0, 0), (0, hidden_here - total.shape[1])))
            ).astype(LOW)
            for moment, total in zip(old_moments, sums)
        ]
    )

    def to_owner(step):
        picked = lax.dynamic_index_in_dim(pieces, ctx_high ^ step, 0, keepdims=False)
        return partner(picked, "ctx", step * low_count) if step else picked

    matrix = jnp.concatenate([to_owner(s) for s in range(OWNERS)], axis=0)
    parts = [matrix] + [partner(matrix, "ctx", s) for s in range(1, low_count)]
    for s in range(1, fsdp_count):
        parts += [partner(part, "fsdp", s) for part in parts[:low_count]]
    groups = [
        jnp.concatenate(parts[i : i + low_count], axis=0) for i in range(0, len(parts), low_count)
    ]
    near_cols = jnp.concatenate(groups, axis=0)
    far_cols = jnp.concatenate([partner(group, "tp", 1) for group in groups], axis=0)
    rows_out = orthogonal_rows(
        near_cols, far_cols, OWNERS * piece, ()
    ).reshape(OWNERS, piece, hidden_here)
    returned = [rows_out[0]] + [
        partner(rows_out[s], "ctx", s * low_count) for s in range(1, OWNERS)
    ]
    returned = jnp.stack([after(part, fresh_up, fresh_down) for part in returned])
    full_hidden = hidden_here * 2
    rates = (
        0.5 * math.sqrt(full_hidden / width),
        0.5 * math.sqrt(width / (width // HD)),
        0.5 * math.sqrt(3 * width / width),
        0.5 * math.sqrt(full_hidden / full_hidden),
    )
    new_up, new_attn, new_qkv, new_down = (
        old_weights[m]
        - rate * lax.dynamic_index_in_dim(returned, ctx_high ^ m, 0, keepdims=False).astype(WIDE)
        for m, rate in enumerate(rates)
    )
    new_attn, new_qkv = new_attn[:, :half], new_qkv[:, : 3 * half]

    vector_rate = 0.3 / math.sqrt(row_count * fsdp_count * ctx_count)
    mom_norm = 0.9 * norm_moment + sum_vectors
    mom_qbias = 0.9 * qbias_moment + sum_qbias
    mom_ubias = 0.9 * ubias_moment + sum_ubias
    return (
        mixed,
        grad_tokens,
        fresh_qkv,
        jnp.stack(jnp.split(new_qkv, 3, axis=1), axis=1),
        fresh_attn,
        new_attn.T,
        fresh_up,
        new_up,
        fresh_down,
        new_down.T,
        mom_norm,
        norm_vectors - vector_rate * mom_norm,
        mom_qbias,
        qkv_bias - vector_rate * mom_qbias,
        mom_ubias,
        up_bias - vector_rate * mom_ubias,
    )


def solution(mesh):
    return jax.shard_map(
        body,
        mesh=mesh,
        in_specs=(
            P(("fsdp", "ctx"), "tp"),
            P(("fsdp", "ctx"), "tp"),
            P("fsdp", None, "tp"),
            P("tp", "fsdp"),
            P("fsdp", "tp"),
            P("tp", "fsdp"),
            P(),
            P(None, "tp"),
            P("tp"),
            P("fsdp", None, "tp"),
            P("tp", "fsdp"),
            P("fsdp", "tp"),
            P("tp", "fsdp"),
            P(),
            P(None, "tp"),
            P("tp"),
            P("fsdp", None),
            P("fsdp", None),
        ),
        out_specs=(
            P(("fsdp", "ctx"), "tp"),
            P(("fsdp", "ctx"), "tp"),
            P("fsdp", None, "tp"),
            P(("fsdp", "ctx"), None, "tp"),
            P("tp", "fsdp"),
            P("tp", ("fsdp", "ctx")),
            P("fsdp", "tp"),
            P(("fsdp", "ctx"), "tp"),
            P("tp", "fsdp"),
            P("tp", ("fsdp", "ctx")),
            P(),
            P(),
            P(None, "tp"),
            P(None, "tp"),
            P("tp"),
            P("tp"),
        ),
        check_vma=False,
    )
```
